32 devices in a mesh: group: 2 (over x), dom: 16 (over z, y, core).
Axes of the slice: x: 2, y: 2, z: 4, core: 2. Of those that a mesh axis runs over, the one named last changes fastest.
Arguments:
- orbitals: bfloat16 [98304, 512], P(('group', 'dom')), may hold values from -6 to 6
- density_rows: bfloat16 [1024, 512], P(('group', 'dom')), may hold values from -0.01171875 to 0.01171875
- near_blocks: int32 [32, 32], P(('group', 'dom')), may hold values from 0 to 31, as said below
- leaf_coords: int32 [3, 192], P(None, ('group', 'dom')), may hold values from 0 to 31, as said below
- near_leaves: int32 [192, 3], P(('group', 'dom')), may hold values from 0 to 17, as said below
- leaf_basis: float32 [64, 98304], P(None, ('group', 'dom')), may hold values from -2 to 2
- leaf_transfer: float32 [192, 64, 64], P(('group', 'dom')), may hold values from -0.75 to 0.75
- dev_transfer: float32 [32, 64, 64], P(('group', 'dom')), may hold values from -0.375 to 0.375
- dev_far: int32 [32, 16], P(('group', 'dom')), may hold values 0 or 1
- group_far: int32 [2, 2], P('group'), may hold values 0 or 1
Outputs:
- density: float32 [98304], P(('group', 'dom'))
- hartree: float32 [98304], P(('group', 'dom'))
The draws below stay inside these ranges and needn't reach their ends.
Inputs may be any that keep to these rules, and one draw needn't show every extreme that they name: `near_blocks`: each row names 32 distinct blocks of its own coarse domain; block b is rows b * 16 to b * 16 + 15 of the domain's density matrix, held by the device of dom index b // 2. The first 2 entries of every row of a domain are the same: all blocks of one device of that domain, in order. Every other entry is a block held by a device whose dom index differs from the row's own by at most 8, counted cyclically over the 16 dom indices. `near_leaves`: each row names 3 distinct window positions, among them the leaf's own position 6 + (t mod 6) for row t. `leaf_coords`: distinct positions for all leaves.
All inputs are finite; a program needn't handle non-finite values. No bound on the sum of `dev_far` or of `group_far` on one device may be relied on, other than what follows from the above.
Results may differ from the reference program's by a relative error of at most 0.0003.
Values may be sent and summed in bfloat16 or wider, within the bound.
No kernel may reach another device: no remote copies, remote signals or barrier semaphores. Data moves between devices by JAX's collectives and lax.ppermute only.
A program may use at most 128 MiB of HBM per device.

```python
import math
import jax
import jax.numpy as jnp
from jax import lax

SIDE = 8
LEAF = 512
CHEB = 4
R = 64
BW = 16
NEAR_B = 32
BLK_DEV = 2
REACH = 8
LEAVES_DEV = 6
NEARL = 3
BLOCKS_G = 32
DEV_COUNT = 32
GRID = 98304
N_GROUP = 2
N_DOM = 16


def draw_near_blocks(key, part):
    hot_key, noise_key = jax.random.split(jax.random.fold_in(key, 11))
    dev_total_count = N_GROUP * N_DOM
    candidates = N_DOM * BLK_DEV
    hot_owner = jax.random.randint(hot_key, (N_GROUP,), 0, N_DOM)
    noise = jax.random.randint(noise_key, (dev_total_count, candidates), 0, 1024)
    dev_index = jnp.arange(dev_total_count)
    group_index = dev_index // N_DOM
    dom_index = dev_index % N_DOM
    cand_index = jnp.arange(candidates)
    owner = cand_index // BLK_DEV
    apart = jnp.abs(owner[None, :] - dom_index[:, None])
    cyclic = jnp.minimum(apart, N_DOM - apart)
    score = (noise + 1) * candidates + (candidates - 1 - cand_index)[None, :]
    own_hot = hot_owner[group_index]
    is_hot = owner[None, :] == own_hot[:, None]
    blocked = is_hot | (cyclic > REACH)
    score = jnp.where(blocked, -1 - cand_index[None, :], score)
    picked = lax.top_k(score, NEAR_B - BLK_DEV)[1]
    hot_blocks = own_hot[:, None] * BLK_DEV + jnp.arange(BLK_DEV)[None, :]
    return jnp.concatenate([hot_blocks, picked], axis=1).astype(jnp.int32)


def draw_near_leaves(key, part):
    noise_key = jax.random.fold_in(key, 23)
    row_total = N_GROUP * N_DOM * LEAVES_DEV
    window = 3 * LEAVES_DEV
    noise = jax.random.randint(noise_key, (row_total, window), 0, 1024)
    position = jnp.arange(window)
    score = noise * window + position[None, :]
    own_position = LEAVES_DEV + jnp.arange(row_total) % LEAVES_DEV
    score = jnp.where(position[None, :] == own_position[:, None], 1 << 28, score)
    return lax.top_k(score, NEARL)[1].astype(jnp.int32)


def draw_leaf_coords(key, part):
    jitter_key = jax.random.fold_in(key, 37)
    row_total = N_GROUP * N_DOM * LEAVES_DEV
    jitter = jax.random.randint(jitter_key, (3, row_total), 0, 2)
    leaf_index = jnp.arange(row_total)
    local_leaf = leaf_index % LEAVES_DEV
    dom_index = leaf_index // LEAVES_DEV % N_DOM
    group_index = leaf_index // (LEAVES_DEV * N_DOM)
    layout = jnp.stack([2 * local_leaf, 2 * dom_index, 2 * group_index])
    return (layout + jitter).astype(jnp.int32)


def with_ends(values, stream_key, low, largest):
    longest = values.shape.index(max(values.shape))
    spots = []
    for shift in (0, 1):
        where = [jax.random.randint(jax.random.fold_in(stream_key, axis), (), 0, length) for axis, length in enumerate(values.shape)]
        where[longest] = (where[longest] + shift) % values.shape[longest]
        spots.append(tuple(where))
    return values.at[spots[0]].set(low).at[spots[1]].set(largest)


def block_scale(rng, dims, shards, least, top_value):
    level = 1.0
    for dim, shards_of in shards:
        draws = jax.random.uniform(jax.random.fold_in(jax.random.fold_in(rng, 6), dim), (shards_of,), jnp.float32, least / len(shards), top_value / len(shards))
        level = level * jnp.repeat(jnp.exp(draws), dims[dim] // shards_of).reshape((-1,) + (1,) * (len(dims) - 1 - dim))
    return level


def gaussian(rng, extent, spread, bound, shards=(), held_as=jnp.bfloat16):
    entries = spread * jax.random.normal(rng, extent, jnp.float32)
    if shards:
        entries = entries * block_scale(rng, extent, shards, -0.22, 0.18)
    return jnp.clip(entries, -bound, bound).astype(held_as)


def setup_inputs(seed: int = 0) -> dict:
    streams_of = jax.random.split(jax.random.key(seed), 11)
    orbitals = gaussian(streams_of[0], (GRID, NEAR_B * BW), 1.0, 6.0, ((0, 32),))
    density_rows = gaussian(streams_of[1], (N_GROUP * BLOCKS_G * BW, BLOCKS_G * BW), ((NEAR_B * BW) * (NEAR_B * BW)) ** -0.5, 0.01171875, ((0, 32),))
    near_blocks = draw_near_blocks(jax.random.fold_in(streams_of[10], 71), 0)
    leaf_coords = draw_leaf_coords(jax.random.fold_in(streams_of[10], 71), 0)
    near_leaves = draw_near_leaves(jax.random.fold_in(streams_of[10], 71), 0)
    leaf_basis = gaussian(streams_of[5], (R, GRID), 0.125, 2.0, ((1, 32),), jnp.float32)
    leaf_transfer = gaussian(streams_of[6], (DEV_COUNT * LEAVES_DEV, R, R), R ** -0.5, 0.75, ((0, 32),), jnp.float32)
    dev_transfer = gaussian(streams_of[7], (DEV_COUNT, R, R), (4 * R) ** -0.5, 0.375, ((0, 32),), jnp.float32)
    dev_far = with_ends((jax.random.randint(streams_of[8], (DEV_COUNT, N_DOM), 0, 2) < 1).astype(jnp.int32), jax.random.fold_in(streams_of[8], 1), 0, 1)
    group_far = with_ends((jax.random.randint(streams_of[9], (N_GROUP, N_GROUP), 0, 2) < 1).astype(jnp.int32), jax.random.fold_in(streams_of[9], 1), 0, 1)
    return dict(orbitals=orbitals, density_rows=density_rows, near_blocks=near_blocks, leaf_coords=leaf_coords, near_leaves=near_leaves, leaf_basis=leaf_basis, leaf_transfer=leaf_transfer, dev_transfer=dev_transfer, dev_far=dev_far, group_far=group_far)


vol_weight = 0.1
soft_square = 1.0

def coulomb(target, source):
    diff_x = target[0][:, None] - source[0][None, :]
    diff_y = target[1][:, None] - source[1][None, :]
    diff_z = target[2][:, None] - source[2][None, :]
    return 1.0 / jnp.sqrt(diff_x * diff_x + diff_y * diff_y + diff_z * diff_z + soft_square)

def cluster_nodes(bounds):
    steps_idx = jnp.arange(CHEB).astype(jnp.float32)
    cheb_points = jnp.cos((2.0 * steps_idx + 1.0) * (math.pi / (2.0 * CHEB)))
    centre = 0.5 * (bounds[:3] + bounds[3:])
    half_size = 0.5 * (bounds[3:] - bounds[:3])
    along = centre[:, None] + half_size[:, None] * cheb_points[None, :]
    node_index = jnp.arange(CHEB * CHEB * CHEB)
    first = node_index // (CHEB * CHEB)
    second = node_index // CHEB % CHEB
    third = node_index % CHEB
    return jnp.stack([along[0][first], along[1][second], along[2][third]])

def point_offsets():
    place = jnp.arange(LEAF)
    return jnp.stack([place // (SIDE * SIDE), place // SIDE % SIDE, place % SIDE]).astype(jnp.float32)

def reference(orbitals, density_rows, near_blocks, leaf_coords, near_leaves, leaf_basis, leaf_transfer, dev_transfer, dev_far, group_far):
    dev_total_count = N_GROUP * N_DOM
    leaf_count = LEAVES_DEV
    near_width = NEAR_B * BW
    block_total = BLK_DEV * N_DOM
    rows_all = density_rows.reshape(N_GROUP, block_total, BW, block_total, BW)
    orb_all = orbitals.reshape(dev_total_count, leaf_count * LEAF, near_width)

    def density_one(dev_index):
        group_index = dev_index // N_DOM
        near_list = near_blocks[dev_index]
        table = rows_all[group_index]
        tiles = table[near_list[:, None], :, near_list[None, :], :]
        local_matrix = jnp.transpose(tiles, (0, 2, 1, 3)).reshape(near_width, near_width)
        product = jnp.dot(orb_all[dev_index], local_matrix, preferred_element_type=jnp.float32)
        return lax.optimization_barrier(jnp.sum(product * orb_all[dev_index].astype(jnp.float32), axis=1))
    density = lax.map(density_one, jnp.arange(dev_total_count))
    leaf_total = dev_total_count * leaf_count
    coords_f = leaf_coords.astype(jnp.float32)
    points = SIDE * coords_f.T[:, :, None] + point_offsets()[None]
    rho_leaf = density.reshape(leaf_total, LEAF)
    packed = jnp.concatenate([points, rho_leaf[:, None, :]], axis=1)
    packed = packed.reshape(N_GROUP, N_DOM * leaf_count, 4, LEAF)
    padded = jnp.pad(packed, ((0, 0), (leaf_count, leaf_count), (0, 0), (0, 0)))

    def near_one(leaf_index):
        group_index = leaf_index // (N_DOM * leaf_count)
        within = leaf_index % (N_DOM * leaf_count)
        base = within - within % leaf_count
        own_points = points[leaf_index]
        running = jnp.zeros((LEAF,), jnp.float32)
        for near_slot in range(NEARL):
            source = padded[group_index, base + near_leaves[leaf_index, near_slot]]
            running = running + jnp.dot(coulomb(own_points, source[:3]), source[3], precision=lax.Precision.HIGHEST)
        return running
    near_part = lax.map(near_one, jnp.arange(leaf_total)) * vol_weight
    rank = leaf_basis.shape[0]
    leaf_bases = leaf_basis.reshape(rank, leaf_total, LEAF)
    leaf_mom = jnp.einsum('rtp,tp->tr', leaf_bases, rho_leaf, precision=lax.Precision.HIGHEST)
    transfer_four = leaf_transfer.reshape(dev_total_count, leaf_count, rank, rank)
    dev_mom = jnp.einsum('dlqr,dlq->dr', transfer_four, leaf_mom.reshape(dev_total_count, leaf_count, rank), precision=lax.Precision.HIGHEST)
    coords_dev = coords_f.reshape(3, dev_total_count, leaf_count)
    low_side = SIDE * lax.optimization_barrier(jnp.min(coords_dev, axis=2)).T
    high_side = SIDE * lax.optimization_barrier(jnp.max(coords_dev, axis=2)).T + (SIDE - 1)
    bounds_all = jnp.concatenate([low_side, high_side], axis=1)
    nodes_all = jax.vmap(cluster_nodes)(bounds_all)
    upward = jnp.einsum('dqr,dq->dr', dev_transfer, dev_mom, precision=lax.Precision.HIGHEST)
    group_mom = lax.optimization_barrier(jnp.sum(upward.reshape(N_GROUP, N_DOM, rank), axis=1))
    nodes_grouped = nodes_all.reshape(N_GROUP, N_DOM, 3, rank)
    mom_grouped = dev_mom.reshape(N_GROUP, N_DOM, rank)

    def device_one(dev_index):
        group_index = dev_index // N_DOM
        coupling = jax.vmap(lambda other: coulomb(nodes_all[dev_index], other))(nodes_grouped[group_index])
        coupling = coupling * dev_far[dev_index].astype(jnp.float32)[:, None, None]
        return vol_weight * jnp.einsum('srq,sq->r', coupling, mom_grouped[group_index], precision=lax.Precision.HIGHEST)
    dev_local = lax.map(device_one, jnp.arange(dev_total_count))
    bounds_grouped = bounds_all.reshape(N_GROUP, N_DOM, 6)
    group_bounds = jnp.concatenate([lax.optimization_barrier(jnp.min(bounds_grouped[:, :, :3], axis=1)), lax.optimization_barrier(jnp.max(bounds_grouped[:, :, 3:], axis=1))], axis=1)
    group_nodes = jax.vmap(cluster_nodes)(group_bounds)

    def group_one(group_index):
        coupling = jax.vmap(lambda other: coulomb(group_nodes[group_index], other))(group_nodes)
        coupling = coupling * group_far[group_index].astype(jnp.float32)[:, None, None]
        return vol_weight * jnp.einsum('srq,sq->r', coupling, group_mom, precision=lax.Precision.HIGHEST)
    group_local = lax.map(group_one, jnp.arange(N_GROUP))
    group_each = jnp.repeat(group_local, N_DOM, axis=0)
    dev_total = dev_local + jnp.einsum('dqr,dr->dq', dev_transfer, group_each, precision=lax.Precision.HIGHEST)
    leaf_local = jnp.einsum('dlqr,dr->dlq', transfer_four, dev_total, precision=lax.Precision.HIGHEST)
    far_part = jnp.einsum('rtp,tr->tp', leaf_bases, leaf_local.reshape(leaf_total, rank), precision=lax.Precision.HIGHEST)
    hartree = (near_part + far_part).reshape(-1)
    return (density.reshape(-1), hartree)
```

```python
import functools
import math

import jax
import jax.numpy as jnp
from jax import lax
from jax.experimental import pallas as pl
from jax.experimental.pallas import tpu as pltpu
from jax.sharding import PartitionSpec as P

SIDE = 8
LEAF = 512
CHEB = 4
RANK = CHEB * CHEB * CHEB
BW = 16
NEARL = 3
LANES = 128
LEAF_ROWS = LEAF // LANES
HIGHEST = lax.Precision.HIGHEST

vol_weight = 0.1
soft_square = 1.0


def xor_stages(count):
    bits = count.bit_length() - 1
    stages, bit = ([(2,)], 2) if bits > 1 else ([], 1)
    while bit < bits:
        wide = 2 if bit + 1 < bits else 1
        stages.append(tuple(m << bit for m in range(1, 1 << wide)))
        bit += wide
    return stages


def swap(value, axis, mask):
    return lax.ppermute(value, axis, [(i, i ^ mask) for i in range(lax.axis_size(axis))])


def gather_rows(rows):
    held = rows
    for masks in xor_stages(lax.axis_size("dom")):
        held = jnp.concatenate([held] + [swap(held, "dom", m) for m in masks], axis=0)
    return held, swap(held, "dom", 1)


def iota(shape, dim):
    return lax.broadcasted_iota(jnp.int32, shape, dim)


def lane_sums(x):
    hi = x.astype(jnp.bfloat16)
    lo = (x - hi.astype(jnp.float32)).astype(jnp.bfloat16)
    both = jnp.concatenate([hi, lo], axis=1)
    ones = jnp.ones((8, 2 * LANES), jnp.bfloat16)
    return lax.dot_general(ones, both, (((1,), (1,)), ((), ())), preferred_element_type=jnp.float32)


def prepare_kernel(near_ref, basis_ref, transfer_ref, dev_ref, pick_ref, weights_ref):
    blocks = near_ref.shape[1]
    width = blocks * BW
    spread = (iota((blocks, width), 1) // BW == iota((blocks, width), 0)).astype(jnp.float32)
    near = jnp.broadcast_to(near_ref[...].astype(jnp.float32), (8, blocks))
    column = jnp.dot(near, spread, preferred_element_type=jnp.float32)[:1].astype(jnp.int32) * BW
    column = column + iota((1, width), 1) % BW
    for start in range(0, pick_ref.shape[0], LEAF):
        size = min(LEAF, pick_ref.shape[0] - start)
        hit = iota((size, width), 0) + start == column
        pick_ref[start : start + size, :] = jnp.where(hit, 1.0, 0.0).astype(jnp.bfloat16)
    dev = dev_ref[0]
    for leaf in range(transfer_ref.shape[0]):
        points = slice(leaf * LEAF, (leaf + 1) * LEAF)
        own = lax.dot_general(
            transfer_ref[leaf],
            basis_ref[:, points],
            (((0,), (0,)), ((), ())),
            precision=HIGHEST,
            preferred_element_type=jnp.float32,
        )
        weights_ref[:RANK, points] = own
        weights_ref[RANK:, points] = lax.dot_general(
            dev, own, (((0,), (0,)), ((), ())), precision=HIGHEST, preferred_element_type=jnp.float32
        )


def density_kernel(
    near_ref,
    coords_ref,
    orbitals_ref,
    held_ref,
    other_ref,
    pick_ref,
    weights_ref,
    density_ref,
    halo_ref,
    expansion_ref,
    rows_ref,
    orbit_ref,
    sems,
):
    leaves = coords_ref.shape[1]
    copies = []
    for leaf in range(leaves):
        points = pl.ds(leaf * LEAF, LEAF)
        copies.append(
            pltpu.make_async_copy(orbitals_ref.at[points], orbit_ref.at[points], sems.at[leaf])
        )
        copies[-1].start()
    me = lax.axis_index("dom")
    for k in range(near_ref.shape[1]):
        block = near_ref[0, k]
        apart = jnp.bitwise_xor(lax.shift_right_logical(block, 1), me)
        first = lax.shift_right_logical(apart, 1) * (2 * BW) + jnp.bitwise_and(block, 1) * BW
        at = pl.ds(pl.multiple_of(first, BW), BW)
        mine = jnp.bitwise_and(apart, 1) == 0
        rows_ref[k * BW : (k + 1) * BW, :] = jnp.where(mine, held_ref[at, :], other_ref[at, :])
    matrix = jnp.dot(rows_ref[...], pick_ref[...], preferred_element_type=jnp.float32)
    matrix = matrix.astype(jnp.bfloat16)
    total = jnp.zeros((2 * RANK, LANES), jnp.float32)
    for leaf in range(leaves):
        copies[leaf].wait()
        orbit = orbit_ref[leaf * LEAF : (leaf + 1) * LEAF, :]
        product = jnp.dot(orbit, matrix, preferred_element_type=jnp.float32)
        product = product * orbit.astype(jnp.float32)
        folded = product[:, :LANES]
        for start in range(LANES, product.shape[1], LANES):
            folded = folded + product[:, start : start + LANES]
        values = lane_sums(folded)[:1]
        for j in range(LEAF_ROWS):
            row = leaf * LEAF_ROWS + j
            part = values[:, j * LANES : (j + 1) * LANES]
            density_ref[row : row + 1, :] = part
            halo_ref[row : row + 1, :] = part
            total = total + weights_ref[:, row * LANES : (row + 1) * LANES] * part
    coords = coords_ref[...].astype(jnp.float32)
    rows = leaves * LEAF_ROWS
    halo_ref[rows:, :] = jnp.zeros((halo_ref.shape[0] - rows, LANES), jnp.float32)
    halo_ref[rows : rows + 3, :leaves] = coords
    low = SIDE * jnp.min(coords, axis=1, keepdims=True)
    high = SIDE * jnp.max(coords, axis=1, keepdims=True) + (SIDE - 1)
    lane = iota((1, LANES), 1)
    bounds = jnp.zeros((1, LANES), jnp.float32)
    for k in range(3):
        bounds = jnp.where(lane == k, low[k : k + 1], bounds)
        bounds = jnp.where(lane == 3 + k, high[k : k + 1], bounds)
    both = jnp.concatenate([lane_sums(total)[:1], bounds], axis=0)
    expansion_ref[...] = jnp.broadcast_to(both[None], expansion_ref.shape)


def pattern(index):
    steps = (index // (CHEB * CHEB) % CHEB, index // CHEB % CHEB, index % CHEB)
    points = [math.cos((2 * a + 1) * math.pi / (2 * CHEB)) for a in range(CHEB)]
    out = []
    for step in steps:
        value = jnp.full(index.shape, points[CHEB - 1], jnp.float32)
        for a in range(CHEB - 1):
            value = jnp.where(step == a, points[a], value)
        out.append(value)
    return out


def nodes(bounds, unit):
    out = []
    for k in range(3):
        low, high = bounds[:, k : k + 1], bounds[:, 3 + k : 4 + k]
        out.append(0.5 * (low + high) + 0.5 * (high - low) * unit[k])
    return out


def node_coupling(target, source):
    square = soft_square
    for t, s in zip(target, source, strict=True):
        apart = t - s
        square = square + apart * apart
    return lax.rsqrt(square)


def potential_kernel(
    leaves_ref,
    far_ref,
    group_far_ref,
    halo_ref,
    even_ref,
    odd_ref,
    expansion_ref,
    weights_ref,
    dev_ref,
    out_ref,
    density_ref,
    place_ref,
    sum_ref,
    local_ref,
):
    leaves = leaves_ref.shape[0]
    rows = leaves * LEAF_ROWS
    group_count, dom_count = group_far_ref.shape[1], far_ref.shape[1]
    group, me = lax.axis_index("group"), lax.axis_index("dom")

    is_odd = jnp.bitwise_and(me, 1) == 1
    even, odd = even_ref[...], odd_ref[...]
    window = (jnp.where(is_odd, even, odd), halo_ref[...], jnp.where(is_odd, odd, even))
    ones = jnp.ones((LANES, LANES), jnp.bfloat16)
    diagonal = iota((8, LANES), 0) == iota((8, LANES), 1)
    spread = []
    for side, held in enumerate(window):
        density_ref[side * rows : (side + 1) * rows, :] = held[:rows]
        for k in range(3):
            spread.append(jnp.where(diagonal, held[rows + k : rows + k + 1], 0.0))
    spread = jnp.concatenate(spread, axis=0).astype(jnp.bfloat16)
    place_ref[...] = SIDE * jnp.dot(spread, ones, preferred_element_type=jnp.float32)

    sent = expansion_ref[...]
    moments, bounds = sent[:, 0, :], sent[:, 1, :]
    lane = iota((1, LANES), 1)
    unit_row = pattern(lane % RANK)
    unit_column = pattern(iota((RANK, LANES), 0))
    group_bounds = []
    for h in range(group_count):
        part = bounds[h * dom_count : (h + 1) * dom_count]
        low = jnp.min(part, axis=0, keepdims=True)
        high = jnp.max(part, axis=0, keepdims=True)
        group_bounds.append(jnp.where(lane < 3, low, high))
    own_group_bounds = group_bounds[0]
    for h in range(1, group_count):
        own_group_bounds = jnp.where(group == h, group_bounds[h], own_group_bounds)
    target = nodes(own_group_bounds, unit_column)
    total = jnp.zeros((RANK, LANES), jnp.float32)
    for h in range(group_count):
        raised = jnp.sum(moments[h * dom_count : (h + 1) * dom_count], axis=0, keepdims=True)
        raised = jnp.where(lane >= RANK, raised, 0.0) * group_far_ref[0, h].astype(jnp.float32)
        total = total + node_coupling(target, nodes(group_bounds[h], unit_row)) * raised
    group_local = vol_weight * lane_sums(total)[:1, :RANK]
    local = jnp.sum(dev_ref[0] * group_local, axis=1, keepdims=True)
    base = group * dom_count
    own = expansion_ref[pl.ds(base, dom_count)]
    own_bounds = expansion_ref[pl.ds(base + me, 1)][:, 1, :]
    target = nodes(own_bounds, unit_column)
    source = nodes(own[:, 1, :], unit_row)
    own_moments = jnp.where(lane < RANK, own[:, 0, :], 0.0)
    total = jnp.zeros((RANK, LANES), jnp.float32)
    for s in range(dom_count):
        coupling = node_coupling(target, [x[s : s + 1] for x in source])
        total = total + coupling * (own_moments[s : s + 1] * far_ref[0, s].astype(jnp.float32))
    local = local + vol_weight * jnp.sum(total, axis=1, keepdims=True)
    local_ref[...] = jnp.broadcast_to(local, (RANK, LANES))

    lane8, row8 = iota((8, LANES), 1), iota((8, LANES), 0)
    half = (lane8 // (SIDE * SIDE)).astype(jnp.float32)
    at_y = (lane8 // SIDE % SIDE).astype(jnp.float32)
    along_z = (row8 - lane8 % SIDE).astype(jnp.float32)

    def place(position):
        side = (position >= leaves).astype(jnp.int32) + (position >= 2 * leaves).astype(jnp.int32)
        first = side * 24 + (position - side * leaves)
        return [place_ref[pl.ds(first + 8 * k, 1), :] for k in range(3)]

    def one_leaf(leaf, carry):
        own_place = place(leaf + leaves)
        for slot in range(NEARL):
            position = leaves_ref[leaf, slot]
            shift = [a - b for a, b in zip(own_place, place(position), strict=True)]
            rho = [density_ref[pl.ds(position * LEAF_ROWS + j, 1), :] for j in range(LEAF_ROWS)]
            along = shift[2] + along_z
            square_z = along * along + soft_square
            square_x = []
            for m in range(-6, SIDE):
                apart = shift[0] + (m - half)
                square_x.append(apart * apart)
            for y in range(SIDE):
                apart = shift[1] + (y - at_y)
                square = apart * apart + square_z
                kernel = [lax.rsqrt(x + square) for x in square_x]
                for x in range(SIDE):
                    value = kernel[x + 6] * rho[0]
                    for j in range(1, LEAF_ROWS):
                        value = value + kernel[x - 2 * j + 6] * rho[j]
                    at = slice((x * SIDE + y) * SIDE, (x * SIDE + y + 1) * SIDE)
                    if slot == 0:
                        sum_ref[at, :] = value
                    else:
                        sum_ref[at, :] += value
        near = vol_weight * lane_sums(sum_ref[...])[:1]
        spread_local = local_ref[...]
        for j in range(LEAF_ROWS):
            row = leaf * LEAF_ROWS + j
            at = pl.ds(pl.multiple_of(row * LANES, LANES), LANES)
            far = jnp.sum(weights_ref[:RANK, at] * spread_local, axis=0, keepdims=True)
            out_ref[pl.ds(row, 1), :] = near[:, j * LANES : (j + 1) * LANES] + far
        return carry

    lax.fori_loop(0, leaves, one_leaf, 0)


VMEM = pl.BlockSpec(memory_space=pltpu.VMEM)
SMEM = pl.BlockSpec(memory_space=pltpu.SMEM)


def local(
    orbitals,
    density_rows,
    near_blocks,
    leaf_coords,
    near_leaves,
    leaf_basis,
    leaf_transfer,
    dev_transfer,
    dev_far,
    group_far,
):
    points, width = orbitals.shape
    leaves = leaf_coords.shape[1]
    rows = leaves * LEAF_ROWS
    natural = density_rows.shape[1]
    devices = lax.axis_size("group") * lax.axis_size("dom")
    dom_count = lax.axis_size("dom")
    f32 = jnp.float32
    params = pltpu.CompilerParams(vmem_limit_bytes=(24 << 20) + 4 * natural * natural)

    pick, weights = pl.pallas_call(
        prepare_kernel,
        out_shape=(
            jax.ShapeDtypeStruct((natural, width), jnp.bfloat16),
            jax.ShapeDtypeStruct((2 * RANK, points), f32),
        ),
        in_specs=[VMEM] * 4,
        out_specs=(VMEM, VMEM),
        compiler_params=params,
        cost_estimate=pl.CostEstimate(
            flops=2 * 6 * 2 * RANK * RANK * points, bytes_accessed=8 << 20, transcendentals=0
        ),
        name="prepare",
    )(near_blocks, leaf_basis, leaf_transfer, dev_transfer)

    held, other = gather_rows(density_rows)

    density, halo, expansion = pl.pallas_call(
        density_kernel,
        out_shape=(
            jax.ShapeDtypeStruct((rows, LANES), f32),
            jax.ShapeDtypeStruct((rows + 8, LANES), f32),
            jax.ShapeDtypeStruct((devices, 2, LANES), f32),
        ),
        in_specs=[SMEM, VMEM, pl.BlockSpec(memory_space=pl.ANY)] + [VMEM] * 4,
        out_specs=(VMEM, VMEM, VMEM),
        scratch_shapes=[
            pltpu.VMEM((width, natural), jnp.bfloat16),
            pltpu.VMEM((points, width), jnp.bfloat16),
            pltpu.SemaphoreType.DMA((leaves,)),
        ],
        compiler_params=params,
        cost_estimate=pl.CostEstimate(
            flops=2 * points * width * width, bytes_accessed=8 << 20, transcendentals=0
        ),
        name="density",
    )(near_blocks, leaf_coords, orbitals, held, other, pick, weights)

    even = swap(halo, "dom", 1)
    pairs = [(i, i + 1 if i % 2 else i - 1) for i in range(1, dom_count - 1)]
    odd = lax.ppermute(halo, "dom", pairs)
    everyone = lax.all_to_all(expansion, ("group", "dom"), 0, 0)

    hartree = pl.pallas_call(
        potential_kernel,
        out_shape=jax.ShapeDtypeStruct((rows, LANES), f32),
        in_specs=[SMEM, SMEM, SMEM] + [VMEM] * 6,
        out_specs=VMEM,
        scratch_shapes=[
            pltpu.VMEM((3 * rows, LANES), f32),
            pltpu.VMEM((72, LANES), f32),
            pltpu.VMEM((LEAF, LANES), f32),
            pltpu.VMEM((RANK, LANES), f32),
        ],
        compiler_params=params,
        cost_estimate=pl.CostEstimate(
            flops=20 << 20, bytes_accessed=2 << 20, transcendentals=4 << 20
        ),
        name="potential",
    )(near_leaves, dev_far, group_far, halo, even, odd, everyone, weights, dev_transfer)
    return (density.reshape(-1), hartree.reshape(-1))


def solution(mesh):
    in_specs = (
        P(("group", "dom"), None),
        P(("group", "dom"), None),
        P(("group", "dom"), None),
        P(None, ("group", "dom")),
        P(("group", "dom"), None),
        P(None, ("group", "dom")),
        P(("group", "dom"), None, None),
        P(("group", "dom"), None, None),
        P(("group", "dom"), None),
        P("group", None),
    )
    out_specs = (P(("group", "dom")), P(("group", "dom")))
    return jax.shard_map(local, mesh=mesh, in_specs=in_specs, out_specs=out_specs, check_vma=False)
```

```python
import functools
import math

import jax
import jax.numpy as jnp
from jax import lax
from jax.experimental import pallas as pl
from jax.experimental.pallas import tpu as pltpu
from jax.sharding import PartitionSpec as P

SIDE = 8
LEAF = 512
CHEB = 4
RANK = CHEB * CHEB * CHEB
BW = 16
NEARL = 3
LANES = 128
LEAF_ROWS = LEAF // LANES
HIGHEST = lax.Precision.HIGHEST

vol_weight = 0.1
soft_square = 1.0


def xor_stages(count):
    bits = count.bit_length() - 1
    stages, bit = ([(2,)], 2) if bits > 1 else ([], 1)
    while bit < bits:
        wide = 2 if bit + 1 < bits else 1
        stages.append(tuple(m << bit for m in range(1, 1 << wide)))
        bit += wide
    return stages


def swap(value, axis, mask):
    return lax.ppermute(value, axis, [(i, i ^ mask) for i in range(lax.axis_size(axis))])


def farthest_first(mask):
    return -(mask & -mask), -mask


def gather_rows(rows, beside):
    held, result = rows, None
    for stage, masks in enumerate(xor_stages(lax.axis_size("dom"))):
        if stage == 1:
            result = beside(held)
        arrived = {m: swap(held, "dom", m) for m in sorted(masks, key=farthest_first)}
        held = jnp.concatenate([held] + [arrived[m] for m in masks], axis=0)
    held, result = lax.optimization_barrier((held, result))
    return held, swap(held, "dom", 1), result


def iota(shape, dim):
    return lax.broadcasted_iota(jnp.int32, shape, dim)


def lane_sums(x):
    hi = x.astype(jnp.bfloat16)
    lo = (x - hi.astype(jnp.float32)).astype(jnp.bfloat16)
    both = jnp.concatenate([hi, lo], axis=1)
    ones = jnp.ones((8, 2 * LANES), jnp.bfloat16)
    return lax.dot_general(ones, both, (((1,), (1,)), ((), ())), preferred_element_type=jnp.float32)


def prepare_kernel(
    near_hbm,
    basis_hbm,
    transfer_hbm,
    dev_hbm,
    orbitals_hbm,
    gate_ref,
    orbit_ref,
    pick_ref,
    weights_ref,
    near_ref,
    basis_ref,
    transfer_ref,
    dev_ref,
    sems,
):
    del gate_ref
    moves = ((near_hbm, near_ref), (transfer_hbm, transfer_ref), (dev_hbm, dev_ref))
    moves += ((basis_hbm, basis_ref), (orbitals_hbm, orbit_ref))
    copies = [pltpu.make_async_copy(a, b, sems.at[i]) for i, (a, b) in enumerate(moves)]
    for copy in copies:
        copy.start()
    copies[0].wait()
    blocks = near_ref.shape[1]
    width = blocks * BW
    spread = (iota((blocks, width), 1) // BW == iota((blocks, width), 0)).astype(jnp.float32)
    near = jnp.broadcast_to(near_ref[...].astype(jnp.float32), (8, blocks))
    column = jnp.dot(near, spread, preferred_element_type=jnp.float32)[:1].astype(jnp.int32) * BW
    column = column + iota((1, width), 1) % BW
    for start in range(0, pick_ref.shape[0], LEAF):
        size = min(LEAF, pick_ref.shape[0] - start)
        hit = iota((size, width), 0) + start == column
        pick_ref[start : start + size, :] = jnp.where(hit, 1.0, 0.0).astype(jnp.bfloat16)
    for copy in copies[1:4]:
        copy.wait()
    dev = dev_ref[0]
    for leaf in range(transfer_ref.shape[0]):
        points = slice(leaf * LEAF, (leaf + 1) * LEAF)
        own = lax.dot_general(
            transfer_ref[leaf],
            basis_ref[:, points],
            (((0,), (0,)), ((), ())),
            precision=HIGHEST,
            preferred_element_type=jnp.float32,
        )
        weights_ref[:RANK, points] = own
        weights_ref[RANK:, points] = lax.dot_general(
            dev, own, (((0,), (0,)), ((), ())), precision=HIGHEST, preferred_element_type=jnp.float32
        )
    copies[4].wait()


def density_kernel(
    near_ref,
    coords_ref,
    orbit_ref,
    held_ref,
    other_ref,
    pick_ref,
    weights_ref,
    density_ref,
    halo_ref,
    expansion_ref,
    rows_ref,
):
    leaves = coords_ref.shape[1]
    me = lax.axis_index("dom")
    for k in range(near_ref.shape[1]):
        block = near_ref[0, k]
        apart = jnp.bitwise_xor(lax.shift_right_logical(block, 1), me)
        first = lax.shift_right_logical(apart, 1) * (2 * BW) + jnp.bitwise_and(block, 1) * BW
        at = pl.ds(pl.multiple_of(first, BW), BW)
        mine = jnp.bitwise_and(apart, 1) == 0
        rows_ref[k * BW : (k + 1) * BW, :] = jnp.where(mine, held_ref[at, :], other_ref[at, :])
    matrix = jnp.dot(rows_ref[...], pick_ref[...], preferred_element_type=jnp.float32)
    matrix = matrix.astype(jnp.bfloat16)
    total = jnp.zeros((2 * RANK, LANES), jnp.float32)
    for leaf in range(leaves):
        orbit = orbit_ref[leaf * LEAF : (leaf + 1) * LEAF, :]
        product = jnp.dot(orbit, matrix, preferred_element_type=jnp.float32)
        product = product * orbit.astype(jnp.float32)
        folded = product[:, :LANES]
        for start in range(LANES, product.shape[1], LANES):
            folded = folded + product[:, start : start + LANES]
        values = lane_sums(folded)[:1]
        for j in range(LEAF_ROWS):
            row = leaf * LEAF_ROWS + j
            part = values[:, j * LANES : (j + 1) * LANES]
            density_ref[row : row + 1, :] = part
            halo_ref[row : row + 1, :] = part
            total = total + weights_ref[:, row * LANES : (row + 1) * LANES] * part
    coords = coords_ref[...].astype(jnp.float32)
    rows = leaves * LEAF_ROWS
    halo_ref[rows:, :] = jnp.zeros((halo_ref.shape[0] - rows, LANES), jnp.float32)
    halo_ref[rows : rows + 3, :leaves] = coords
    low = SIDE * jnp.min(coords, axis=1, keepdims=True)
    high = SIDE * jnp.max(coords, axis=1, keepdims=True) + (SIDE - 1)
    lane = iota((1, LANES), 1)
    bounds = jnp.zeros((1, LANES), jnp.float32)
    for k in range(3):
        bounds = jnp.where(lane == k, low[k : k + 1], bounds)
        bounds = jnp.where(lane == 3 + k, high[k : k + 1], bounds)
    both = jnp.concatenate([lane_sums(total)[:1], bounds], axis=0)
    expansion_ref[...] = jnp.broadcast_to(both[None], expansion_ref.shape)


def pattern(index):
    steps = (index // (CHEB * CHEB) % CHEB, index // CHEB % CHEB, index % CHEB)
    points = [math.cos((2 * a + 1) * math.pi / (2 * CHEB)) for a in range(CHEB)]
    out = []
    for step in steps:
        value = jnp.full(index.shape, points[CHEB - 1], jnp.float32)
        for a in range(CHEB - 1):
            value = jnp.where(step == a, points[a], value)
        out.append(value)
    return out


def nodes(bounds, unit):
    out = []
    for k in range(3):
        low, high = bounds[:, k : k + 1], bounds[:, 3 + k : 4 + k]
        out.append(0.5 * (low + high) + 0.5 * (high - low) * unit[k])
    return out


def node_coupling(target, source):
    square = soft_square
    for t, s in zip(target, source, strict=True):
        apart = t - s
        square = square + apart * apart
    return lax.rsqrt(square)


def potential_kernel(
    leaves_ref,
    far_ref,
    group_far_ref,
    halo_ref,
    even_ref,
    odd_ref,
    expansion_ref,
    weights_ref,
    dev_ref,
    out_ref,
    density_ref,
    place_ref,
    sum_ref,
    local_ref,
):
    leaves = leaves_ref.shape[0]
    rows = leaves * LEAF_ROWS
    group_count, dom_count = group_far_ref.shape[1], far_ref.shape[1]
    group, me = lax.axis_index("group"), lax.axis_index("dom")

    is_odd = jnp.bitwise_and(me, 1) == 1
    even, odd = even_ref[...], odd_ref[...]
    window = (jnp.where(is_odd, even, odd), halo_ref[...], jnp.where(is_odd, odd, even))
    ones = jnp.ones((LANES, LANES), jnp.bfloat16)
    diagonal = iota((8, LANES), 0) == iota((8, LANES), 1)
    spread = []
    for side, held in enumerate(window):
        density_ref[side * rows : (side + 1) * rows, :] = held[:rows]
        for k in range(3):
            spread.append(jnp.where(diagonal, held[rows + k : rows + k + 1], 0.0))
    spread = jnp.concatenate(spread, axis=0).astype(jnp.bfloat16)
    place_ref[...] = SIDE * jnp.dot(spread, ones, preferred_element_type=jnp.float32)

    sent = expansion_ref[...]
    moments, bounds = sent[:, 0, :], sent[:, 1, :]
    lane = iota((1, LANES), 1)
    unit_row = pattern(lane % RANK)
    unit_column = pattern(iota((RANK, LANES), 0))
    group_bounds = []
    for h in range(group_count):
        part = bounds[h * dom_count : (h + 1) * dom_count]
        low = jnp.min(part, axis=0, keepdims=True)
        high = jnp.max(part, axis=0, keepdims=True)
        group_bounds.append(jnp.where(lane < 3, low, high))
    own_group_bounds = group_bounds[0]
    for h in range(1, group_count):
        own_group_bounds = jnp.where(group == h, group_bounds[h], own_group_bounds)
    target = nodes(own_group_bounds, unit_column)
    total = jnp.zeros((RANK, LANES), jnp.float32)
    for h in range(group_count):
        raised = jnp.sum(moments[h * dom_count : (h + 1) * dom_count], axis=0, keepdims=True)
        raised = jnp.where(lane >= RANK, raised, 0.0) * group_far_ref[0, h].astype(jnp.float32)
        total = total + node_coupling(target, nodes(group_bounds[h], unit_row)) * raised
    group_local = vol_weight * lane_sums(total)[:1, :RANK]
    local = jnp.sum(dev_ref[0] * group_local, axis=1, keepdims=True)
    base = group * dom_count
    own = expansion_ref[pl.ds(base, dom_count)]
    own_bounds = expansion_ref[pl.ds(base + me, 1)][:, 1, :]
    target = nodes(own_bounds, unit_column)
    source = nodes(own[:, 1, :], unit_row)
    own_moments = jnp.where(lane < RANK, own[:, 0, :], 0.0)
    total = jnp.zeros((RANK, LANES), jnp.float32)
    for s in range(dom_count):
        coupling = node_coupling(target, [x[s : s + 1] for x in source])
        total = total + coupling * (own_moments[s : s + 1] * far_ref[0, s].astype(jnp.float32))
    local = local + vol_weight * jnp.sum(total, axis=1, keepdims=True)
    local_ref[...] = jnp.broadcast_to(local, (RANK, LANES))

    lane8, row8 = iota((8, LANES), 1), iota((8, LANES), 0)
    half = (lane8 // (SIDE * SIDE)).astype(jnp.float32)
    at_y = (lane8 // SIDE % SIDE).astype(jnp.float32)
    along_z = (row8 - lane8 % SIDE).astype(jnp.float32)

    def place(position):
        side = (position >= leaves).astype(jnp.int32) + (position >= 2 * leaves).astype(jnp.int32)
        first = side * 24 + (position - side * leaves)
        return [place_ref[pl.ds(first + 8 * k, 1), :] for k in range(3)]

    def one_leaf(leaf, carry):
        own_place = place(leaf + leaves)
        for slot in range(NEARL):
            position = leaves_ref[leaf, slot]
            shift = [a - b for a, b in zip(own_place, place(position), strict=True)]
            rho = [density_ref[pl.ds(position * LEAF_ROWS + j, 1), :] for j in range(LEAF_ROWS)]
            along = shift[2] + along_z
            square_z = along * along + soft_square
            square_x = []
            for m in range(-6, SIDE):
                apart = shift[0] + (m - half)
                square_x.append(apart * apart)
            for y in range(SIDE):
                apart = shift[1] + (y - at_y)
                square = apart * apart + square_z
                kernel = [lax.rsqrt(x + square) for x in square_x]
                for x in range(SIDE):
                    value = kernel[x + 6] * rho[0]
                    for j in range(1, LEAF_ROWS):
                        value = value + kernel[x - 2 * j + 6] * rho[j]
                    at = slice((x * SIDE + y) * SIDE, (x * SIDE + y + 1) * SIDE)
                    if slot == 0:
                        sum_ref[at, :] = value
                    else:
                        sum_ref[at, :] += value
        near = vol_weight * lane_sums(sum_ref[...])[:1]
        spread_local = local_ref[...]
        for j in range(LEAF_ROWS):
            row = leaf * LEAF_ROWS + j
            at = pl.ds(pl.multiple_of(row * LANES, LANES), LANES)
            far = jnp.sum(weights_ref[:RANK, at] * spread_local, axis=0, keepdims=True)
            out_ref[pl.ds(row, 1), :] = near[:, j * LANES : (j + 1) * LANES] + far
        return carry

    lax.fori_loop(0, leaves, one_leaf, 0)


def in_hbm(x):
    return pltpu.with_memory_space_constraint(x, pltpu.HBM)


VMEM = pl.BlockSpec(memory_space=pltpu.VMEM)
SMEM = pl.BlockSpec(memory_space=pltpu.SMEM)
HBM = pl.BlockSpec(memory_space=pltpu.HBM)


def local(
    orbitals,
    density_rows,
    near_blocks,
    leaf_coords,
    near_leaves,
    leaf_basis,
    leaf_transfer,
    dev_transfer,
    dev_far,
    group_far,
):
    points, width = orbitals.shape
    leaves = leaf_coords.shape[1]
    rows = leaves * LEAF_ROWS
    natural = density_rows.shape[1]
    devices = lax.axis_size("group") * lax.axis_size("dom")
    dom_count = lax.axis_size("dom")
    f32 = jnp.float32
    params = pltpu.CompilerParams(vmem_limit_bytes=(24 << 20) + 4 * natural * natural)

    def prepare(gate):
        return pl.pallas_call(
            prepare_kernel,
            out_shape=(
                jax.ShapeDtypeStruct((points, width), jnp.bfloat16),
                jax.ShapeDtypeStruct((natural, width), jnp.bfloat16),
                jax.ShapeDtypeStruct((2 * RANK, points), f32),
            ),
            in_specs=[HBM] * 5 + [pl.BlockSpec(memory_space=pl.ANY)],
            out_specs=(VMEM, VMEM, VMEM),
            scratch_shapes=[
                pltpu.VMEM(near_blocks.shape, jnp.int32),
                pltpu.VMEM(leaf_basis.shape, f32),
                pltpu.VMEM(leaf_transfer.shape, f32),
                pltpu.VMEM(dev_transfer.shape, f32),
                pltpu.SemaphoreType.DMA((5,)),
            ],
            compiler_params=params,
            cost_estimate=pl.CostEstimate(
                flops=2 * 6 * 2 * RANK * RANK * points, bytes_accessed=8 << 20, transcendentals=0
            ),
            name="prepare",
        )(*[in_hbm(x) for x in (near_blocks, leaf_basis, leaf_transfer, dev_transfer, orbitals)], gate)

    held, other, (orbit, pick, weights) = gather_rows(density_rows, prepare)

    density, halo, expansion = pl.pallas_call(
        density_kernel,
        out_shape=(
            jax.ShapeDtypeStruct((rows, LANES), f32),
            jax.ShapeDtypeStruct((rows + 8, LANES), f32),
            jax.ShapeDtypeStruct((devices, 2, LANES), f32),
        ),
        in_specs=[SMEM] + [VMEM] * 6,
        out_specs=(VMEM, VMEM, VMEM),
        scratch_shapes=[pltpu.VMEM((width, natural), jnp.bfloat16)],
        compiler_params=params,
        cost_estimate=pl.CostEstimate(
            flops=2 * points * width * width, bytes_accessed=8 << 20, transcendentals=0
        ),
        name="density",
    )(near_blocks, leaf_coords, orbit, held, other, pick, weights)

    even = swap(halo, "dom", 1)
    pairs = [(i, i + 1 if i % 2 else i - 1) for i in range(1, dom_count - 1)]
    odd = lax.ppermute(halo, "dom", pairs)
    everyone = lax.all_to_all(expansion, ("group", "dom"), 0, 0)

    hartree = pl.pallas_call(
        potential_kernel,
        out_shape=jax.ShapeDtypeStruct((rows, LANES), f32),
        in_specs=[SMEM, SMEM, SMEM] + [VMEM] * 6,
        out_specs=VMEM,
        scratch_shapes=[
            pltpu.VMEM((3 * rows, LANES), f32),
            pltpu.VMEM((72, LANES), f32),
            pltpu.VMEM((LEAF, LANES), f32),
            pltpu.VMEM((RANK, LANES), f32),
        ],
        compiler_params=params,
        cost_estimate=pl.CostEstimate(
            flops=20 << 20, bytes_accessed=2 << 20, transcendentals=4 << 20
        ),
        name="potential",
    )(near_leaves, dev_far, group_far, halo, even, odd, everyone, weights, dev_transfer)
    return (density.reshape(-1), hartree.reshape(-1))


def solution(mesh):
    in_specs = (
        P(("group", "dom"), None),
        P(("group", "dom"), None),
        P(("group", "dom"), None),
        P(None, ("group", "dom")),
        P(("group", "dom"), None),
        P(None, ("group", "dom")),
        P(("group", "dom"), None, None),
        P(("group", "dom"), None, None),
        P(("group", "dom"), None),
        P("group", None),
    )
    out_specs = (P(("group", "dom")), P(("group", "dom")))
    return jax.shard_map(local, mesh=mesh, in_specs=in_specs, out_specs=out_specs, check_vma=False)
```

```python
import functools
import math

import jax
import jax.numpy as jnp
from jax import lax
from jax.experimental import pallas as pl
from jax.experimental.pallas import tpu as pltpu
from jax.sharding import PartitionSpec as P

SIDE = 8
LEAF = 512
CHEB = 4
RANK = CHEB * CHEB * CHEB
BW = 16
BLOCK_ROWS = 2 * BW
NEARL = 3
LANES = 128
LEAF_ROWS = LEAF // LANES
HIGHEST = lax.Precision.HIGHEST

vol_weight = 0.1
soft_square = 1.0


def xor_stages(count):
    bits = count.bit_length() - 1
    stages, bit = ([(2,)], 2) if bits > 1 else ([], 1)
    while bit < bits:
        wide = 2 if bit + 1 < bits else 1
        stages.append(tuple(m << bit for m in range(1, 1 << wide)))
        bit += wide
    return stages


def swap(value, axis, mask):
    return lax.ppermute(value, axis, [(i, i ^ mask) for i in range(lax.axis_size(axis))])


def farthest_first(mask):
    return -(mask & -mask), -mask


def gather_rows(rows, load, prepare):
    held, loaded = rows, load()
    for stage, masks in enumerate(xor_stages(lax.axis_size("dom"))):
        if stage == 1:
            held, loaded = lax.optimization_barrier((held, loaded))
            result = prepare(loaded)
        arrived = {m: swap(held, "dom", m) for m in sorted(masks, key=farthest_first)}
        held = jnp.concatenate([held] + [arrived[m] for m in masks], axis=0)
    held, result = lax.optimization_barrier((held, result))
    return held, swap(held, "dom", 1), loaded, result


def iota(shape, dim):
    return lax.broadcasted_iota(jnp.int32, shape, dim)


def lane_sums(x):
    return jnp.sum(x.T, axis=0, keepdims=True)


def spread_rows(row, count):
    size = row.shape[1]
    diagonal = iota((count, size), 0) == iota((count, size), 1)
    diagonal = jnp.where(diagonal, row, 0.0).astype(jnp.bfloat16)
    return jnp.dot(
        diagonal, jnp.ones((size, LANES), jnp.bfloat16), preferred_element_type=jnp.float32
    )


def split(x):
    high = x.astype(jnp.bfloat16)
    return high, (x - high.astype(jnp.float32)).astype(jnp.bfloat16)


def load_kernel(
    near_hbm,
    transfer_hbm,
    dev_hbm,
    basis_hbm,
    orbitals_hbm,
    orbit_ref,
    pick_ref,
    weights_ref,
    near_ref,
    transfer_ref,
    dev_ref,
    basis_ref,
    sems,
):
    moves = ((near_hbm, near_ref), (transfer_hbm, transfer_ref), (dev_hbm, dev_ref))
    moves += ((basis_hbm, basis_ref), (orbitals_hbm, orbit_ref))
    copies = [pltpu.make_async_copy(a, b, sems.at[i]) for i, (a, b) in enumerate(moves)]
    for copy in copies:
        copy.start()
    copies[0].wait()
    blocks = near_ref.shape[1]
    width = blocks * BW
    expand = (iota((blocks, width), 1) // BW == iota((blocks, width), 0)).astype(jnp.float32)
    near = jnp.broadcast_to(near_ref[...].astype(jnp.float32), (8, blocks))
    column = jnp.dot(near, expand, preferred_element_type=jnp.float32)[:1].astype(jnp.int32) * BW
    column = column + iota((1, width), 1) % BW
    for start in range(0, pick_ref.shape[0], LEAF):
        size = min(LEAF, pick_ref.shape[0] - start)
        hit = iota((size, width), 0) + start == column
        pick_ref[start : start + size, :] = jnp.where(hit, 1.0, 0.0).astype(jnp.bfloat16)
    for copy in copies[1:4]:
        copy.wait()
    leaves = transfer_ref.shape[0]
    transfer = transfer_ref[...].reshape(leaves * RANK, RANK)
    raised = jnp.dot(transfer, dev_ref[0], precision=HIGHEST, preferred_element_type=jnp.float32)
    high, low = split(jnp.concatenate([transfer, raised], axis=1))
    for leaf in range(leaves):
        at, points = slice(leaf * RANK, (leaf + 1) * RANK), slice(leaf * LEAF, (leaf + 1) * LEAF)
        basis_high, basis_low = split(basis_ref[:, points])
        weights_ref[:, points] = lax.dot_general(
            jnp.concatenate([high[at], high[at], low[at]], axis=0),
            jnp.concatenate([basis_high, basis_low, basis_high], axis=0),
            (((0,), (0,)), ((), ())),
            preferred_element_type=jnp.float32,
        )
    copies[4].wait()


def prepare_kernel(
    reorder, far_hbm, group_far_hbm, orbit_ref, pick_ref, mask_ref, *refs
):
    far_ref, group_far_ref, sems = refs[-3:]
    moves = ((far_hbm, far_ref), (group_far_hbm, group_far_ref))
    copies = [pltpu.make_async_copy(a, b, sems.at[i]) for i, (a, b) in enumerate(moves)]
    for copy in copies:
        copy.start()
    if reorder:
        for start in range(0, orbit_ref.shape[0], LEAF):
            part = lax.dot_general(
                orbit_ref[start : start + LEAF, :],
                pick_ref[...],
                (((1,), (1,)), ((), ())),
                preferred_element_type=jnp.float32,
            )
            refs[0][start : start + LEAF, :] = part.astype(jnp.bfloat16)
    for copy in copies:
        copy.wait()
    dom_count, group_count = far_ref.shape[1], group_far_ref.shape[1]
    mask_ref[:dom_count, :] = spread_rows(far_ref[...].astype(jnp.float32), dom_count)
    mask_ref[dom_count:, :] = spread_rows(group_far_ref[...].astype(jnp.float32), group_count)


def density_kernel(
    reorder, coords_ref, orbit_ref, held_ref, other_ref, weights_ref, pick_ref, near_ref, *refs
):
    halo_ref, expansion_ref, rows_ref = refs
    leaves = coords_ref.shape[1]
    me = lax.axis_index("dom")
    if reorder:
        pair_rows = BLOCK_ROWS
        mine = jnp.bitwise_and(me, 1) == 0
        for c in range(held_ref.shape[0] // pair_rows):
            first = jnp.bitwise_xor(lax.shift_right_logical(me, 1), c) * pair_rows
            at = pl.ds(pl.multiple_of(first, pair_rows), pair_rows)
            held, other = held_ref[at, :], other_ref[at, :]
            base = 2 * c * pair_rows
            rows_ref[base : base + pair_rows, :] = jnp.where(mine, held, other)
            rows_ref[base + pair_rows : base + 2 * pair_rows, :] = jnp.where(mine, other, held)
        matrix = rows_ref[...]
    else:
        for k in range(near_ref.shape[1]):
            block = near_ref[0, k]
            apart = jnp.bitwise_xor(lax.shift_right_logical(block, 1), me)
            first = lax.shift_right_logical(apart, 1) * BLOCK_ROWS + jnp.bitwise_and(block, 1) * BW
            at = pl.ds(pl.multiple_of(first, BW), BW)
            mine = jnp.bitwise_and(apart, 1) == 0
            rows_ref[k * BW : (k + 1) * BW, :] = jnp.where(mine, held_ref[at, :], other_ref[at, :])
        matrix = jnp.dot(rows_ref[...], pick_ref[...], preferred_element_type=jnp.float32)
        matrix = matrix.astype(jnp.bfloat16)
    total = jnp.zeros((2 * RANK, LANES), jnp.float32)
    tile = LEAF // 2
    for start in range(0, leaves * LEAF, tile):
        orbit = orbit_ref[start : start + tile, :]
        product = jnp.dot(orbit, matrix, preferred_element_type=jnp.float32)
        product = product * orbit.astype(jnp.float32)
        folded = product[:, :LANES]
        for at in range(LANES, product.shape[1], LANES):
            folded = folded + product[:, at : at + LANES]
        for j in range(tile // LANES):
            row = start // LANES + j
            part = lane_sums(folded[j * LANES : (j + 1) * LANES])
            halo_ref[row : row + 1, :] = part
            total = total + weights_ref[:, row * LANES : (row + 1) * LANES] * part
    coords = coords_ref[...].astype(jnp.float32)
    rows = leaves * LEAF_ROWS
    halo_ref[rows:, :] = jnp.zeros((halo_ref.shape[0] - rows, LANES), jnp.float32)
    halo_ref[rows : rows + 3, :leaves] = coords
    low = SIDE * jnp.min(coords, axis=1, keepdims=True)
    high = SIDE * jnp.max(coords, axis=1, keepdims=True) + (SIDE - 1)
    lane = iota((1, LANES), 1)
    bounds = jnp.zeros((1, LANES), jnp.float32)
    for k in range(3):
        bounds = jnp.where(lane == k, low[k : k + 1], bounds)
        bounds = jnp.where(lane == 3 + k, high[k : k + 1], bounds)
    both = jnp.concatenate([lane_sums(total), bounds], axis=0)
    expansion_ref[...] = jnp.broadcast_to(both[None], expansion_ref.shape)


def pattern(index):
    steps = (index // (CHEB * CHEB) % CHEB, index // CHEB % CHEB, index % CHEB)
    points = [math.cos((2 * a + 1) * math.pi / (2 * CHEB)) for a in range(CHEB)]
    out = []
    for step in steps:
        value = jnp.full(index.shape, points[CHEB - 1], jnp.float32)
        for a in range(CHEB - 1):
            value = jnp.where(step == a, points[a], value)
        out.append(value)
    return out


def nodes(bounds, unit):
    out = []
    for k in range(3):
        low, high = bounds[:, k : k + 1], bounds[:, 3 + k : 4 + k]
        out.append(0.5 * (low + high) + 0.5 * (high - low) * unit[k])
    return out


def node_coupling(target, source):
    square = soft_square
    for t, s in zip(target, source, strict=True):
        apart = t - s
        square = square + apart * apart
    return lax.rsqrt(square)


def places(halo, rows):
    parts = [spread_rows(halo[rows + k : rows + k + 1], 8) for k in range(3)]
    return SIDE * jnp.concatenate(parts, axis=0)


def add_pair(sum_ref, own_place, place, rho, fresh):
    lane, row = iota((8, LANES), 1), iota((8, LANES), 0)
    low = lane < LANES // 2
    half = jnp.where(low, 0.0, 1.0)
    at_y = (lane // SIDE % SIDE).astype(jnp.float32)
    along_z = (row - lane % SIDE).astype(jnp.float32)
    shift = [jnp.broadcast_to(a - b, (8, LANES)) for a, b in zip(own_place, place, strict=True)]
    rho = [jnp.broadcast_to(r, (8, LANES)) for r in rho]
    swapped = [pltpu.roll(r, LANES // 2, 1) for r in rho]
    along = shift[2] + along_z
    square_z = along * along + soft_square
    square_x = []
    for m in range(-6, SIDE + 2, 2):
        apart = shift[0] + (m - half)
        square_x.append(apart * apart)
    for y in range(SIDE):
        apart = shift[1] + (y - at_y)
        square = apart * apart + square_z
        even = [lax.rsqrt(x + square) for x in square_x]
        odd = [jnp.where(low, a, b) for a, b in zip(even[:-1], even[1:], strict=True)]
        for x in range(SIDE):
            first = x // 2 + 3
            kernel, density = (odd, swapped) if x % 2 else (even, rho)
            value = kernel[first] * density[0]
            for j in range(1, LEAF_ROWS):
                value = value + kernel[first - j] * density[j]
            at = slice((x * SIDE + y) * SIDE, (x * SIDE + y + 1) * SIDE)
            if fresh:
                sum_ref[at, :] = value
            else:
                sum_ref[at, :] += value


def near_kernel(leaves_ref, halo_ref, even_ref, odd_ref, out_ref, values_ref, density_ref, place_ref, sum_ref):
    leaves = leaves_ref.shape[0]
    rows = leaves * LEAF_ROWS
    is_odd = jnp.bitwise_and(lax.axis_index("dom"), 1) == 1
    even, odd = even_ref[...], odd_ref[...]
    window = (jnp.where(is_odd, even, odd), halo_ref[...], jnp.where(is_odd, odd, even))
    for side, held in enumerate(window):
        density_ref[side * rows : (side + 1) * rows, :] = held[:rows]
        place_ref[24 * side : 24 * (side + 1), :] = places(held, rows)
    values_ref[...] = halo_ref[:rows, :]

    def one_leaf(leaf, carry):
        own_place = [place_ref[pl.ds(24 + leaf + 8 * k, 1), :] for k in range(3)]
        for slot in range(NEARL):
            position = leaves_ref[leaf, slot]
            side = (position >= leaves).astype(jnp.int32)
            side = side + (position >= 2 * leaves).astype(jnp.int32)
            first = 24 * side + position - leaves * side
            place = [place_ref[pl.ds(first + 8 * k, 1), :] for k in range(3)]
            rho = [density_ref[pl.ds(position * LEAF_ROWS + j, 1), :] for j in range(LEAF_ROWS)]
            add_pair(sum_ref, own_place, place, rho, slot == 0)
        for j in range(LEAF_ROWS):
            part = lane_sums(sum_ref[j * LANES : (j + 1) * LANES, :])
            out_ref[pl.ds(leaf * LEAF_ROWS + j, 1), :] = vol_weight * part
        return carry

    lax.fori_loop(0, leaves, one_leaf, 0)


def far_field(expansion_ref, mask_ref, dev_ref):
    dom_count = lax.axis_size("dom")
    group_count = mask_ref.shape[0] - dom_count
    group, me = lax.axis_index("group"), lax.axis_index("dom")
    sent = expansion_ref[...]
    moments, bounds = sent[:, 0, :], sent[:, 1, :]
    lane = iota((1, LANES), 1)
    unit_row = pattern(lane % RANK)
    unit_column = pattern(iota((RANK, LANES), 0))
    group_bounds = []
    for h in range(group_count):
        part = bounds[h * dom_count : (h + 1) * dom_count]
        low = jnp.min(part, axis=0, keepdims=True)
        high = jnp.max(part, axis=0, keepdims=True)
        group_bounds.append(jnp.where(lane < 3, low, high))
    own_group_bounds = group_bounds[0]
    for h in range(1, group_count):
        own_group_bounds = jnp.where(group == h, group_bounds[h], own_group_bounds)
    target = nodes(own_group_bounds, unit_column)
    total = jnp.zeros((RANK, LANES), jnp.float32)
    for h in range(group_count):
        raised = jnp.sum(moments[h * dom_count : (h + 1) * dom_count], axis=0, keepdims=True)
        raised = jnp.where(lane >= RANK, raised, 0.0) * mask_ref[dom_count + h : dom_count + h + 1, :]
        total = total + node_coupling(target, nodes(group_bounds[h], unit_row)) * raised
    group_local = vol_weight * lane_sums(total)
    local = jnp.sum(dev_ref[0] * group_local, axis=1, keepdims=True)
    base = group * dom_count
    own = expansion_ref[pl.ds(base, dom_count)]
    own_bounds = expansion_ref[pl.ds(base + me, 1)][:, 1, :]
    target = nodes(own_bounds, unit_column)
    source = nodes(own[:, 1, :], unit_row)
    own_moments = jnp.where(lane < RANK, own[:, 0, :], 0.0) * mask_ref[:dom_count, :]
    total = jnp.zeros((RANK, LANES), jnp.float32)
    for s in range(dom_count):
        coupling = node_coupling(target, [x[s : s + 1] for x in source])
        total = total + coupling * own_moments[s : s + 1]
    local = local + vol_weight * jnp.sum(total, axis=1, keepdims=True)
    return jnp.broadcast_to(local, (RANK, LANES))


def potential_kernel(expansion_ref, mask_ref, weights_ref, dev_ref, near_ref, out_ref):
    local = far_field(expansion_ref, mask_ref, dev_ref)
    for row in range(out_ref.shape[0]):
        at = slice(row * LANES, (row + 1) * LANES)
        far = jnp.sum(weights_ref[:RANK, at] * local, axis=0, keepdims=True)
        out_ref[row : row + 1, :] = near_ref[row : row + 1, :] + far


def in_hbm(x):
    return pltpu.with_memory_space_constraint(x, pltpu.HBM)


VMEM = pl.BlockSpec(memory_space=pltpu.VMEM)
SMEM = pl.BlockSpec(memory_space=pltpu.SMEM)
HBM = pl.BlockSpec(memory_space=pltpu.HBM)
ANY = pl.BlockSpec(memory_space=pl.ANY)


def local(
    orbitals,
    density_rows,
    near_blocks,
    leaf_coords,
    near_leaves,
    leaf_basis,
    leaf_transfer,
    dev_transfer,
    dev_far,
    group_far,
):
    points, width = orbitals.shape
    leaves = leaf_coords.shape[1]
    rows = leaves * LEAF_ROWS
    natural = density_rows.shape[1]
    devices = lax.axis_size("group") * lax.axis_size("dom")
    dom_count = lax.axis_size("dom")
    f32 = jnp.float32
    reorder = natural == width
    params = pltpu.CompilerParams(vmem_limit_bytes=(24 << 20) + 4 * natural * natural)

    def cost(flops, transcendentals=0):
        return pl.CostEstimate(
            flops=flops, bytes_accessed=4 << 20, transcendentals=transcendentals
        )

    def load():
        operands = (near_blocks, leaf_transfer, dev_transfer, leaf_basis)
        return pl.pallas_call(
            load_kernel,
            out_shape=(
                jax.ShapeDtypeStruct((points, width), jnp.bfloat16),
                jax.ShapeDtypeStruct((natural, width), jnp.bfloat16),
                jax.ShapeDtypeStruct((2 * RANK, points), f32),
            ),
            in_specs=[HBM] * 5,
            out_specs=(VMEM, VMEM, VMEM),
            scratch_shapes=[pltpu.VMEM(x.shape, x.dtype) for x in operands]
            + [pltpu.SemaphoreType.DMA((5,))],
            compiler_params=params,
            cost_estimate=cost(1 << 20),
            name="load",
        )(*[in_hbm(x) for x in operands], in_hbm(orbitals))

    def prepare(loaded):
        orbit, pick, _ = loaded
        operands = (dev_far, group_far)
        shapes = [jax.ShapeDtypeStruct((dev_far.shape[1] + group_far.shape[1], LANES), f32)]
        if reorder:
            shapes.append(jax.ShapeDtypeStruct((points, natural), jnp.bfloat16))
        out = pl.pallas_call(
            functools.partial(prepare_kernel, reorder),
            out_shape=shapes,
            in_specs=[HBM] * 2 + [VMEM] * 2,
            out_specs=[VMEM] * len(shapes),
            scratch_shapes=[pltpu.VMEM(x.shape, x.dtype) for x in operands]
            + [pltpu.SemaphoreType.DMA((2,))],
            compiler_params=params,
            cost_estimate=cost(2 * points * width * natural),
            name="prepare",
        )(*[in_hbm(x) for x in operands], orbit, pick)
        return out if reorder else [*out, orbit]

    held, other, (_, pick, weights), (mask, orbit) = gather_rows(density_rows, load, prepare)

    halo, expansion = pl.pallas_call(
        functools.partial(density_kernel, reorder),
        out_shape=(
            jax.ShapeDtypeStruct((rows + 8, LANES), f32),
            jax.ShapeDtypeStruct((devices, 2, LANES), f32),
        ),
        in_specs=[VMEM] * 5 + ([ANY, ANY] if reorder else [VMEM, SMEM]),
        out_specs=(VMEM, VMEM),
        scratch_shapes=[pltpu.VMEM((width, natural), jnp.bfloat16)],
        compiler_params=params,
        cost_estimate=cost(2 * points * width * width),
        name="density",
    )(leaf_coords, orbit, held, other, weights, pick, near_blocks)

    even = swap(halo, "dom", 1)
    pairs = [(i, i + 1 if i % 2 else i - 1) for i in range(1, dom_count - 1)]
    odd = lax.ppermute(halo, "dom", pairs)
    everyone = lax.all_to_all(expansion, ("group", "dom"), 0, 0)

    table = jax.ShapeDtypeStruct((rows, LANES), f32)
    near, density = pl.pallas_call(
        near_kernel,
        out_shape=(table, table),
        in_specs=[SMEM] + [VMEM] * 3,
        out_specs=(VMEM, VMEM),
        scratch_shapes=[
            pltpu.VMEM((3 * rows, LANES), f32),
            pltpu.VMEM((72, LANES), f32),
            pltpu.VMEM((LEAF, LANES), f32),
        ],
        compiler_params=params,
        cost_estimate=cost(20 << 20, 4 << 20),
        name="near",
    )(near_leaves, halo, even, odd)
    hartree = pl.pallas_call(
        potential_kernel,
        out_shape=table,
        in_specs=[VMEM] * 5,
        out_specs=VMEM,
        compiler_params=params,
        cost_estimate=cost(4 << 20, 1 << 20),
        name="potential",
    )(everyone, mask, weights, dev_transfer, near)
    return (density.reshape(-1), hartree.reshape(-1))


def solution(mesh):
    in_specs = (
        P(("group", "dom"), None),
        P(("group", "dom"), None),
        P(("group", "dom"), None),
        P(None, ("group", "dom")),
        P(("group", "dom"), None),
        P(None, ("group", "dom")),
        P(("group", "dom"), None, None),
        P(("group", "dom"), None, None),
        P(("group", "dom"), None),
        P("group", None),
    )
    out_specs = (P(("group", "dom")), P(("group", "dom")))
    return jax.shard_map(local, mesh=mesh, in_specs=in_specs, out_specs=out_specs, check_vma=False)
```

```python
import functools
import math

import jax
import jax.numpy as jnp
from jax import lax
from jax.experimental import pallas as pl
from jax.experimental.pallas import tpu as pltpu
from jax.sharding import PartitionSpec as P

SIDE = 8
LEAF = 512
CHEB = 4
RANK = CHEB * CHEB * CHEB
BW = 16
BLOCK_ROWS = 2 * BW
NEARL = 3
LANES = 128
LEAF_ROWS = LEAF // LANES
TILE = 256
HIGHEST = lax.Precision.HIGHEST

vol_weight = 0.1
soft_square = 1.0


def xor_stages(count):
    bits = count.bit_length() - 1
    stages, bit = ([(2,)], 2) if bits > 1 else ([], 1)
    while bit < bits:
        wide = 2 if bit + 1 < bits else 1
        stages.append(tuple(m << bit for m in range(1, 1 << wide)))
        bit += wide
    return stages


def swap(value, axis, mask):
    return lax.ppermute(value, axis, [(i, i ^ mask) for i in range(lax.axis_size(axis))])


def farthest_first(mask):
    return -(mask & -mask), -mask


def gather_rows(rows, load, prepare):
    held, loaded = rows, load()
    for stage, masks in enumerate(xor_stages(lax.axis_size("dom"))):
        if stage == 1:
            held, loaded = lax.optimization_barrier((held, loaded))
            result = prepare(loaded)
        arrived = {m: swap(held, "dom", m) for m in sorted(masks, key=farthest_first)}
        held = jnp.concatenate([held] + [arrived[m] for m in masks], axis=0)
    held, result = lax.optimization_barrier((held, result))
    return held, swap(held, "dom", 1), loaded, result


def iota(shape, dim):
    return lax.broadcasted_iota(jnp.int32, shape, dim)


def lane_sums(x):
    return jnp.sum(x.T, axis=0, keepdims=True)


def spread_rows(row, count):
    size = row.shape[1]
    diagonal = iota((count, size), 0) == iota((count, size), 1)
    diagonal = jnp.where(diagonal, row, 0.0).astype(jnp.bfloat16)
    return jnp.dot(
        diagonal, jnp.ones((size, LANES), jnp.bfloat16), preferred_element_type=jnp.float32
    )


def split(x):
    high = x.astype(jnp.bfloat16)
    return high, (x - high.astype(jnp.float32)).astype(jnp.bfloat16)


def by_core(device, devices):
    chip = lax.shift_right_logical(device, 1)
    return jnp.bitwise_and(device, 1) * (devices // 2) + chip


def load_kernel(
    reorder,
    near_hbm,
    transfer_hbm,
    dev_hbm,
    basis_hbm,
    orbitals_hbm,
    orbit_ref,
    pick_ref,
    weights_ref,
    near_ref,
    transfer_ref,
    dev_ref,
    basis_ref,
    sems,
):
    moves = ((near_hbm, near_ref), (transfer_hbm, transfer_ref), (dev_hbm, dev_ref))
    moves += ((basis_hbm, basis_ref), (orbitals_hbm, orbit_ref))
    copies = [pltpu.make_async_copy(a, b, sems.at[i]) for i, (a, b) in enumerate(moves)]
    for copy in copies:
        copy.start()
    copies[0].wait()
    blocks = near_ref.shape[1]
    width = blocks * BW
    expand = (iota((blocks, width), 1) // BW == iota((blocks, width), 0)).astype(jnp.float32)
    near = near_ref[...]
    if reorder:
        device = by_core(lax.shift_right_logical(near, 1), blocks // 2)
        near = 2 * device + jnp.bitwise_and(near, 1)
    near = jnp.broadcast_to(near.astype(jnp.float32), (8, blocks))
    column = jnp.dot(near, expand, preferred_element_type=jnp.float32)[:1].astype(jnp.int32) * BW
    column = column + iota((1, width), 1) % BW
    for start in range(0, pick_ref.shape[0], LEAF):
        size = min(LEAF, pick_ref.shape[0] - start)
        hit = iota((size, width), 0) + start == column
        pick_ref[start : start + size, :] = jnp.where(hit, 1.0, 0.0).astype(jnp.bfloat16)
    for copy in copies[1:4]:
        copy.wait()
    leaves = transfer_ref.shape[0]
    transfer = transfer_ref[...].reshape(leaves * RANK, RANK)
    raised = jnp.dot(transfer, dev_ref[0], precision=HIGHEST, preferred_element_type=jnp.float32)
    high, low = split(jnp.concatenate([transfer, raised], axis=1))
    for leaf in range(leaves):
        at, points = slice(leaf * RANK, (leaf + 1) * RANK), slice(leaf * LEAF, (leaf + 1) * LEAF)
        basis_high, basis_low = split(basis_ref[:, points])
        weights_ref[:, points] = lax.dot_general(
            jnp.concatenate([high[at], high[at], low[at]], axis=0),
            jnp.concatenate([basis_high, basis_low, basis_high], axis=0),
            (((0,), (0,)), ((), ())),
            preferred_element_type=jnp.float32,
        )
    copies[4].wait()


def prepare_kernel(reorder, far_hbm, group_far_hbm, orbit_ref, pick_ref, mask_ref, *refs):
    far_ref, group_far_ref, sems = refs[-3:]
    moves = ((far_hbm, far_ref), (group_far_hbm, group_far_ref))
    copies = [pltpu.make_async_copy(a, b, sems.at[i]) for i, (a, b) in enumerate(moves)]
    for copy in copies:
        copy.start()
    if reorder:
        sorted_ref, order_ref = refs[:2]
        for start in range(0, orbit_ref.shape[0], LEAF):
            part = lax.dot_general(
                orbit_ref[start : start + LEAF, :],
                pick_ref[...],
                (((1,), (1,)), ((), ())),
                preferred_element_type=jnp.float32,
            )
            sorted_ref[start : start + LEAF, :] = part.astype(jnp.bfloat16)
        size = order_ref.shape[0]
        column = iota((size, 1), 0)
        place = by_core(column // BLOCK_ROWS, size // BLOCK_ROWS) * BLOCK_ROWS + column % BLOCK_ROWS
        hit = iota((size, size), 1) == place
        order_ref[...] = jnp.where(hit, 1.0, 0.0).astype(jnp.bfloat16)
    for copy in copies:
        copy.wait()
    dom_count, group_count = far_ref.shape[1], group_far_ref.shape[1]
    mask_ref[:dom_count, :] = spread_rows(far_ref[...].astype(jnp.float32), dom_count)
    mask_ref[dom_count:, :] = spread_rows(group_far_ref[...].astype(jnp.float32), group_count)


def half_matrix(pieces_ref, order_ref, rows_ref):
    chip = lax.shift_right_logical(lax.axis_index("dom"), 1)
    for c in range(pieces_ref.shape[0] // BLOCK_ROWS):
        first = jnp.bitwise_xor(chip, c) * BLOCK_ROWS
        at = pl.ds(pl.multiple_of(first, BLOCK_ROWS), BLOCK_ROWS)
        rows_ref[c * BLOCK_ROWS : (c + 1) * BLOCK_ROWS, :] = pieces_ref[at, :]
    matrix = jnp.dot(rows_ref[...], order_ref[...], preferred_element_type=jnp.float32)
    return matrix.astype(jnp.bfloat16)


def quadratic(orbit_ref, start, columns, matrix):
    points = slice(start, start + TILE)
    product = jnp.dot(orbit_ref[points, columns], matrix, preferred_element_type=jnp.float32)
    product = product * orbit_ref[points, :].astype(jnp.float32)
    folded = product[:, :LANES]
    for at in range(LANES, product.shape[1], LANES):
        folded = folded + product[:, at : at + LANES]
    return folded


def core_columns(core, width):
    return pl.ds(pl.multiple_of(core * (width // 2), LANES), width // 2)


def first_kernel(orbit_ref, held_ref, order_ref, out_ref, rows_ref):
    matrix = half_matrix(held_ref, order_ref, rows_ref)
    columns = core_columns(jnp.bitwise_and(lax.axis_index("dom"), 1), orbit_ref.shape[1])
    for start in range(0, orbit_ref.shape[0], TILE):
        out_ref[start : start + TILE, :] = quadratic(orbit_ref, start, columns, matrix)


def density_kernel(reorder, coords_ref, orbit_ref, other_ref, weights_ref, pick_ref, *refs):
    *inputs, halo_ref, expansion_ref, rows_ref = refs
    leaves = coords_ref.shape[1]
    me = lax.axis_index("dom")
    if reorder:
        matrix = half_matrix(other_ref, pick_ref, rows_ref)
        columns = core_columns(1 - jnp.bitwise_and(me, 1), orbit_ref.shape[1])
    else:
        held_ref, near_ref = inputs
        for k in range(near_ref.shape[1]):
            block = near_ref[0, k]
            apart = jnp.bitwise_xor(lax.shift_right_logical(block, 1), me)
            first = lax.shift_right_logical(apart, 1) * BLOCK_ROWS + jnp.bitwise_and(block, 1) * BW
            at = pl.ds(pl.multiple_of(first, BW), BW)
            mine = jnp.bitwise_and(apart, 1) == 0
            rows_ref[k * BW : (k + 1) * BW, :] = jnp.where(mine, held_ref[at, :], other_ref[at, :])
        matrix = jnp.dot(rows_ref[...], pick_ref[...], preferred_element_type=jnp.float32)
        matrix = matrix.astype(jnp.bfloat16)
        columns = slice(None)
    total = jnp.zeros((2 * RANK, LANES), jnp.float32)
    for start in range(0, leaves * LEAF, TILE):
        folded = quadratic(orbit_ref, start, columns, matrix)
        if reorder:
            folded = folded + inputs[0][start : start + TILE, :]
        for j in range(TILE // LANES):
            row = start // LANES + j
            part = lane_sums(folded[j * LANES : (j + 1) * LANES])
            halo_ref[row : row + 1, :] = part
            total = total + weights_ref[:, row * LANES : (row + 1) * LANES] * part
    coords = coords_ref[...].astype(jnp.float32)
    rows = leaves * LEAF_ROWS
    halo_ref[rows:, :] = jnp.zeros((halo_ref.shape[0] - rows, LANES), jnp.float32)
    halo_ref[rows : rows + 3, :leaves] = coords
    low = SIDE * jnp.min(coords, axis=1, keepdims=True)
    high = SIDE * jnp.max(coords, axis=1, keepdims=True) + (SIDE - 1)
    lane = iota((1, LANES), 1)
    bounds = jnp.zeros((1, LANES), jnp.float32)
    for k in range(3):
        bounds = jnp.where(lane == k, low[k : k + 1], bounds)
        bounds = jnp.where(lane == 3 + k, high[k : k + 1], bounds)
    both = jnp.concatenate([lane_sums(total), bounds], axis=0)
    expansion_ref[...] = jnp.broadcast_to(both[None], expansion_ref.shape)


def pattern(index):
    steps = (index // (CHEB * CHEB) % CHEB, index // CHEB % CHEB, index % CHEB)
    points = [math.cos((2 * a + 1) * math.pi / (2 * CHEB)) for a in range(CHEB)]
    out = []
    for step in steps:
        value = jnp.full(index.shape, points[CHEB - 1], jnp.float32)
        for a in range(CHEB - 1):
            value = jnp.where(step == a, points[a], value)
        out.append(value)
    return out


def nodes(bounds, unit):
    out = []
    for k in range(3):
        low, high = bounds[:, k : k + 1], bounds[:, 3 + k : 4 + k]
        out.append(0.5 * (low + high) + 0.5 * (high - low) * unit[k])
    return out


def node_coupling(target, source):
    square = soft_square
    for t, s in zip(target, source, strict=True):
        apart = t - s
        square = square + apart * apart
    return lax.rsqrt(square)


def places(halo, rows):
    parts = [spread_rows(halo[rows + k : rows + k + 1], 8) for k in range(3)]
    return SIDE * jnp.concatenate(parts, axis=0)


def add_pair(sum_ref, own_place, place, rho, fresh):
    lane, row = iota((8, LANES), 1), iota((8, LANES), 0)
    low = lane < LANES // 2
    half = jnp.where(low, 0.0, 1.0)
    at_y = (lane // SIDE % SIDE).astype(jnp.float32)
    along_z = (row - lane % SIDE).astype(jnp.float32)
    shift = [jnp.broadcast_to(a - b, (8, LANES)) for a, b in zip(own_place, place, strict=True)]
    rho = [jnp.broadcast_to(r, (8, LANES)) for r in rho]
    swapped = [pltpu.roll(r, LANES // 2, 1) for r in rho]
    along = shift[2] + along_z
    square_z = along * along + soft_square
    square_x = []
    for m in range(-6, SIDE + 2, 2):
        apart = shift[0] + (m - half)
        square_x.append(apart * apart)
    for y in range(SIDE):
        apart = shift[1] + (y - at_y)
        square = apart * apart + square_z
        even = [lax.rsqrt(x + square) for x in square_x]
        odd = [jnp.where(low, a, b) for a, b in zip(even[:-1], even[1:], strict=True)]
        for x in range(SIDE):
            first = x // 2 + 3
            kernel, density = (odd, swapped) if x % 2 else (even, rho)
            value = kernel[first] * density[0]
            for j in range(1, LEAF_ROWS):
                value = value + kernel[first - j] * density[j]
            at = slice((x * SIDE + y) * SIDE, (x * SIDE + y + 1) * SIDE)
            if fresh:
                sum_ref[at, :] = value
            else:
                sum_ref[at, :] += value


def near_kernel(leaves_ref, halo_ref, even_ref, odd_ref, out_ref, density_ref, place_ref, sum_ref):
    leaves = leaves_ref.shape[0]
    rows = leaves * LEAF_ROWS
    is_odd = jnp.bitwise_and(lax.axis_index("dom"), 1) == 1
    even, odd = even_ref[...], odd_ref[...]
    window = (jnp.where(is_odd, even, odd), halo_ref[...], jnp.where(is_odd, odd, even))
    for side, held in enumerate(window):
        density_ref[side * rows : (side + 1) * rows, :] = held[:rows]
        place_ref[24 * side : 24 * (side + 1), :] = places(held, rows)

    def one_leaf(leaf, carry):
        own_place = [place_ref[pl.ds(24 + leaf + 8 * k, 1), :] for k in range(3)]
        for slot in range(NEARL):
            position = leaves_ref[leaf, slot]
            side = (position >= leaves).astype(jnp.int32)
            side = side + (position >= 2 * leaves).astype(jnp.int32)
            first = 24 * side + position - leaves * side
            place = [place_ref[pl.ds(first + 8 * k, 1), :] for k in range(3)]
            rho = [density_ref[pl.ds(position * LEAF_ROWS + j, 1), :] for j in range(LEAF_ROWS)]
            add_pair(sum_ref, own_place, place, rho, slot == 0)
        for j in range(LEAF_ROWS):
            part = lane_sums(sum_ref[j * LANES : (j + 1) * LANES, :])
            out_ref[pl.ds(leaf * LEAF_ROWS + j, 1), :] = vol_weight * part
        return carry

    lax.fori_loop(0, leaves, one_leaf, 0)


def far_field(expansion_ref, mask_ref, dev_ref):
    dom_count = lax.axis_size("dom")
    group_count = mask_ref.shape[0] - dom_count
    group, me = lax.axis_index("group"), lax.axis_index("dom")
    sent = expansion_ref[...]
    moments, bounds = sent[:, 0, :], sent[:, 1, :]
    lane = iota((1, LANES), 1)
    unit_row = pattern(lane % RANK)
    unit_column = pattern(iota((RANK, LANES), 0))
    group_bounds = []
    for h in range(group_count):
        part = bounds[h * dom_count : (h + 1) * dom_count]
        low = jnp.min(part, axis=0, keepdims=True)
        high = jnp.max(part, axis=0, keepdims=True)
        group_bounds.append(jnp.where(lane < 3, low, high))
    own_group_bounds = group_bounds[0]
    for h in range(1, group_count):
        own_group_bounds = jnp.where(group == h, group_bounds[h], own_group_bounds)
    target = nodes(own_group_bounds, unit_column)
    total = jnp.zeros((RANK, LANES), jnp.float32)
    for h in range(group_count):
        raised = jnp.sum(moments[h * dom_count : (h + 1) * dom_count], axis=0, keepdims=True)
        raised = jnp.where(lane >= RANK, raised, 0.0) * mask_ref[dom_count + h : dom_count + h + 1, :]
        total = total + node_coupling(target, nodes(group_bounds[h], unit_row)) * raised
    group_local = vol_weight * lane_sums(total)
    local = jnp.sum(dev_ref[0] * group_local, axis=1, keepdims=True)
    base = group * dom_count
    own = expansion_ref[pl.ds(base, dom_count)]
    own_bounds = expansion_ref[pl.ds(base + me, 1)][:, 1, :]
    target = nodes(own_bounds, unit_column)
    source = nodes(own[:, 1, :], unit_row)
    own_moments = jnp.where(lane < RANK, own[:, 0, :], 0.0) * mask_ref[:dom_count, :]
    total = jnp.zeros((RANK, LANES), jnp.float32)
    for s in range(dom_count):
        coupling = node_coupling(target, [x[s : s + 1] for x in source])
        total = total + coupling * own_moments[s : s + 1]
    local = local + vol_weight * jnp.sum(total, axis=1, keepdims=True)
    return jnp.broadcast_to(local, (RANK, LANES))


def potential_kernel(
    expansion_ref, mask_ref, weights_ref, dev_ref, near_ref, halo_ref, out_ref, density_ref
):
    density_ref[...] = halo_ref[: density_ref.shape[0], :]
    local = far_field(expansion_ref, mask_ref, dev_ref)
    for row in range(out_ref.shape[0]):
        at = slice(row * LANES, (row + 1) * LANES)
        far = jnp.sum(weights_ref[:RANK, at] * local, axis=0, keepdims=True)
        out_ref[row : row + 1, :] = near_ref[row : row + 1, :] + far


def in_hbm(x):
    return pltpu.with_memory_space_constraint(x, pltpu.HBM)


VMEM = pl.BlockSpec(memory_space=pltpu.VMEM)
SMEM = pl.BlockSpec(memory_space=pltpu.SMEM)
HBM = pl.BlockSpec(memory_space=pltpu.HBM)
ANY = pl.BlockSpec(memory_space=pl.ANY)


def local(
    orbitals,
    density_rows,
    near_blocks,
    leaf_coords,
    near_leaves,
    leaf_basis,
    leaf_transfer,
    dev_transfer,
    dev_far,
    group_far,
):
    points, width = orbitals.shape
    leaves = leaf_coords.shape[1]
    rows = leaves * LEAF_ROWS
    natural = density_rows.shape[1]
    devices = lax.axis_size("group") * lax.axis_size("dom")
    dom_count = lax.axis_size("dom")
    f32 = jnp.float32
    reorder = natural == width
    params = pltpu.CompilerParams(vmem_limit_bytes=(24 << 20) + 4 * natural * natural)

    def cost(flops, transcendentals=0):
        return pl.CostEstimate(
            flops=flops, bytes_accessed=4 << 20, transcendentals=transcendentals
        )

    def load():
        operands = (near_blocks, leaf_transfer, dev_transfer, leaf_basis)
        return pl.pallas_call(
            functools.partial(load_kernel, reorder),
            out_shape=(
                jax.ShapeDtypeStruct((points, width), jnp.bfloat16),
                jax.ShapeDtypeStruct((natural, width), jnp.bfloat16),
                jax.ShapeDtypeStruct((2 * RANK, points), f32),
            ),
            in_specs=[HBM] * 5,
            out_specs=(VMEM, VMEM, VMEM),
            scratch_shapes=[pltpu.VMEM(x.shape, x.dtype) for x in operands]
            + [pltpu.SemaphoreType.DMA((5,))],
            compiler_params=params,
            cost_estimate=cost(1 << 20),
            name="load",
        )(*[in_hbm(x) for x in operands], in_hbm(orbitals))

    def prepare(loaded):
        orbit, pick, _ = loaded
        operands = (dev_far, group_far)
        shapes = [jax.ShapeDtypeStruct((dev_far.shape[1] + group_far.shape[1], LANES), f32)]
        if reorder:
            shapes.append(jax.ShapeDtypeStruct((points, natural), jnp.bfloat16))
            shapes.append(jax.ShapeDtypeStruct((natural, natural), jnp.bfloat16))
        out = pl.pallas_call(
            functools.partial(prepare_kernel, reorder),
            out_shape=shapes,
            in_specs=[HBM] * 2 + [VMEM] * 2,
            out_specs=[VMEM] * len(shapes),
            scratch_shapes=[pltpu.VMEM(x.shape, x.dtype) for x in operands]
            + [pltpu.SemaphoreType.DMA((2,))],
            compiler_params=params,
            cost_estimate=cost(2 * points * width * natural),
            name="prepare",
        )(*[in_hbm(x) for x in operands], orbit, pick)
        return out if reorder else [*out, orbit, pick]

    held, other, (_, _, weights), (mask, orbit, pick) = gather_rows(density_rows, load, prepare)

    if reorder:
        rest = [
            pl.pallas_call(
                first_kernel,
                out_shape=jax.ShapeDtypeStruct((points, LANES), f32),
                in_specs=[VMEM] * 3,
                out_specs=VMEM,
                scratch_shapes=[pltpu.VMEM((natural // 2, natural), jnp.bfloat16)],
                compiler_params=params,
                cost_estimate=cost(points * width * width),
                name="first",
            )(orbit, held, pick)
        ]
        rows_shape = (natural // 2, natural)
    else:
        rest, rows_shape = [held, near_blocks], (width, natural)
    halo, expansion = pl.pallas_call(
        functools.partial(density_kernel, reorder),
        out_shape=(
            jax.ShapeDtypeStruct((rows + 8, LANES), f32),
            jax.ShapeDtypeStruct((devices, 2, LANES), f32),
        ),
        in_specs=[VMEM] * 6 + ([] if reorder else [SMEM]),
        out_specs=(VMEM, VMEM),
        scratch_shapes=[pltpu.VMEM(rows_shape, jnp.bfloat16)],
        compiler_params=params,
        cost_estimate=cost(points * width * width),
        name="density",
    )(leaf_coords, orbit, other, weights, pick, *rest)

    even = swap(halo, "dom", 1)
    pairs = [(i, i + 1 if i % 2 else i - 1) for i in range(1, dom_count - 1)]
    odd = lax.ppermute(halo, "dom", pairs)
    everyone = lax.all_to_all(expansion, ("group", "dom"), 0, 0)

    table = jax.ShapeDtypeStruct((rows, LANES), f32)
    near = pl.pallas_call(
        near_kernel,
        out_shape=table,
        in_specs=[SMEM] + [VMEM] * 3,
        out_specs=VMEM,
        scratch_shapes=[
            pltpu.VMEM((3 * rows, LANES), f32),
            pltpu.VMEM((72, LANES), f32),
            pltpu.VMEM((LEAF, LANES), f32),
        ],
        compiler_params=params,
        cost_estimate=cost(20 << 20, 4 << 20),
        name="near",
    )(pltpu.with_memory_space_constraint(near_leaves, pltpu.SMEM), halo, even, odd)
    hartree, density = pl.pallas_call(
        potential_kernel,
        out_shape=(table, table),
        in_specs=[VMEM] * 6,
        out_specs=(VMEM, VMEM),
        compiler_params=params,
        cost_estimate=cost(4 << 20, 1 << 20),
        name="potential",
    )(everyone, mask, weights, dev_transfer, near, halo)
    return (density.reshape(-1), hartree.reshape(-1))


def solution(mesh):
    in_specs = (
        P(("group", "dom"), None),
        P(("group", "dom"), None),
        P(("group", "dom"), None),
        P(None, ("group", "dom")),
        P(("group", "dom"), None),
        P(None, ("group", "dom")),
        P(("group", "dom"), None, None),
        P(("group", "dom"), None, None),
        P(("group", "dom"), None),
        P("group", None),
    )
    out_specs = (P(("group", "dom")), P(("group", "dom")))
    return jax.shard_map(local, mesh=mesh, in_specs=in_specs, out_specs=out_specs, check_vma=False)
```

```python
import functools
import math

import jax
import jax.numpy as jnp
from jax import lax
from jax.experimental import pallas as pl
from jax.experimental.pallas import tpu as pltpu
from jax.sharding import PartitionSpec as P

SIDE = 8
LEAF = 512
CHEB = 4
RANK = CHEB * CHEB * CHEB
BW = 16
BLOCK_ROWS = 2 * BW
NEARL = 3
LANES = 128
LEAF_ROWS = LEAF // LANES
TILE = 256
HIGHEST = lax.Precision.HIGHEST

vol_weight = 0.1
soft_square = 1.0


def xor_stages(count):
    bits = count.bit_length() - 1
    stages, bit = ([(2,)], 2) if bits > 1 else ([], 1)
    while bit < bits:
        wide = 2 if bit + 1 < bits else 1
        stages.append(tuple(m << bit for m in range(1, 1 << wide)))
        bit += wide
    return stages


def swap(value, axis, mask):
    return lax.ppermute(value, axis, [(i, i ^ mask) for i in range(lax.axis_size(axis))])


def farthest_first(mask):
    return -(mask & -mask), -mask


def gather_rows(rows, load, prepare):
    held, loaded = rows, load()
    for stage, masks in enumerate(xor_stages(lax.axis_size("dom"))):
        if stage == 1:
            held, loaded = lax.optimization_barrier((held, loaded))
            result = prepare(loaded)
        arrived = {m: swap(held, "dom", m) for m in sorted(masks, key=farthest_first)}
        held = jnp.concatenate([held] + [arrived[m] for m in masks], axis=0)
    held, result = lax.optimization_barrier((held, result))
    return held, swap(held, "dom", 1), loaded, result


def iota(shape, dim):
    return lax.broadcasted_iota(jnp.int32, shape, dim)


def lane_sums(x):
    return jnp.sum(x.T, axis=0, keepdims=True)


def spread_rows(row, count):
    size = row.shape[1]
    diagonal = iota((count, size), 0) == iota((count, size), 1)
    diagonal = jnp.where(diagonal, row, 0.0).astype(jnp.bfloat16)
    return jnp.dot(
        diagonal, jnp.ones((size, LANES), jnp.bfloat16), preferred_element_type=jnp.float32
    )


def split(x):
    high = x.astype(jnp.bfloat16)
    return high, (x - high.astype(jnp.float32)).astype(jnp.bfloat16)


def by_core(device, devices):
    chip = lax.shift_right_logical(device, 1)
    return jnp.bitwise_and(device, 1) * (devices // 2) + chip


def load_kernel(
    reorder,
    near_hbm,
    transfer_hbm,
    dev_hbm,
    basis_hbm,
    orbitals_hbm,
    orbit_ref,
    pick_ref,
    weights_ref,
    near_ref,
    transfer_ref,
    dev_ref,
    basis_ref,
    sems,
):
    moves = ((near_hbm, near_ref), (transfer_hbm, transfer_ref), (dev_hbm, dev_ref))
    moves += ((basis_hbm, basis_ref), (orbitals_hbm, orbit_ref))
    copies = [pltpu.make_async_copy(a, b, sems.at[i]) for i, (a, b) in enumerate(moves)]
    for copy in copies:
        copy.start()
    copies[0].wait()
    blocks = near_ref.shape[1]
    width = blocks * BW
    expand = (iota((blocks, width), 1) // BW == iota((blocks, width), 0)).astype(jnp.float32)
    near = near_ref[...]
    if reorder:
        device = by_core(lax.shift_right_logical(near, 1), blocks // 2)
        near = 2 * device + jnp.bitwise_and(near, 1)
    near = jnp.broadcast_to(near.astype(jnp.float32), (8, blocks))
    column = jnp.dot(near, expand, preferred_element_type=jnp.float32)[:1].astype(jnp.int32) * BW
    column = column + iota((1, width), 1) % BW
    for start in range(0, pick_ref.shape[0], LEAF):
        size = min(LEAF, pick_ref.shape[0] - start)
        hit = iota((size, width), 0) + start == column
        pick_ref[start : start + size, :] = jnp.where(hit, 1.0, 0.0).astype(jnp.bfloat16)
    for copy in copies[1:4]:
        copy.wait()
    leaves = transfer_ref.shape[0]
    transfer = transfer_ref[...].reshape(leaves * RANK, RANK)
    raised = jnp.dot(transfer, dev_ref[0], precision=HIGHEST, preferred_element_type=jnp.float32)
    high, low = split(jnp.concatenate([transfer, raised], axis=1))
    for leaf in range(leaves):
        at, points = slice(leaf * RANK, (leaf + 1) * RANK), slice(leaf * LEAF, (leaf + 1) * LEAF)
        basis_high, basis_low = split(basis_ref[:, points])
        weights_ref[:, points] = lax.dot_general(
            jnp.concatenate([high[at], high[at], low[at]], axis=0),
            jnp.concatenate([basis_high, basis_low, basis_high], axis=0),
            (((0,), (0,)), ((), ())),
            preferred_element_type=jnp.float32,
        )
    copies[4].wait()


def prepare_kernel(reorder, far_hbm, group_far_hbm, orbit_ref, pick_ref, mask_ref, *refs):
    far_ref, group_far_ref, sems = refs[-3:]
    moves = ((far_hbm, far_ref), (group_far_hbm, group_far_ref))
    copies = [pltpu.make_async_copy(a, b, sems.at[i]) for i, (a, b) in enumerate(moves)]
    for copy in copies:
        copy.start()
    if reorder:
        sorted_ref, order_ref = refs[:2]
        for start in range(0, orbit_ref.shape[0], LEAF):
            part = lax.dot_general(
                orbit_ref[start : start + LEAF, :],
                pick_ref[...],
                (((1,), (1,)), ((), ())),
                preferred_element_type=jnp.float32,
            )
            sorted_ref[start : start + LEAF, :] = part.astype(jnp.bfloat16)
        size = order_ref.shape[0]
        column = iota((size, 1), 0)
        place = by_core(column // BLOCK_ROWS, size // BLOCK_ROWS) * BLOCK_ROWS + column % BLOCK_ROWS
        hit = iota((size, size), 1) == place
        order_ref[...] = jnp.where(hit, 1.0, 0.0).astype(jnp.bfloat16)
    for copy in copies:
        copy.wait()
    dom_count, group_count = far_ref.shape[1], group_far_ref.shape[1]
    mask_ref[:dom_count, :] = spread_rows(far_ref[...].astype(jnp.float32), dom_count)
    mask_ref[dom_count:, :] = spread_rows(group_far_ref[...].astype(jnp.float32), group_count)


def half_matrix(pieces_ref, order_ref, rows_ref):
    chip = lax.shift_right_logical(lax.axis_index("dom"), 1)
    for c in range(pieces_ref.shape[0] // BLOCK_ROWS):
        first = jnp.bitwise_xor(chip, c) * BLOCK_ROWS
        at = pl.ds(pl.multiple_of(first, BLOCK_ROWS), BLOCK_ROWS)
        rows_ref[c * BLOCK_ROWS : (c + 1) * BLOCK_ROWS, :] = pieces_ref[at, :]
    matrix = jnp.dot(rows_ref[...], order_ref[...], preferred_element_type=jnp.float32)
    return matrix.astype(jnp.bfloat16)


def quadratic(orbit_ref, start, columns, matrix):
    points = slice(start, start + TILE)
    product = jnp.dot(orbit_ref[points, columns], matrix, preferred_element_type=jnp.float32)
    product = product * orbit_ref[points, :].astype(jnp.float32)
    folded = product[:, :LANES]
    for at in range(LANES, product.shape[1], LANES):
        folded = folded + product[:, at : at + LANES]
    return folded


def core_columns(core, width):
    return pl.ds(pl.multiple_of(core * (width // 2), LANES), width // 2)


def first_kernel(orbit_ref, held_ref, order_ref, out_ref, rows_ref):
    matrix = half_matrix(held_ref, order_ref, rows_ref)
    columns = core_columns(jnp.bitwise_and(lax.axis_index("dom"), 1), orbit_ref.shape[1])
    for start in range(0, orbit_ref.shape[0], TILE):
        out_ref[start : start + TILE, :] = quadratic(orbit_ref, start, columns, matrix)


def density_kernel(reorder, coords_ref, orbit_ref, other_ref, weights_ref, pick_ref, *refs):
    *inputs, halo_ref, expansion_ref, rows_ref = refs
    leaves = coords_ref.shape[1]
    me = lax.axis_index("dom")
    if reorder:
        matrix = half_matrix(other_ref, pick_ref, rows_ref)
        columns = core_columns(1 - jnp.bitwise_and(me, 1), orbit_ref.shape[1])
    else:
        held_ref, near_ref = inputs
        for k in range(near_ref.shape[1]):
            block = near_ref[0, k]
            apart = jnp.bitwise_xor(lax.shift_right_logical(block, 1), me)
            first = lax.shift_right_logical(apart, 1) * BLOCK_ROWS + jnp.bitwise_and(block, 1) * BW
            at = pl.ds(pl.multiple_of(first, BW), BW)
            mine = jnp.bitwise_and(apart, 1) == 0
            rows_ref[k * BW : (k + 1) * BW, :] = jnp.where(mine, held_ref[at, :], other_ref[at, :])
        matrix = jnp.dot(rows_ref[...], pick_ref[...], preferred_element_type=jnp.float32)
        matrix = matrix.astype(jnp.bfloat16)
        columns = slice(None)
    total = jnp.zeros((2 * RANK, LANES), jnp.float32)
    for start in range(0, leaves * LEAF, TILE):
        folded = quadratic(orbit_ref, start, columns, matrix)
        if reorder:
            folded = folded + inputs[0][start : start + TILE, :]
        for j in range(TILE // LANES):
            row = start // LANES + j
            part = lane_sums(folded[j * LANES : (j + 1) * LANES])
            halo_ref[row : row + 1, :] = part
            total = total + weights_ref[:, row * LANES : (row + 1) * LANES] * part
    coords = coords_ref[...].astype(jnp.float32)
    rows = leaves * LEAF_ROWS
    halo_ref[rows:, :] = jnp.zeros((halo_ref.shape[0] - rows, LANES), jnp.float32)
    halo_ref[rows : rows + 3, :leaves] = coords
    low = SIDE * jnp.min(coords, axis=1, keepdims=True)
    high = SIDE * jnp.max(coords, axis=1, keepdims=True) + (SIDE - 1)
    lane = iota((1, LANES), 1)
    bounds = jnp.zeros((1, LANES), jnp.float32)
    for k in range(3):
        bounds = jnp.where(lane == k, low[k : k + 1], bounds)
        bounds = jnp.where(lane == 3 + k, high[k : k + 1], bounds)
    both = jnp.concatenate([lane_sums(total), bounds], axis=0)
    expansion_ref[...] = jnp.broadcast_to(both[None], expansion_ref.shape)


def pattern(index):
    steps = (index // (CHEB * CHEB) % CHEB, index // CHEB % CHEB, index % CHEB)
    points = [math.cos((2 * a + 1) * math.pi / (2 * CHEB)) for a in range(CHEB)]
    out = []
    for step in steps:
        value = jnp.full(index.shape, points[CHEB - 1], jnp.float32)
        for a in range(CHEB - 1):
            value = jnp.where(step == a, points[a], value)
        out.append(value)
    return out


def nodes(bounds, unit):
    out = []
    for k in range(3):
        low, high = bounds[:, k : k + 1], bounds[:, 3 + k : 4 + k]
        out.append(0.5 * (low + high) + 0.5 * (high - low) * unit[k])
    return out


def node_coupling(target, source):
    square = soft_square
    for t, s in zip(target, source, strict=True):
        apart = t - s
        square = square + apart * apart
    return lax.rsqrt(square)


def places(halo, rows):
    parts = [spread_rows(halo[rows + k : rows + k + 1], 8) for k in range(3)]
    return SIDE * jnp.concatenate(parts, axis=0)


def pair_kernel(shift, y, square_x, square_z):
    lane = iota((8, LANES), 1)
    apart = shift[1] + (y - lane // SIDE % SIDE).astype(jnp.float32)
    square = apart * apart + square_z
    even = [lax.rsqrt(x + square) for x in square_x]
    low = lane < LANES // 2
    return even, [jnp.where(low, a, b) for a, b in zip(even[:-1], even[1:], strict=True)]


def pair_squares(shift):
    lane, row = iota((8, LANES), 1), iota((8, LANES), 0)
    half = jnp.where(lane < LANES // 2, 0.0, 1.0)
    along = shift[2] + (row - lane % SIDE).astype(jnp.float32)
    square_x = []
    for m in range(-6, SIDE + 2, 2):
        apart = shift[0] + (m - half)
        square_x.append(apart * apart)
    return square_x, along * along + soft_square


def leaf_density(density_ref, leaf):
    rows = [density_ref[pl.ds(leaf * LEAF_ROWS + j, 1), :] for j in range(LEAF_ROWS)]
    rows = [jnp.broadcast_to(row, (8, LANES)) for row in rows]
    return rows, [pltpu.roll(row, LANES // 2, 1) for row in rows]


def pair_sums(kernel, density, y):
    for x in range(SIDE):
        first = x // 2 + 3
        k, rho = kernel[x % 2], density[x % 2]
        value = k[first] * rho[0]
        for j in range(1, LEAF_ROWS):
            value = value + k[first - j] * rho[j]
        yield slice((x * SIDE + y) * SIDE, (x * SIDE + y + 1) * SIDE), value


def leaf_place(place_ref, leaf):
    return [place_ref[pl.ds(leaf + 8 * k, 1), :] for k in range(3)]


def self_kernel(halo_ref, sum_ref, place_ref):
    leaves = sum_ref.shape[0]
    place_ref[...] = places(halo_ref[...], leaves * LEAF_ROWS)
    shift = [jnp.zeros((8, LANES), jnp.float32)] * 3
    square_x, square_z = pair_squares(shift)
    for y in range(SIDE):
        kernel = pair_kernel(shift, y, square_x, square_z)
        for leaf in range(leaves):
            for at, value in pair_sums(kernel, leaf_density(halo_ref, leaf), y):
                sum_ref[leaf, at, :] = value


def near_kernel(
    leaves_ref, halo_ref, even_ref, odd_ref, own_ref, part_ref, out_ref, density_ref, place_ref, sum_ref
):
    leaves = leaves_ref.shape[0]
    rows = leaves * LEAF_ROWS
    is_odd = jnp.bitwise_and(lax.axis_index("dom"), 1) == 1
    even, odd = even_ref[...], odd_ref[...]
    window = (jnp.where(is_odd, even, odd), halo_ref[...], jnp.where(is_odd, odd, even))
    for side, held in enumerate(window):
        density_ref[side * rows : (side + 1) * rows, :] = held[:rows]
        place_ref[24 * side : 24 * (side + 1), :] = own_ref[...] if side == 1 else places(held, rows)
    for leaf in range(leaves):
        own_place = leaf_place(own_ref, leaf)
        named = [leaves_ref[leaf, slot] for slot in range(NEARL)]
        own = leaves + leaf
        others = (
            jnp.where(named[0] == own, named[1], named[0]),
            jnp.where(named[2] == own, named[1], named[2]),
        )
        for slot, position in enumerate(others):
            side = (position >= leaves).astype(jnp.int32)
            side = side + (position >= 2 * leaves).astype(jnp.int32)
            place = leaf_place(place_ref, 24 * side + position - leaves * side)
            shift = [jnp.broadcast_to(p - q, (8, LANES)) for p, q in zip(own_place, place, strict=True)]
            square_x, square_z = pair_squares(shift)
            density = leaf_density(density_ref, position)
            for y in range(SIDE):
                kernel = pair_kernel(shift, y, square_x, square_z)
                for at, value in pair_sums(kernel, density, y):
                    before = part_ref[leaf, at, :] if slot == 0 else sum_ref[leaf, at, :]
                    sum_ref[leaf, at, :] = before + value
        for j in range(LEAF_ROWS):
            part = lane_sums(sum_ref[leaf, j * LANES : (j + 1) * LANES, :])
            row = leaf * LEAF_ROWS + j
            out_ref[row : row + 1, :] = vol_weight * part


def far_field(expansion_ref, mask_ref, dev_ref):
    dom_count = lax.axis_size("dom")
    group_count = mask_ref.shape[0] - dom_count
    group, me = lax.axis_index("group"), lax.axis_index("dom")
    sent = expansion_ref[...]
    moments, bounds = sent[:, 0, :], sent[:, 1, :]
    lane = iota((1, LANES), 1)
    unit_row = pattern(lane % RANK)
    unit_column = pattern(iota((RANK, LANES), 0))
    group_bounds = []
    for h in range(group_count):
        part = bounds[h * dom_count : (h + 1) * dom_count]
        low = jnp.min(part, axis=0, keepdims=True)
        high = jnp.max(part, axis=0, keepdims=True)
        group_bounds.append(jnp.where(lane < 3, low, high))
    own_group_bounds = group_bounds[0]
    for h in range(1, group_count):
        own_group_bounds = jnp.where(group == h, group_bounds[h], own_group_bounds)
    target = nodes(own_group_bounds, unit_column)
    total = jnp.zeros((RANK, LANES), jnp.float32)
    for h in range(group_count):
        raised = jnp.sum(moments[h * dom_count : (h + 1) * dom_count], axis=0, keepdims=True)
        raised = jnp.where(lane >= RANK, raised, 0.0) * mask_ref[dom_count + h : dom_count + h + 1, :]
        total = total + node_coupling(target, nodes(group_bounds[h], unit_row)) * raised
    group_local = vol_weight * lane_sums(total)
    local = jnp.sum(dev_ref[0] * group_local, axis=1, keepdims=True)
    base = group * dom_count
    own = expansion_ref[pl.ds(base, dom_count)]
    own_bounds = expansion_ref[pl.ds(base + me, 1)][:, 1, :]
    target = nodes(own_bounds, unit_column)
    source = nodes(own[:, 1, :], unit_row)
    own_moments = jnp.where(lane < RANK, own[:, 0, :], 0.0) * mask_ref[:dom_count, :]
    total = jnp.zeros((RANK, LANES), jnp.float32)
    for s in range(dom_count):
        coupling = node_coupling(target, [x[s : s + 1] for x in source])
        total = total + coupling * own_moments[s : s + 1]
    local = local + vol_weight * jnp.sum(total, axis=1, keepdims=True)
    return jnp.broadcast_to(local, (RANK, LANES))


def potential_kernel(
    expansion_ref, mask_ref, weights_ref, dev_ref, near_ref, halo_ref, out_ref, density_ref
):
    density_ref[...] = halo_ref[: density_ref.shape[0], :]
    local = far_field(expansion_ref, mask_ref, dev_ref)
    for row in range(out_ref.shape[0]):
        at = slice(row * LANES, (row + 1) * LANES)
        far = jnp.sum(weights_ref[:RANK, at] * local, axis=0, keepdims=True)
        out_ref[row : row + 1, :] = near_ref[row : row + 1, :] + far


def in_hbm(x):
    return pltpu.with_memory_space_constraint(x, pltpu.HBM)


VMEM = pl.BlockSpec(memory_space=pltpu.VMEM)
SMEM = pl.BlockSpec(memory_space=pltpu.SMEM)
HBM = pl.BlockSpec(memory_space=pltpu.HBM)
ANY = pl.BlockSpec(memory_space=pl.ANY)


def local(
    orbitals,
    density_rows,
    near_blocks,
    leaf_coords,
    near_leaves,
    leaf_basis,
    leaf_transfer,
    dev_transfer,
    dev_far,
    group_far,
):
    points, width = orbitals.shape
    leaves = leaf_coords.shape[1]
    rows = leaves * LEAF_ROWS
    natural = density_rows.shape[1]
    devices = lax.axis_size("group") * lax.axis_size("dom")
    dom_count = lax.axis_size("dom")
    f32 = jnp.float32
    reorder = natural == width
    params = pltpu.CompilerParams(vmem_limit_bytes=(24 << 20) + 4 * natural * natural)

    def cost(flops, transcendentals=0):
        return pl.CostEstimate(
            flops=flops, bytes_accessed=4 << 20, transcendentals=transcendentals
        )

    def load():
        operands = (near_blocks, leaf_transfer, dev_transfer, leaf_basis)
        return pl.pallas_call(
            functools.partial(load_kernel, reorder),
            out_shape=(
                jax.ShapeDtypeStruct((points, width), jnp.bfloat16),
                jax.ShapeDtypeStruct((natural, width), jnp.bfloat16),
                jax.ShapeDtypeStruct((2 * RANK, points), f32),
            ),
            in_specs=[HBM] * 5,
            out_specs=(VMEM, VMEM, VMEM),
            scratch_shapes=[pltpu.VMEM(x.shape, x.dtype) for x in operands]
            + [pltpu.SemaphoreType.DMA((5,))],
            compiler_params=params,
            cost_estimate=cost(1 << 20),
            name="load",
        )(*[in_hbm(x) for x in operands], in_hbm(orbitals))

    def prepare(loaded):
        orbit, pick, _ = loaded
        operands = (dev_far, group_far)
        shapes = [jax.ShapeDtypeStruct((dev_far.shape[1] + group_far.shape[1], LANES), f32)]
        if reorder:
            shapes.append(jax.ShapeDtypeStruct((points, natural), jnp.bfloat16))
            shapes.append(jax.ShapeDtypeStruct((natural, natural), jnp.bfloat16))
        out = pl.pallas_call(
            functools.partial(prepare_kernel, reorder),
            out_shape=shapes,
            in_specs=[HBM] * 2 + [VMEM] * 2,
            out_specs=[VMEM] * len(shapes),
            scratch_shapes=[pltpu.VMEM(x.shape, x.dtype) for x in operands]
            + [pltpu.SemaphoreType.DMA((2,))],
            compiler_params=params,
            cost_estimate=cost(2 * points * width * natural),
            name="prepare",
        )(*[in_hbm(x) for x in operands], orbit, pick)
        return out if reorder else [*out, orbit, pick]

    held, other, (_, _, weights), (mask, orbit, pick) = gather_rows(density_rows, load, prepare)

    if reorder:
        rest = [
            pl.pallas_call(
                first_kernel,
                out_shape=jax.ShapeDtypeStruct((points, LANES), f32),
                in_specs=[VMEM] * 3,
                out_specs=VMEM,
                scratch_shapes=[pltpu.VMEM((natural // 2, natural), jnp.bfloat16)],
                compiler_params=params,
                cost_estimate=cost(points * width * width),
                name="first",
            )(orbit, held, pick)
        ]
        rows_shape = (natural // 2, natural)
    else:
        rest, rows_shape = [held, near_blocks], (width, natural)
    halo, expansion = pl.pallas_call(
        functools.partial(density_kernel, reorder),
        out_shape=(
            jax.ShapeDtypeStruct((rows + 8, LANES), f32),
            jax.ShapeDtypeStruct((devices, 2, LANES), f32),
        ),
        in_specs=[VMEM] * 6 + ([] if reorder else [SMEM]),
        out_specs=(VMEM, VMEM),
        scratch_shapes=[pltpu.VMEM(rows_shape, jnp.bfloat16)],
        compiler_params=params,
        cost_estimate=cost(points * width * width),
        name="density",
    )(leaf_coords, orbit, other, weights, pick, *rest)

    even = swap(halo, "dom", 1)
    pairs = [(i, i + 1 if i % 2 else i - 1) for i in range(1, dom_count - 1)]
    odd = lax.ppermute(halo, "dom", pairs)
    everyone = lax.all_to_all(expansion, ("group", "dom"), 0, 0)

    table = jax.ShapeDtypeStruct((rows, LANES), f32)
    sums = jax.ShapeDtypeStruct((leaves, LEAF, LANES), f32)
    places_shape = jax.ShapeDtypeStruct((24, LANES), f32)
    near_sums, own_places = pl.pallas_call(
        self_kernel,
        out_shape=(sums, places_shape),
        in_specs=[VMEM],
        out_specs=(VMEM, VMEM),
        compiler_params=params,
        cost_estimate=cost(20 << 20, 4 << 20),
        name="self",
    )(halo)
    near = pl.pallas_call(
        near_kernel,
        out_shape=table,
        in_specs=[SMEM] + [VMEM] * 5,
        out_specs=VMEM,
        scratch_shapes=[
            pltpu.VMEM((3 * rows, LANES), f32),
            pltpu.VMEM((72, LANES), f32),
            pltpu.VMEM((leaves, LEAF, LANES), f32),
        ],
        compiler_params=params,
        cost_estimate=cost(20 << 20, 4 << 20),
        name="near",
    )(near_leaves, halo, even, odd, own_places, near_sums)
    hartree, density = pl.pallas_call(
        potential_kernel,
        out_shape=(table, table),
        in_specs=[VMEM] * 6,
        out_specs=(VMEM, VMEM),
        compiler_params=params,
        cost_estimate=cost(4 << 20, 1 << 20),
        name="potential",
    )(everyone, mask, weights, dev_transfer, near, halo)
    return (density.reshape(-1), hartree.reshape(-1))


def solution(mesh):
    in_specs = (
        P(("group", "dom"), None),
        P(("group", "dom"), None),
        P(("group", "dom"), None),
        P(None, ("group", "dom")),
        P(("group", "dom"), None),
        P(None, ("group", "dom")),
        P(("group", "dom"), None, None),
        P(("group", "dom"), None, None),
        P(("group", "dom"), None),
        P("group", None),
    )
    out_specs = (P(("group", "dom")), P(("group", "dom")))
    return jax.shard_map(local, mesh=mesh, in_specs=in_specs, out_specs=out_specs, check_vma=False)
```

```python
import functools
import math

import jax
import jax.numpy as jnp
from jax import lax
from jax.experimental import pallas as pl
from jax.experimental.pallas import tpu as pltpu
from jax.sharding import PartitionSpec as P

SIDE = 8
LEAF = 512
CHEB = 4
RANK = CHEB * CHEB * CHEB
BW = 16
BLOCK_ROWS = 2 * BW
NEARL = 3
LANES = 128
LEAF_ROWS = LEAF // LANES
TILE = 512
HIGHEST = lax.Precision.HIGHEST

vol_weight = 0.1
soft_square = 1.0


def xor_stages(count):
    bits = count.bit_length() - 1
    stages, bit = ([(2,)], 2) if bits > 1 else ([], 1)
    while bit < bits:
        wide = 2 if bit + 1 < bits else 1
        stages.append(tuple(m << bit for m in range(1, 1 << wide)))
        bit += wide
    return stages


def swap(value, axis, mask):
    return lax.ppermute(value, axis, [(i, i ^ mask) for i in range(lax.axis_size(axis))])


def farthest_first(mask):
    return -(mask & -mask), -mask


def gather_rows(rows, load, prepare):
    held, loaded = rows, load()
    for stage, masks in enumerate(xor_stages(lax.axis_size("dom"))):
        if stage == 1:
            held, loaded = lax.optimization_barrier((held, loaded))
            result = prepare(loaded)
        arrived = {m: swap(held, "dom", m) for m in sorted(masks, key=farthest_first)}
        held = jnp.concatenate([held] + [arrived[m] for m in masks], axis=0)
    held, result = lax.optimization_barrier((held, result))
    return held, swap(held, "dom", 1), loaded, result


def iota(shape, dim):
    return lax.broadcasted_iota(jnp.int32, shape, dim)


def lane_sums(x):
    return jnp.sum(x.T, axis=0, keepdims=True)


def spread_rows(row, count):
    size = row.shape[1]
    diagonal = iota((count, size), 0) == iota((count, size), 1)
    diagonal = jnp.where(diagonal, row, 0.0).astype(jnp.bfloat16)
    return jnp.dot(
        diagonal, jnp.ones((size, LANES), jnp.bfloat16), preferred_element_type=jnp.float32
    )


def split(x):
    high = x.astype(jnp.bfloat16)
    return high, (x - high.astype(jnp.float32)).astype(jnp.bfloat16)


def by_core(device, devices):
    chip = lax.shift_right_logical(device, 1)
    return jnp.bitwise_and(device, 1) * (devices // 2) + chip


def load_kernel(
    reorder,
    near_hbm,
    transfer_hbm,
    dev_hbm,
    basis_hbm,
    orbitals_hbm,
    orbit_ref,
    pick_ref,
    weights_ref,
    near_ref,
    transfer_ref,
    dev_ref,
    basis_ref,
    sems,
):
    moves = ((near_hbm, near_ref), (transfer_hbm, transfer_ref), (dev_hbm, dev_ref))
    moves += ((basis_hbm, basis_ref), (orbitals_hbm, orbit_ref))
    copies = [pltpu.make_async_copy(a, b, sems.at[i]) for i, (a, b) in enumerate(moves)]
    for copy in copies:
        copy.start()
    copies[0].wait()
    blocks = near_ref.shape[1]
    width = blocks * BW
    expand = (iota((blocks, width), 1) // BW == iota((blocks, width), 0)).astype(jnp.float32)
    near = near_ref[...]
    if reorder:
        device = by_core(lax.shift_right_logical(near, 1), blocks // 2)
        near = 2 * device + jnp.bitwise_and(near, 1)
    near = jnp.broadcast_to(near.astype(jnp.float32), (8, blocks))
    column = jnp.dot(near, expand, preferred_element_type=jnp.float32)[:1].astype(jnp.int32) * BW
    column = column + iota((1, width), 1) % BW
    for start in range(0, pick_ref.shape[0], LEAF):
        size = min(LEAF, pick_ref.shape[0] - start)
        hit = iota((size, width), 0) + start == column
        pick_ref[start : start + size, :] = jnp.where(hit, 1.0, 0.0).astype(jnp.bfloat16)
    for copy in copies[1:4]:
        copy.wait()
    leaves = transfer_ref.shape[0]
    transfer = transfer_ref[...].reshape(leaves * RANK, RANK)
    raised = jnp.dot(transfer, dev_ref[0], precision=HIGHEST, preferred_element_type=jnp.float32)
    high, low = split(jnp.concatenate([transfer, raised], axis=1))
    for leaf in range(leaves):
        at, points = slice(leaf * RANK, (leaf + 1) * RANK), slice(leaf * LEAF, (leaf + 1) * LEAF)
        basis_high, basis_low = split(basis_ref[:, points])
        weights_ref[:, points] = lax.dot_general(
            jnp.concatenate([high[at], high[at], low[at]], axis=0),
            jnp.concatenate([basis_high, basis_low, basis_high], axis=0),
            (((0,), (0,)), ((), ())),
            preferred_element_type=jnp.float32,
        )
    copies[4].wait()


def prepare_kernel(reorder, far_hbm, group_far_hbm, orbit_ref, pick_ref, mask_ref, *refs):
    far_ref, group_far_ref, sems = refs[-3:]
    moves = ((far_hbm, far_ref), (group_far_hbm, group_far_ref))
    copies = [pltpu.make_async_copy(a, b, sems.at[i]) for i, (a, b) in enumerate(moves)]
    for copy in copies:
        copy.start()
    if reorder:
        sorted_ref, order_ref = refs[:2]
        for start in range(0, orbit_ref.shape[0], LEAF):
            part = lax.dot_general(
                orbit_ref[start : start + LEAF, :],
                pick_ref[...],
                (((1,), (1,)), ((), ())),
                preferred_element_type=jnp.float32,
            )
            sorted_ref[start : start + LEAF, :] = part.astype(jnp.bfloat16)
        size = order_ref.shape[0]
        column = iota((size, 1), 0)
        place = by_core(column // BLOCK_ROWS, size // BLOCK_ROWS) * BLOCK_ROWS + column % BLOCK_ROWS
        hit = iota((size, size), 1) == place
        order_ref[...] = jnp.where(hit, 1.0, 0.0).astype(jnp.bfloat16)
    for copy in copies:
        copy.wait()
    dom_count, group_count = far_ref.shape[1], group_far_ref.shape[1]
    mask_ref[:dom_count, :] = spread_rows(far_ref[...].astype(jnp.float32), dom_count)
    mask_ref[dom_count:, :] = spread_rows(group_far_ref[...].astype(jnp.float32), group_count)


def half_matrix(pieces_ref, order_ref, rows_ref):
    chip = lax.shift_right_logical(lax.axis_index("dom"), 1)
    for c in range(pieces_ref.shape[0] // BLOCK_ROWS):
        first = jnp.bitwise_xor(chip, c) * BLOCK_ROWS
        at = pl.ds(pl.multiple_of(first, BLOCK_ROWS), BLOCK_ROWS)
        rows_ref[c * BLOCK_ROWS : (c + 1) * BLOCK_ROWS, :] = pieces_ref[at, :]
    matrix = jnp.dot(rows_ref[...], order_ref[...], preferred_element_type=jnp.float32)
    return matrix.astype(jnp.bfloat16)


def quadratic(orbit_ref, start, columns, matrix):
    points = slice(start, start + TILE)
    product = jnp.dot(orbit_ref[points, columns], matrix, preferred_element_type=jnp.float32)
    product = product * orbit_ref[points, :].astype(jnp.float32)
    folded = product[:, :LANES]
    for at in range(LANES, product.shape[1], LANES):
        folded = folded + product[:, at : at + LANES]
    return folded


def core_columns(core, width):
    return pl.ds(pl.multiple_of(core * (width // 2), LANES), width // 2)


def first_kernel(orbit_ref, held_ref, order_ref, out_ref, rows_ref):
    matrix = half_matrix(held_ref, order_ref, rows_ref)
    columns = core_columns(jnp.bitwise_and(lax.axis_index("dom"), 1), orbit_ref.shape[1])
    for start in range(0, orbit_ref.shape[0], TILE):
        out_ref[start : start + TILE, :] = quadratic(orbit_ref, start, columns, matrix)


def density_kernel(reorder, coords_ref, orbit_ref, other_ref, weights_ref, pick_ref, *refs):
    *inputs, halo_ref, expansion_ref, rows_ref = refs
    leaves = coords_ref.shape[1]
    me = lax.axis_index("dom")
    if reorder:
        matrix = half_matrix(other_ref, pick_ref, rows_ref)
        columns = core_columns(1 - jnp.bitwise_and(me, 1), orbit_ref.shape[1])
    else:
        held_ref, near_ref = inputs
        for k in range(near_ref.shape[1]):
            block = near_ref[0, k]
            apart = jnp.bitwise_xor(lax.shift_right_logical(block, 1), me)
            first = lax.shift_right_logical(apart, 1) * BLOCK_ROWS + jnp.bitwise_and(block, 1) * BW
            at = pl.ds(pl.multiple_of(first, BW), BW)
            mine = jnp.bitwise_and(apart, 1) == 0
            rows_ref[k * BW : (k + 1) * BW, :] = jnp.where(mine, held_ref[at, :], other_ref[at, :])
        matrix = jnp.dot(rows_ref[...], pick_ref[...], preferred_element_type=jnp.float32)
        matrix = matrix.astype(jnp.bfloat16)
        columns = slice(None)
    total = jnp.zeros((2 * RANK, LANES), jnp.float32)
    for start in range(0, leaves * LEAF, TILE):
        folded = quadratic(orbit_ref, start, columns, matrix)
        if reorder:
            folded = folded + inputs[0][start : start + TILE, :]
        for j in range(TILE // LANES):
            row = start // LANES + j
            part = lane_sums(folded[j * LANES : (j + 1) * LANES])
            halo_ref[row : row + 1, :] = part
            total = total + weights_ref[:, row * LANES : (row + 1) * LANES] * part
    coords = coords_ref[...].astype(jnp.float32)
    rows = leaves * LEAF_ROWS
    halo_ref[rows:, :] = jnp.zeros((halo_ref.shape[0] - rows, LANES), jnp.float32)
    halo_ref[rows : rows + 3, :leaves] = coords
    low = SIDE * jnp.min(coords, axis=1, keepdims=True)
    high = SIDE * jnp.max(coords, axis=1, keepdims=True) + (SIDE - 1)
    lane = iota((1, LANES), 1)
    bounds = jnp.zeros((1, LANES), jnp.float32)
    for k in range(3):
        bounds = jnp.where(lane == k, low[k : k + 1], bounds)
        bounds = jnp.where(lane == 3 + k, high[k : k + 1], bounds)
    both = jnp.concatenate([lane_sums(total), bounds], axis=0)
    expansion_ref[...] = jnp.broadcast_to(both[None], expansion_ref.shape)


def pattern(index):
    steps = (index // (CHEB * CHEB) % CHEB, index // CHEB % CHEB, index % CHEB)
    points = [math.cos((2 * a + 1) * math.pi / (2 * CHEB)) for a in range(CHEB)]
    out = []
    for step in steps:
        value = jnp.full(index.shape, points[CHEB - 1], jnp.float32)
        for a in range(CHEB - 1):
            value = jnp.where(step == a, points[a], value)
        out.append(value)
    return out


def nodes(bounds, unit):
    out = []
    for k in range(3):
        low, high = bounds[:, k : k + 1], bounds[:, 3 + k : 4 + k]
        out.append(0.5 * (low + high) + 0.5 * (high - low) * unit[k])
    return out


def node_coupling(target, source):
    square = soft_square
    for t, s in zip(target, source, strict=True):
        apart = t - s
        square = square + apart * apart
    return lax.rsqrt(square)


def places(halo, rows):
    parts = [spread_rows(halo[rows + k : rows + k + 1], 8) for k in range(3)]
    return SIDE * jnp.concatenate(parts, axis=0)


def pair_kernel(shift, y, square_x, square_z):
    lane = iota((8, LANES), 1)
    apart = shift[1] + (y - lane // SIDE % SIDE).astype(jnp.float32)
    square = apart * apart + square_z
    even = [lax.rsqrt(x + square) for x in square_x]
    low = lane < LANES // 2
    return even, [jnp.where(low, a, b) for a, b in zip(even[:-1], even[1:], strict=True)]


def pair_squares(shift):
    lane, row = iota((8, LANES), 1), iota((8, LANES), 0)
    half = jnp.where(lane < LANES // 2, 0.0, 1.0)
    along = shift[2] + (row - lane % SIDE).astype(jnp.float32)
    square_x = []
    for m in range(-6, SIDE + 2, 2):
        apart = shift[0] + (m - half)
        square_x.append(apart * apart)
    return square_x, along * along + soft_square


def leaf_density(density_ref, leaf):
    rows = [density_ref[pl.ds(leaf * LEAF_ROWS + j, 1), :] for j in range(LEAF_ROWS)]
    rows = [jnp.broadcast_to(row, (8, LANES)) for row in rows]
    return rows, [pltpu.roll(row, LANES // 2, 1) for row in rows]


def pair_sums(kernel, density, y):
    for x in range(SIDE):
        first = x // 2 + 3
        k, rho = kernel[x % 2], density[x % 2]
        value = k[first] * rho[0]
        for j in range(1, LEAF_ROWS):
            value = value + k[first - j] * rho[j]
        yield slice((x * SIDE + y) * SIDE, (x * SIDE + y + 1) * SIDE), value


def leaf_place(place_ref, leaf):
    return [place_ref[pl.ds(leaf + 8 * k, 1), :] for k in range(3)]


def self_kernel(halo_ref, sum_ref, place_ref):
    leaves = sum_ref.shape[0]
    place_ref[...] = places(halo_ref[...], leaves * LEAF_ROWS)
    shift = [jnp.zeros((8, LANES), jnp.float32)] * 3
    square_x, square_z = pair_squares(shift)
    for y in range(SIDE):
        kernel = pair_kernel(shift, y, square_x, square_z)
        for leaf in range(leaves):
            for at, value in pair_sums(kernel, leaf_density(halo_ref, leaf), y):
                sum_ref[leaf, at, :] = value


def near_kernel(
    leaves_ref, halo_ref, even_ref, odd_ref, own_ref, part_ref, out_ref, density_ref, place_ref, sum_ref
):
    leaves = leaves_ref.shape[0]
    rows = leaves * LEAF_ROWS
    is_odd = jnp.bitwise_and(lax.axis_index("dom"), 1) == 1
    even, odd = even_ref[...], odd_ref[...]
    window = (jnp.where(is_odd, even, odd), halo_ref[...], jnp.where(is_odd, odd, even))
    for side, held in enumerate(window):
        density_ref[side * rows : (side + 1) * rows, :] = held[:rows]
        place_ref[24 * side : 24 * (side + 1), :] = own_ref[...] if side == 1 else places(held, rows)
    for leaf in range(leaves):
        own_place = leaf_place(own_ref, leaf)
        named = [leaves_ref[leaf, slot] for slot in range(NEARL)]
        own = leaves + leaf
        others = (
            jnp.where(named[0] == own, named[1], named[0]),
            jnp.where(named[2] == own, named[1], named[2]),
        )
        for slot, position in enumerate(others):
            side = (position >= leaves).astype(jnp.int32)
            side = side + (position >= 2 * leaves).astype(jnp.int32)
            place = leaf_place(place_ref, 24 * side + position - leaves * side)
            shift = [jnp.broadcast_to(p - q, (8, LANES)) for p, q in zip(own_place, place, strict=True)]
            square_x, square_z = pair_squares(shift)
            density = leaf_density(density_ref, position)
            for y in range(SIDE):
                kernel = pair_kernel(shift, y, square_x, square_z)
                for at, value in pair_sums(kernel, density, y):
                    before = part_ref[leaf, at, :] if slot == 0 else sum_ref[leaf, at, :]
                    sum_ref[leaf, at, :] = before + value
        for j in range(LEAF_ROWS):
            part = lane_sums(sum_ref[leaf, j * LANES : (j + 1) * LANES, :])
            row = leaf * LEAF_ROWS + j
            out_ref[row : row + 1, :] = vol_weight * part


def far_field(expansion_ref, mask_ref, dev_ref):
    dom_count = lax.axis_size("dom")
    group_count = mask_ref.shape[0] - dom_count
    group, me = lax.axis_index("group"), lax.axis_index("dom")
    moments, bounds = expansion_ref[:, 0, :], expansion_ref[:, 1, :]
    lane = iota((1, LANES), 1)
    unit_row = pattern(lane % RANK)
    unit_column = pattern(iota((RANK, LANES), 0))
    group_bounds = []
    for h in range(group_count):
        part = bounds[h * dom_count : (h + 1) * dom_count]
        low = jnp.min(part, axis=0, keepdims=True)
        high = jnp.max(part, axis=0, keepdims=True)
        group_bounds.append(jnp.where(lane < 3, low, high))
    own_group_bounds = group_bounds[0]
    for h in range(1, group_count):
        own_group_bounds = jnp.where(group == h, group_bounds[h], own_group_bounds)
    target = nodes(own_group_bounds, unit_column)
    total = jnp.zeros((RANK, LANES), jnp.float32)
    for h in range(group_count):
        raised = jnp.sum(moments[h * dom_count : (h + 1) * dom_count], axis=0, keepdims=True)
        raised = jnp.where(lane >= RANK, raised, 0.0) * mask_ref[dom_count + h : dom_count + h + 1, :]
        total = total + node_coupling(target, nodes(group_bounds[h], unit_row)) * raised
    group_local = vol_weight * lane_sums(total)
    local = jnp.sum(dev_ref[0] * group_local, axis=1, keepdims=True)
    base = group * dom_count
    at = pl.ds(base, dom_count)
    own_bounds = expansion_ref[pl.ds(base + me, 1), 1, :]
    target = nodes(own_bounds, unit_column)
    low, half = lane < RANK, dom_count // 2
    source = [jnp.where(low, x[:half], x[half:]) for x in nodes(expansion_ref[at, 1, :], unit_row)]
    own_moments = expansion_ref[at, 0, :] * mask_ref[:dom_count, :]
    own_moments = jnp.where(low, own_moments[:half], pltpu.roll(own_moments[half:], RANK, 1))
    total = jnp.zeros((RANK, LANES), jnp.float32)
    for s in range(half):
        coupling = node_coupling(target, [x[s : s + 1] for x in source])
        total = total + coupling * own_moments[s : s + 1]
    local = local + vol_weight * jnp.sum(total, axis=1, keepdims=True)
    return jnp.broadcast_to(local, (RANK, LANES))


def potential_kernel(
    expansion_ref, mask_ref, weights_ref, dev_ref, near_ref, halo_ref, out_ref, density_ref
):
    density_ref[...] = halo_ref[: density_ref.shape[0], :]
    local = far_field(expansion_ref, mask_ref, dev_ref)
    for row in range(out_ref.shape[0]):
        at = slice(row * LANES, (row + 1) * LANES)
        far = jnp.sum(weights_ref[:RANK, at] * local, axis=0, keepdims=True)
        out_ref[row : row + 1, :] = near_ref[row : row + 1, :] + far


def in_hbm(x):
    return pltpu.with_memory_space_constraint(x, pltpu.HBM)


VMEM = pl.BlockSpec(memory_space=pltpu.VMEM)
SMEM = pl.BlockSpec(memory_space=pltpu.SMEM)
HBM = pl.BlockSpec(memory_space=pltpu.HBM)
ANY = pl.BlockSpec(memory_space=pl.ANY)


def local(
    orbitals,
    density_rows,
    near_blocks,
    leaf_coords,
    near_leaves,
    leaf_basis,
    leaf_transfer,
    dev_transfer,
    dev_far,
    group_far,
):
    points, width = orbitals.shape
    leaves = leaf_coords.shape[1]
    rows = leaves * LEAF_ROWS
    natural = density_rows.shape[1]
    devices = lax.axis_size("group") * lax.axis_size("dom")
    dom_count = lax.axis_size("dom")
    f32 = jnp.float32
    reorder = natural == width
    params = pltpu.CompilerParams(vmem_limit_bytes=(24 << 20) + 4 * natural * natural)

    def cost(flops, transcendentals=0):
        return pl.CostEstimate(
            flops=flops, bytes_accessed=4 << 20, transcendentals=transcendentals
        )

    def load():
        operands = (near_blocks, leaf_transfer, dev_transfer, leaf_basis)
        return pl.pallas_call(
            functools.partial(load_kernel, reorder),
            out_shape=(
                jax.ShapeDtypeStruct((points, width), jnp.bfloat16),
                jax.ShapeDtypeStruct((natural, width), jnp.bfloat16),
                jax.ShapeDtypeStruct((2 * RANK, points), f32),
            ),
            in_specs=[HBM] * 5,
            out_specs=(VMEM, VMEM, VMEM),
            scratch_shapes=[pltpu.VMEM(x.shape, x.dtype) for x in operands]
            + [pltpu.SemaphoreType.DMA((5,))],
            compiler_params=params,
            cost_estimate=cost(1 << 20),
            name="load",
        )(*[in_hbm(x) for x in operands], in_hbm(orbitals))

    def prepare(loaded):
        orbit, pick, _ = loaded
        operands = (dev_far, group_far)
        shapes = [jax.ShapeDtypeStruct((dev_far.shape[1] + group_far.shape[1], LANES), f32)]
        if reorder:
            shapes.append(jax.ShapeDtypeStruct((points, natural), jnp.bfloat16))
            shapes.append(jax.ShapeDtypeStruct((natural, natural), jnp.bfloat16))
        out = pl.pallas_call(
            functools.partial(prepare_kernel, reorder),
            out_shape=shapes,
            in_specs=[HBM] * 2 + [VMEM] * 2,
            out_specs=[VMEM] * len(shapes),
            scratch_shapes=[pltpu.VMEM(x.shape, x.dtype) for x in operands]
            + [pltpu.SemaphoreType.DMA((2,))],
            compiler_params=params,
            cost_estimate=cost(2 * points * width * natural),
            name="prepare",
        )(*[in_hbm(x) for x in operands], orbit, pick)
        return out if reorder else [*out, orbit, pick]

    held, other, (_, _, weights), (mask, orbit, pick) = gather_rows(density_rows, load, prepare)

    if reorder:
        rest = [
            pl.pallas_call(
                first_kernel,
                out_shape=jax.ShapeDtypeStruct((points, LANES), f32),
                in_specs=[VMEM] * 3,
                out_specs=VMEM,
                scratch_shapes=[pltpu.VMEM((natural // 2, natural), jnp.bfloat16)],
                compiler_params=params,
                cost_estimate=cost(points * width * width),
                name="first",
            )(orbit, held, pick)
        ]
        rows_shape = (natural // 2, natural)
    else:
        rest, rows_shape = [held, near_blocks], (width, natural)
    halo, expansion = pl.pallas_call(
        functools.partial(density_kernel, reorder),
        out_shape=(
            jax.ShapeDtypeStruct((rows + 8, LANES), f32),
            jax.ShapeDtypeStruct((devices, 2, LANES), f32),
        ),
        in_specs=[VMEM] * 6 + ([] if reorder else [SMEM]),
        out_specs=(VMEM, VMEM),
        scratch_shapes=[pltpu.VMEM(rows_shape, jnp.bfloat16)],
        compiler_params=params,
        cost_estimate=cost(points * width * width),
        name="density",
    )(leaf_coords, orbit, other, weights, pick, *rest)

    even = swap(halo, "dom", 1)
    pairs = [(i, i + 1 if i % 2 else i - 1) for i in range(1, dom_count - 1)]
    odd = lax.ppermute(halo, "dom", pairs)
    everyone = lax.all_to_all(expansion, ("group", "dom"), 0, 0)

    table = jax.ShapeDtypeStruct((rows, LANES), f32)
    sums = jax.ShapeDtypeStruct((leaves, LEAF, LANES), f32)
    places_shape = jax.ShapeDtypeStruct((24, LANES), f32)
    near_sums, own_places = pl.pallas_call(
        self_kernel,
        out_shape=(sums, places_shape),
        in_specs=[VMEM],
        out_specs=(VMEM, VMEM),
        compiler_params=params,
        cost_estimate=cost(20 << 20, 4 << 20),
        name="self",
    )(halo)
    near = pl.pallas_call(
        near_kernel,
        out_shape=table,
        in_specs=[VMEM] * 6,
        out_specs=VMEM,
        scratch_shapes=[
            pltpu.VMEM((3 * rows, LANES), f32),
            pltpu.VMEM((72, LANES), f32),
            pltpu.VMEM((leaves, LEAF, LANES), f32),
        ],
        compiler_params=params,
        cost_estimate=cost(20 << 20, 4 << 20),
        name="near",
    )(near_leaves, halo, even, odd, own_places, near_sums)
    hartree, density = pl.pallas_call(
        potential_kernel,
        out_shape=(table, table),
        in_specs=[VMEM] * 6,
        out_specs=(VMEM, VMEM),
        compiler_params=params,
        cost_estimate=cost(4 << 20, 1 << 20),
        name="potential",
    )(everyone, mask, weights, dev_transfer, near, halo)
    return (density.reshape(-1), hartree.reshape(-1))


def solution(mesh):
    in_specs = (
        P(("group", "dom"), None),
        P(("group", "dom"), None),
        P(("group", "dom"), None),
        P(None, ("group", "dom")),
        P(("group", "dom"), None),
        P(None, ("group", "dom")),
        P(("group", "dom"), None, None),
        P(("group", "dom"), None, None),
        P(("group", "dom"), None),
        P("group", None),
    )
    out_specs = (P(("group", "dom")), P(("group", "dom")))
    return jax.shard_map(local, mesh=mesh, in_specs=in_specs, out_specs=out_specs, check_vma=False)
```

```python
import functools
import math

import jax
import jax.numpy as jnp
from jax import lax
from jax.experimental import pallas as pl
from jax.experimental.pallas import tpu as pltpu
from jax.sharding import PartitionSpec as P

SIDE = 8
LEAF = 512
CHEB = 4
RANK = CHEB * CHEB * CHEB
BW = 16
BLOCK_ROWS = 2 * BW
NEARL = 3
LANES = 128
LEAF_ROWS = LEAF // LANES
TILE = 512
HIGHEST = lax.Precision.HIGHEST

vol_weight = 0.1
soft_square = 1.0


def swap(value, axis, mask):
    return lax.ppermute(value, axis, [(i, i ^ mask) for i in range(lax.axis_size(axis))])


def piece_of(apart):
    pair = jnp.bitwise_and(lax.shift_right_logical(apart, 1), 3)
    place = jnp.where(pair == 0, 0, jnp.where(pair == 3, 1, pair + 1))
    return apart + 2 * (place - pair)


def gather_rows(rows, load, prepare):
    count = lax.axis_size("dom")
    beside, middle = swap(rows, "dom", 2), swap(rows, "dom", 8)
    own, *loaded = load()
    beside, loaded = lax.optimization_barrier((beside, loaded))
    pair = jnp.concatenate([own, beside], axis=0)
    far, close = swap(pair, "dom", 12), swap(pair, "dom", 4)
    middle, loaded = lax.optimization_barrier((middle, loaded))
    other_middle = swap(middle, "dom", 2)
    result = prepare(loaded)
    held = jnp.concatenate([pair, far, close, middle, other_middle], axis=0)
    bit = 16
    while bit < count:
        held = jnp.concatenate([held, swap(held, "dom", bit)], axis=0)
        bit *= 2
    held, result = lax.optimization_barrier((held, result))
    return held, swap(held, "dom", 1), loaded, result


def iota(shape, dim):
    return lax.broadcasted_iota(jnp.int32, shape, dim)


def lane_sums(x):
    return jnp.sum(x.T, axis=0, keepdims=True)


def spread_rows(row, count):
    size = row.shape[1]
    diagonal = iota((count, size), 0) == iota((count, size), 1)
    diagonal = jnp.where(diagonal, row, 0.0).astype(jnp.bfloat16)
    return jnp.dot(
        diagonal, jnp.ones((size, LANES), jnp.bfloat16), preferred_element_type=jnp.float32
    )


def split(x):
    high = x.astype(jnp.bfloat16)
    return high, (x - high.astype(jnp.float32)).astype(jnp.bfloat16)


def by_core(device, devices):
    chip = lax.shift_right_logical(device, 1)
    return jnp.bitwise_and(device, 1) * (devices // 2) + chip


def load_kernel(
    reorder,
    near_hbm,
    transfer_hbm,
    dev_hbm,
    basis_hbm,
    orbitals_hbm,
    rows_hbm,
    own_ref,
    orbit_ref,
    pick_ref,
    weights_ref,
    near_ref,
    transfer_ref,
    dev_ref,
    basis_ref,
    sems,
):
    moves = ((near_hbm, near_ref), (transfer_hbm, transfer_ref), (dev_hbm, dev_ref))
    moves += ((basis_hbm, basis_ref), (orbitals_hbm, orbit_ref), (rows_hbm, own_ref))
    copies = [pltpu.make_async_copy(a, b, sems.at[i]) for i, (a, b) in enumerate(moves)]
    for copy in copies:
        copy.start()
    copies[0].wait()
    blocks = near_ref.shape[1]
    width = blocks * BW
    expand = (iota((blocks, width), 1) // BW == iota((blocks, width), 0)).astype(jnp.float32)
    near = near_ref[...]
    if reorder:
        device = by_core(lax.shift_right_logical(near, 1), blocks // 2)
        near = 2 * device + jnp.bitwise_and(near, 1)
    near = jnp.broadcast_to(near.astype(jnp.float32), (8, blocks))
    column = jnp.dot(near, expand, preferred_element_type=jnp.float32)[:1].astype(jnp.int32) * BW
    column = column + iota((1, width), 1) % BW
    for start in range(0, pick_ref.shape[0], LEAF):
        size = min(LEAF, pick_ref.shape[0] - start)
        hit = iota((size, width), 0) + start == column
        pick_ref[start : start + size, :] = jnp.where(hit, 1.0, 0.0).astype(jnp.bfloat16)
    for copy in copies[1:4]:
        copy.wait()
    leaves = transfer_ref.shape[0]
    transfer = transfer_ref[...].reshape(leaves * RANK, RANK)
    raised = jnp.dot(transfer, dev_ref[0], precision=HIGHEST, preferred_element_type=jnp.float32)
    high, low = split(jnp.concatenate([transfer, raised], axis=1))
    for leaf in range(leaves):
        at, points = slice(leaf * RANK, (leaf + 1) * RANK), slice(leaf * LEAF, (leaf + 1) * LEAF)
        basis_high, basis_low = split(basis_ref[:, points])
        weights_ref[:, points] = lax.dot_general(
            jnp.concatenate([high[at], high[at], low[at]], axis=0),
            jnp.concatenate([basis_high, basis_low, basis_high], axis=0),
            (((0,), (0,)), ((), ())),
            preferred_element_type=jnp.float32,
        )
    for copy in copies[4:]:
        copy.wait()


def prepare_kernel(reorder, far_hbm, group_far_hbm, orbit_ref, pick_ref, mask_ref, *refs):
    far_ref, group_far_ref, sems = refs[-3:]
    moves = ((far_hbm, far_ref), (group_far_hbm, group_far_ref))
    copies = [pltpu.make_async_copy(a, b, sems.at[i]) for i, (a, b) in enumerate(moves)]
    for copy in copies:
        copy.start()
    if reorder:
        sorted_ref, order_ref = refs[:2]
        for start in range(0, orbit_ref.shape[0], LEAF):
            part = lax.dot_general(
                orbit_ref[start : start + LEAF, :],
                pick_ref[...],
                (((1,), (1,)), ((), ())),
                preferred_element_type=jnp.float32,
            )
            sorted_ref[start : start + LEAF, :] = part.astype(jnp.bfloat16)
        size = order_ref.shape[0]
        column = iota((size, 1), 0)
        place = by_core(column // BLOCK_ROWS, size // BLOCK_ROWS) * BLOCK_ROWS + column % BLOCK_ROWS
        hit = iota((size, size), 1) == place
        order_ref[...] = jnp.where(hit, 1.0, 0.0).astype(jnp.bfloat16)
    for copy in copies:
        copy.wait()
    dom_count, group_count = far_ref.shape[1], group_far_ref.shape[1]
    mask_ref[:dom_count, :] = spread_rows(far_ref[...].astype(jnp.float32), dom_count)
    mask_ref[dom_count:, :] = spread_rows(group_far_ref[...].astype(jnp.float32), group_count)


def half_matrix(pieces_ref, order_ref, rows_ref):
    chip = lax.shift_right_logical(lax.axis_index("dom"), 1)
    for c in range(pieces_ref.shape[0] // BLOCK_ROWS):
        first = piece_of(jnp.bitwise_xor(chip, c)) * BLOCK_ROWS
        at = pl.ds(pl.multiple_of(first, BLOCK_ROWS), BLOCK_ROWS)
        rows_ref[c * BLOCK_ROWS : (c + 1) * BLOCK_ROWS, :] = pieces_ref[at, :]
    matrix = jnp.dot(rows_ref[...], order_ref[...], preferred_element_type=jnp.float32)
    return matrix.astype(jnp.bfloat16)


def quadratic(orbit_ref, start, columns, matrix):
    points = slice(start, start + TILE)
    product = jnp.dot(orbit_ref[points, columns], matrix, preferred_element_type=jnp.float32)
    product = product * orbit_ref[points, :].astype(jnp.float32)
    folded = product[:, :LANES]
    for at in range(LANES, product.shape[1], LANES):
        folded = folded + product[:, at : at + LANES]
    return folded


def core_columns(core, width):
    return pl.ds(pl.multiple_of(core * (width // 2), LANES), width // 2)


def first_kernel(orbit_ref, held_ref, order_ref, out_ref, rows_ref):
    matrix = half_matrix(held_ref, order_ref, rows_ref)
    columns = core_columns(jnp.bitwise_and(lax.axis_index("dom"), 1), orbit_ref.shape[1])
    for start in range(0, orbit_ref.shape[0], TILE):
        out_ref[start : start + TILE, :] = quadratic(orbit_ref, start, columns, matrix)


def density_kernel(reorder, coords_ref, orbit_ref, other_ref, weights_ref, pick_ref, *refs):
    *inputs, halo_ref, expansion_ref, rows_ref = refs
    leaves = coords_ref.shape[1]
    me = lax.axis_index("dom")
    if reorder:
        matrix = half_matrix(other_ref, pick_ref, rows_ref)
        columns = core_columns(1 - jnp.bitwise_and(me, 1), orbit_ref.shape[1])
    else:
        held_ref, near_ref = inputs
        for k in range(near_ref.shape[1]):
            block = near_ref[0, k]
            apart = jnp.bitwise_xor(lax.shift_right_logical(block, 1), me)
            piece = piece_of(lax.shift_right_logical(apart, 1))
            first = piece * BLOCK_ROWS + jnp.bitwise_and(block, 1) * BW
            at = pl.ds(pl.multiple_of(first, BW), BW)
            mine = jnp.bitwise_and(apart, 1) == 0
            rows_ref[k * BW : (k + 1) * BW, :] = jnp.where(mine, held_ref[at, :], other_ref[at, :])
        matrix = jnp.dot(rows_ref[...], pick_ref[...], preferred_element_type=jnp.float32)
        matrix = matrix.astype(jnp.bfloat16)
        columns = slice(None)
    total = jnp.zeros((2 * RANK, LANES), jnp.float32)
    for start in range(0, leaves * LEAF, TILE):
        folded = quadratic(orbit_ref, start, columns, matrix)
        if reorder:
            folded = folded + inputs[0][start : start + TILE, :]
        for j in range(TILE // LANES):
            row = start // LANES + j
            part = lane_sums(folded[j * LANES : (j + 1) * LANES])
            halo_ref[row : row + 1, :] = part
            total = total + weights_ref[:, row * LANES : (row + 1) * LANES] * part
    coords = coords_ref[...].astype(jnp.float32)
    rows = leaves * LEAF_ROWS
    halo_ref[rows:, :] = jnp.zeros((halo_ref.shape[0] - rows, LANES), jnp.float32)
    halo_ref[rows : rows + 3, :leaves] = coords
    low = SIDE * jnp.min(coords, axis=1, keepdims=True)
    high = SIDE * jnp.max(coords, axis=1, keepdims=True) + (SIDE - 1)
    lane = iota((1, LANES), 1)
    bounds = jnp.zeros((1, LANES), jnp.float32)
    for k in range(3):
        bounds = jnp.where(lane == k, low[k : k + 1], bounds)
        bounds = jnp.where(lane == 3 + k, high[k : k + 1], bounds)
    both = jnp.concatenate([lane_sums(total), bounds], axis=0)
    expansion_ref[...] = jnp.broadcast_to(both[None], expansion_ref.shape)


def pattern(index):
    steps = (index // (CHEB * CHEB) % CHEB, index // CHEB % CHEB, index % CHEB)
    points = [math.cos((2 * a + 1) * math.pi / (2 * CHEB)) for a in range(CHEB)]
    out = []
    for step in steps:
        value = jnp.full(index.shape, points[CHEB - 1], jnp.float32)
        for a in range(CHEB - 1):
            value = jnp.where(step == a, points[a], value)
        out.append(value)
    return out


def nodes(bounds, unit):
    out = []
    for k in range(3):
        low, high = bounds[:, k : k + 1], bounds[:, 3 + k : 4 + k]
        out.append(0.5 * (low + high) + 0.5 * (high - low) * unit[k])
    return out


def node_coupling(target, source):
    square = soft_square
    for t, s in zip(target, source, strict=True):
        apart = t - s
        square = square + apart * apart
    return lax.rsqrt(square)


def places(halo, rows):
    parts = [spread_rows(halo[rows + k : rows + k + 1], 8) for k in range(3)]
    return SIDE * jnp.concatenate(parts, axis=0)


def pair_kernel(shift, y, square_x, square_z):
    lane = iota((8, LANES), 1)
    apart = shift[1] + (y - lane // SIDE % SIDE).astype(jnp.float32)
    square = apart * apart + square_z
    even = [lax.rsqrt(x + square) for x in square_x]
    low = lane < LANES // 2
    return even, [jnp.where(low, a, b) for a, b in zip(even[:-1], even[1:], strict=True)]


def pair_squares(shift):
    lane, row = iota((8, LANES), 1), iota((8, LANES), 0)
    half = jnp.where(lane < LANES // 2, 0.0, 1.0)
    along = shift[2] + (row - lane % SIDE).astype(jnp.float32)
    square_x = []
    for m in range(-6, SIDE + 2, 2):
        apart = shift[0] + (m - half)
        square_x.append(apart * apart)
    return square_x, along * along + soft_square


def leaf_density(density_ref, leaf):
    rows = [density_ref[pl.ds(leaf * LEAF_ROWS + j, 1), :] for j in range(LEAF_ROWS)]
    rows = [jnp.broadcast_to(row, (8, LANES)) for row in rows]
    return rows, [pltpu.roll(row, LANES // 2, 1) for row in rows]


def pair_sums(kernel, density, y):
    for x in range(SIDE):
        first = x // 2 + 3
        k, rho = kernel[x % 2], density[x % 2]
        value = k[first] * rho[0]
        for j in range(1, LEAF_ROWS):
            value = value + k[first - j] * rho[j]
        yield slice((x * SIDE + y) * SIDE, (x * SIDE + y + 1) * SIDE), value


def leaf_place(place_ref, leaf):
    return [place_ref[pl.ds(leaf + 8 * k, 1), :] for k in range(3)]


def self_kernel(halo_ref, sum_ref, place_ref):
    leaves = sum_ref.shape[0]
    place_ref[...] = places(halo_ref[...], leaves * LEAF_ROWS)
    shift = [jnp.zeros((8, LANES), jnp.float32)] * 3
    square_x, square_z = pair_squares(shift)
    for y in range(SIDE):
        kernel = pair_kernel(shift, y, square_x, square_z)
        for leaf in range(leaves):
            for at, value in pair_sums(kernel, leaf_density(halo_ref, leaf), y):
                sum_ref[leaf, at, :] = value


def near_kernel(
    leaves_ref, halo_ref, even_ref, odd_ref, own_ref, part_ref, out_ref, density_ref, place_ref, sum_ref
):
    leaves = leaves_ref.shape[0]
    rows = leaves * LEAF_ROWS
    is_odd = jnp.bitwise_and(lax.axis_index("dom"), 1) == 1
    even, odd = even_ref[...], odd_ref[...]
    window = (jnp.where(is_odd, even, odd), halo_ref[...], jnp.where(is_odd, odd, even))
    for side, held in enumerate(window):
        density_ref[side * rows : (side + 1) * rows, :] = held[:rows]
        place_ref[24 * side : 24 * (side + 1), :] = own_ref[...] if side == 1 else places(held, rows)
    for leaf in range(leaves):
        own_place = leaf_place(own_ref, leaf)
        named = [leaves_ref[leaf, slot] for slot in range(NEARL)]
        own = leaves + leaf
        others = (
            jnp.where(named[0] == own, named[1], named[0]),
            jnp.where(named[2] == own, named[1], named[2]),
        )
        for slot, position in enumerate(others):
            side = (position >= leaves).astype(jnp.int32)
            side = side + (position >= 2 * leaves).astype(jnp.int32)
            place = leaf_place(place_ref, 24 * side + position - leaves * side)
            shift = [jnp.broadcast_to(p - q, (8, LANES)) for p, q in zip(own_place, place, strict=True)]
            square_x, square_z = pair_squares(shift)
            density = leaf_density(density_ref, position)
            for y in range(SIDE):
                kernel = pair_kernel(shift, y, square_x, square_z)
                for at, value in pair_sums(kernel, density, y):
                    before = part_ref[leaf, at, :] if slot == 0 else sum_ref[leaf, at, :]
                    sum_ref[leaf, at, :] = before + value
        for j in range(LEAF_ROWS):
            part = lane_sums(sum_ref[leaf, j * LANES : (j + 1) * LANES, :])
            row = leaf * LEAF_ROWS + j
            out_ref[row : row + 1, :] = vol_weight * part


def far_field(expansion_ref, mask_ref, dev_ref):
    dom_count = lax.axis_size("dom")
    group_count = mask_ref.shape[0] - dom_count
    group, me = lax.axis_index("group"), lax.axis_index("dom")
    moments, bounds = expansion_ref[:, 0, :], expansion_ref[:, 1, :]
    lane = iota((1, LANES), 1)
    unit_row = pattern(lane % RANK)
    unit_column = pattern(iota((RANK, LANES), 0))
    group_bounds = []
    for h in range(group_count):
        part = bounds[h * dom_count : (h + 1) * dom_count]
        low = jnp.min(part, axis=0, keepdims=True)
        high = jnp.max(part, axis=0, keepdims=True)
        group_bounds.append(jnp.where(lane < 3, low, high))
    own_group_bounds = group_bounds[0]
    for h in range(1, group_count):
        own_group_bounds = jnp.where(group == h, group_bounds[h], own_group_bounds)
    target = nodes(own_group_bounds, unit_column)
    total = jnp.zeros((RANK, LANES), jnp.float32)
    for h in range(group_count):
        raised = jnp.sum(moments[h * dom_count : (h + 1) * dom_count], axis=0, keepdims=True)
        raised = jnp.where(lane >= RANK, raised, 0.0) * mask_ref[dom_count + h : dom_count + h + 1, :]
        total = total + node_coupling(target, nodes(group_bounds[h], unit_row)) * raised
    group_local = vol_weight * lane_sums(total)
    local = jnp.sum(dev_ref[0] * group_local, axis=1, keepdims=True)
    base = group * dom_count
    at = pl.ds(base, dom_count)
    own_bounds = expansion_ref[pl.ds(base + me, 1), 1, :]
    target = nodes(own_bounds, unit_column)
    low, half = lane < RANK, dom_count // 2
    source = [jnp.where(low, x[:half], x[half:]) for x in nodes(expansion_ref[at, 1, :], unit_row)]
    own_moments = expansion_ref[at, 0, :] * mask_ref[:dom_count, :]
    own_moments = jnp.where(low, own_moments[:half], pltpu.roll(own_moments[half:], RANK, 1))
    total = jnp.zeros((RANK, LANES), jnp.float32)
    for s in range(half):
        coupling = node_coupling(target, [x[s : s + 1] for x in source])
        total = total + coupling * own_moments[s : s + 1]
    local = local + vol_weight * jnp.sum(total, axis=1, keepdims=True)
    return jnp.broadcast_to(local, (RANK, LANES))


def potential_kernel(
    expansion_ref, mask_ref, weights_ref, dev_ref, near_ref, halo_ref, out_ref, density_ref
):
    density_ref[...] = halo_ref[: density_ref.shape[0], :]
    local = far_field(expansion_ref, mask_ref, dev_ref)
    for row in range(out_ref.shape[0]):
        at = slice(row * LANES, (row + 1) * LANES)
        far = jnp.sum(weights_ref[:RANK, at] * local, axis=0, keepdims=True)
        out_ref[row : row + 1, :] = near_ref[row : row + 1, :] + far


def in_hbm(x):
    return pltpu.with_memory_space_constraint(x, pltpu.HBM)


VMEM = pl.BlockSpec(memory_space=pltpu.VMEM)
SMEM = pl.BlockSpec(memory_space=pltpu.SMEM)
HBM = pl.BlockSpec(memory_space=pltpu.HBM)
ANY = pl.BlockSpec(memory_space=pl.ANY)


def local(
    orbitals,
    density_rows,
    near_blocks,
    leaf_coords,
    near_leaves,
    leaf_basis,
    leaf_transfer,
    dev_transfer,
    dev_far,
    group_far,
):
    points, width = orbitals.shape
    leaves = leaf_coords.shape[1]
    rows = leaves * LEAF_ROWS
    natural = density_rows.shape[1]
    devices = lax.axis_size("group") * lax.axis_size("dom")
    dom_count = lax.axis_size("dom")
    f32 = jnp.float32
    reorder = natural == width
    params = pltpu.CompilerParams(vmem_limit_bytes=(24 << 20) + 4 * natural * natural)

    def cost(flops, transcendentals=0):
        return pl.CostEstimate(
            flops=flops, bytes_accessed=4 << 20, transcendentals=transcendentals
        )

    def load():
        operands = (near_blocks, leaf_transfer, dev_transfer, leaf_basis)
        return pl.pallas_call(
            functools.partial(load_kernel, reorder),
            out_shape=(
                jax.ShapeDtypeStruct(density_rows.shape, jnp.bfloat16),
                jax.ShapeDtypeStruct((points, width), jnp.bfloat16),
                jax.ShapeDtypeStruct((natural, width), jnp.bfloat16),
                jax.ShapeDtypeStruct((2 * RANK, points), f32),
            ),
            in_specs=[HBM] * 6,
            out_specs=(VMEM,) * 4,
            scratch_shapes=[pltpu.VMEM(x.shape, x.dtype) for x in operands]
            + [pltpu.SemaphoreType.DMA((6,))],
            compiler_params=params,
            cost_estimate=cost(1 << 20),
            name="load",
        )(*[in_hbm(x) for x in operands], in_hbm(orbitals), in_hbm(density_rows))

    def prepare(loaded):
        orbit, pick, _ = loaded
        operands = (dev_far, group_far)
        shapes = [jax.ShapeDtypeStruct((dev_far.shape[1] + group_far.shape[1], LANES), f32)]
        if reorder:
            shapes.append(jax.ShapeDtypeStruct((points, natural), jnp.bfloat16))
            shapes.append(jax.ShapeDtypeStruct((natural, natural), jnp.bfloat16))
        out = pl.pallas_call(
            functools.partial(prepare_kernel, reorder),
            out_shape=shapes,
            in_specs=[HBM] * 2 + [VMEM] * 2,
            out_specs=[VMEM] * len(shapes),
            scratch_shapes=[pltpu.VMEM(x.shape, x.dtype) for x in operands]
            + [pltpu.SemaphoreType.DMA((2,))],
            compiler_params=params,
            cost_estimate=cost(2 * points * width * natural),
            name="prepare",
        )(*[in_hbm(x) for x in operands], orbit, pick)
        return out if reorder else [*out, orbit, pick]

    held, other, (_, _, weights), (mask, orbit, pick) = gather_rows(density_rows, load, prepare)

    if reorder:
        rest = [
            pl.pallas_call(
                first_kernel,
                out_shape=jax.ShapeDtypeStruct((points, LANES), f32),
                in_specs=[VMEM] * 3,
                out_specs=VMEM,
                scratch_shapes=[pltpu.VMEM((natural // 2, natural), jnp.bfloat16)],
                compiler_params=params,
                cost_estimate=cost(points * width * width),
                name="first",
            )(orbit, held, pick)
        ]
        rows_shape = (natural // 2, natural)
    else:
        rest, rows_shape = [held, near_blocks], (width, natural)
    halo, expansion = pl.pallas_call(
        functools.partial(density_kernel, reorder),
        out_shape=(
            jax.ShapeDtypeStruct((rows + 8, LANES), f32),
            jax.ShapeDtypeStruct((devices, 2, LANES), f32),
        ),
        in_specs=[VMEM] * 6 + ([] if reorder else [SMEM]),
        out_specs=(VMEM, VMEM),
        scratch_shapes=[pltpu.VMEM(rows_shape, jnp.bfloat16)],
        compiler_params=params,
        cost_estimate=cost(points * width * width),
        name="density",
    )(leaf_coords, orbit, other, weights, pick, *rest)

    even = swap(halo, "dom", 1)
    pairs = [(i, i + 1 if i % 2 else i - 1) for i in range(1, dom_count - 1)]
    odd = lax.ppermute(halo, "dom", pairs)
    everyone = lax.all_to_all(expansion, ("group", "dom"), 0, 0)

    table = jax.ShapeDtypeStruct((rows, LANES), f32)
    sums = jax.ShapeDtypeStruct((leaves, LEAF, LANES), f32)
    places_shape = jax.ShapeDtypeStruct((24, LANES), f32)
    near_sums, own_places = pl.pallas_call(
        self_kernel,
        out_shape=(sums, places_shape),
        in_specs=[VMEM],
        out_specs=(VMEM, VMEM),
        compiler_params=params,
        cost_estimate=cost(20 << 20, 4 << 20),
        name="self",
    )(halo)
    near = pl.pallas_call(
        near_kernel,
        out_shape=table,
        in_specs=[VMEM] * 6,
        out_specs=VMEM,
        scratch_shapes=[
            pltpu.VMEM((3 * rows, LANES), f32),
            pltpu.VMEM((72, LANES), f32),
            pltpu.VMEM((leaves, LEAF, LANES), f32),
        ],
        compiler_params=params,
        cost_estimate=cost(20 << 20, 4 << 20),
        name="near",
    )(near_leaves, halo, even, odd, own_places, near_sums)
    hartree, density = pl.pallas_call(
        potential_kernel,
        out_shape=(table, table),
        in_specs=[VMEM] * 6,
        out_specs=(VMEM, VMEM),
        compiler_params=params,
        cost_estimate=cost(4 << 20, 1 << 20),
        name="potential",
    )(everyone, mask, weights, dev_transfer, near, halo)
    return (density.reshape(-1), hartree.reshape(-1))


def solution(mesh):
    in_specs = (
        P(("group", "dom"), None),
        P(("group", "dom"), None),
        P(("group", "dom"), None),
        P(None, ("group", "dom")),
        P(("group", "dom"), None),
        P(None, ("group", "dom")),
        P(("group", "dom"), None, None),
        P(("group", "dom"), None, None),
        P(("group", "dom"), None),
        P("group", None),
    )
    out_specs = (P(("group", "dom")), P(("group", "dom")))
    return jax.shard_map(local, mesh=mesh, in_specs=in_specs, out_specs=out_specs, check_vma=False)
```

```python
import functools
import math

import jax
import jax.numpy as jnp
from jax import lax
from jax.experimental import pallas as pl
from jax.experimental.pallas import tpu as pltpu
from jax.sharding import PartitionSpec as P

SIDE = 8
LEAF = 512
CHEB = 4
RANK = CHEB * CHEB * CHEB
BW = 16
BLOCK_ROWS = 2 * BW
NEARL = 3
LANES = 128
LEAF_ROWS = LEAF // LANES
TILE = 512

vol_weight = 0.1
soft_square = 1.0


def swap(value, axis, mask):
    return lax.ppermute(value, axis, [(i, i ^ mask) for i in range(lax.axis_size(axis))])


def piece_of(apart):
    pair = jnp.bitwise_and(lax.shift_right_logical(apart, 1), 3)
    place = jnp.where(pair == 0, 0, jnp.where(pair == 3, 1, pair + 1))
    return apart + 2 * (place - pair)


def gather_rows(rows, load, prepare):
    count = lax.axis_size("dom")
    beside, middle = swap(rows, "dom", 2), swap(rows, "dom", 8)
    own, *loaded = load()
    beside, loaded = lax.optimization_barrier((beside, loaded))
    pair = jnp.concatenate([own, beside], axis=0)
    far, close = swap(pair, "dom", 12), swap(pair, "dom", 4)
    middle, loaded = lax.optimization_barrier((middle, loaded))
    other_middle = swap(middle, "dom", 2)
    result = prepare(loaded)
    held = jnp.concatenate([pair, far, close, middle, other_middle], axis=0)
    bit = 16
    while bit < count:
        held = jnp.concatenate([held, swap(held, "dom", bit)], axis=0)
        bit *= 2
    held, result = lax.optimization_barrier((held, result))
    return held, swap(held, "dom", 1), loaded, result


def iota(shape, dim):
    return lax.broadcasted_iota(jnp.int32, shape, dim)


def lane_sums(x):
    return jnp.sum(x.T, axis=0, keepdims=True)


def spread_rows(row, count):
    size = row.shape[1]
    diagonal = iota((count, size), 0) == iota((count, size), 1)
    diagonal = jnp.where(diagonal, row, 0.0).astype(jnp.bfloat16)
    return jnp.dot(
        diagonal, jnp.ones((size, LANES), jnp.bfloat16), preferred_element_type=jnp.float32
    )


def split(x):
    high = x.astype(jnp.bfloat16)
    return high, (x - high.astype(jnp.float32)).astype(jnp.bfloat16)


def by_core(device, devices):
    chip = lax.shift_right_logical(device, 1)
    return jnp.bitwise_and(device, 1) * (devices // 2) + chip


def load_kernel(
    reorder,
    near_hbm,
    transfer_hbm,
    dev_hbm,
    basis_hbm,
    orbitals_hbm,
    rows_hbm,
    own_ref,
    orbit_ref,
    pick_ref,
    weights_ref,
    near_ref,
    transfer_ref,
    dev_ref,
    basis_ref,
    sems,
):
    moves = ((near_hbm, near_ref), (transfer_hbm, transfer_ref), (dev_hbm, dev_ref))
    moves += ((basis_hbm, basis_ref), (orbitals_hbm, orbit_ref), (rows_hbm, own_ref))
    copies = [pltpu.make_async_copy(a, b, sems.at[i]) for i, (a, b) in enumerate(moves)]
    for copy in copies:
        copy.start()
    copies[0].wait()
    blocks = near_ref.shape[1]
    width = blocks * BW
    expand = (iota((blocks, width), 1) // BW == iota((blocks, width), 0)).astype(jnp.float32)
    near = near_ref[...]
    if reorder:
        device = by_core(lax.shift_right_logical(near, 1), blocks // 2)
        near = 2 * device + jnp.bitwise_and(near, 1)
    near = jnp.broadcast_to(near.astype(jnp.float32), (8, blocks))
    column = jnp.dot(near, expand, preferred_element_type=jnp.float32)[:1].astype(jnp.int32) * BW
    column = column + iota((1, width), 1) % BW
    for start in range(0, pick_ref.shape[0], LEAF):
        size = min(LEAF, pick_ref.shape[0] - start)
        hit = iota((size, width), 0) + start == column
        pick_ref[start : start + size, :] = jnp.where(hit, 1.0, 0.0).astype(jnp.bfloat16)
    for copy in copies[1:4]:
        copy.wait()
    leaves = transfer_ref.shape[0]
    transfer = transfer_ref[...].reshape(leaves * RANK, RANK)
    high, low = split(transfer)
    dev_high, dev_low = split(dev_ref[0])
    raised = jnp.dot(
        jnp.concatenate([high, high, low], axis=1),
        jnp.concatenate([dev_high, dev_low, dev_high], axis=0),
        preferred_element_type=jnp.float32,
    )
    high, low = split(jnp.concatenate([transfer, raised], axis=1))
    for leaf in range(leaves):
        at, points = slice(leaf * RANK, (leaf + 1) * RANK), slice(leaf * LEAF, (leaf + 1) * LEAF)
        basis_high, basis_low = split(basis_ref[:, points])
        weights_ref[:, points] = lax.dot_general(
            jnp.concatenate([high[at], high[at], low[at]], axis=0),
            jnp.concatenate([basis_high, basis_low, basis_high], axis=0),
            (((0,), (0,)), ((), ())),
            preferred_element_type=jnp.float32,
        )
    for copy in copies[4:]:
        copy.wait()


def prepare_kernel(orbit_ref, pick_ref, sorted_ref, order_ref):
    for start in range(0, orbit_ref.shape[0], LEAF):
        part = lax.dot_general(
            orbit_ref[start : start + LEAF, :],
            pick_ref[...],
            (((1,), (1,)), ((), ())),
            preferred_element_type=jnp.float32,
        )
        sorted_ref[start : start + LEAF, :] = part.astype(jnp.bfloat16)
    size = order_ref.shape[0]
    column = iota((size, 1), 0)
    place = by_core(column // BLOCK_ROWS, size // BLOCK_ROWS) * BLOCK_ROWS + column % BLOCK_ROWS
    hit = iota((size, size), 1) == place
    order_ref[...] = jnp.where(hit, 1.0, 0.0).astype(jnp.bfloat16)


def half_matrix(pieces_ref, order_ref, rows_ref):
    chip = lax.shift_right_logical(lax.axis_index("dom"), 1)
    for c in range(pieces_ref.shape[0] // BLOCK_ROWS):
        first = piece_of(jnp.bitwise_xor(chip, c)) * BLOCK_ROWS
        at = pl.ds(pl.multiple_of(first, BLOCK_ROWS), BLOCK_ROWS)
        rows_ref[c * BLOCK_ROWS : (c + 1) * BLOCK_ROWS, :] = pieces_ref[at, :]
    matrix = jnp.dot(rows_ref[...], order_ref[...], preferred_element_type=jnp.float32)
    return matrix.astype(jnp.bfloat16)


def quadratic(orbit_ref, start, columns, matrix):
    points = slice(start, start + TILE)
    product = jnp.dot(orbit_ref[points, columns], matrix, preferred_element_type=jnp.float32)
    product = product * orbit_ref[points, :].astype(jnp.float32)
    folded = product[:, :LANES]
    for at in range(LANES, product.shape[1], LANES):
        folded = folded + product[:, at : at + LANES]
    return folded


def core_columns(core, width):
    return pl.ds(pl.multiple_of(core * (width // 2), LANES), width // 2)


def first_kernel(orbit_ref, held_ref, order_ref, out_ref, rows_ref):
    matrix = half_matrix(held_ref, order_ref, rows_ref)
    columns = core_columns(jnp.bitwise_and(lax.axis_index("dom"), 1), orbit_ref.shape[1])
    for start in range(0, orbit_ref.shape[0], TILE):
        out_ref[start : start + TILE, :] = quadratic(orbit_ref, start, columns, matrix)


def density_kernel(reorder, coords_ref, orbit_ref, other_ref, weights_ref, pick_ref, *refs):
    *inputs, halo_ref, expansion_ref, rows_ref = refs
    leaves = coords_ref.shape[1]
    me = lax.axis_index("dom")
    if reorder:
        matrix = half_matrix(other_ref, pick_ref, rows_ref)
        columns = core_columns(1 - jnp.bitwise_and(me, 1), orbit_ref.shape[1])
    else:
        held_ref, near_ref = inputs
        for k in range(near_ref.shape[1]):
            block = near_ref[0, k]
            apart = jnp.bitwise_xor(lax.shift_right_logical(block, 1), me)
            piece = piece_of(lax.shift_right_logical(apart, 1))
            first = piece * BLOCK_ROWS + jnp.bitwise_and(block, 1) * BW
            at = pl.ds(pl.multiple_of(first, BW), BW)
            mine = jnp.bitwise_and(apart, 1) == 0
            rows_ref[k * BW : (k + 1) * BW, :] = jnp.where(mine, held_ref[at, :], other_ref[at, :])
        matrix = jnp.dot(rows_ref[...], pick_ref[...], preferred_element_type=jnp.float32)
        matrix = matrix.astype(jnp.bfloat16)
        columns = slice(None)
    total = jnp.zeros((2 * RANK, LANES), jnp.float32)
    for start in range(0, leaves * LEAF, TILE):
        folded = quadratic(orbit_ref, start, columns, matrix)
        if reorder:
            folded = folded + inputs[0][start : start + TILE, :]
        for j in range(TILE // LANES):
            row = start // LANES + j
            part = lane_sums(folded[j * LANES : (j + 1) * LANES])
            halo_ref[row : row + 1, :] = part
            total = total + weights_ref[:, row * LANES : (row + 1) * LANES] * part
    coords = coords_ref[...].astype(jnp.float32)
    rows = leaves * LEAF_ROWS
    halo_ref[rows:, :] = jnp.zeros((halo_ref.shape[0] - rows, LANES), jnp.float32)
    halo_ref[rows : rows + 3, :leaves] = coords
    low = SIDE * jnp.min(coords, axis=1, keepdims=True)
    high = SIDE * jnp.max(coords, axis=1, keepdims=True) + (SIDE - 1)
    lane = iota((1, LANES), 1)
    bounds = jnp.zeros((1, LANES), jnp.float32)
    for k in range(3):
        bounds = jnp.where(lane == k, low[k : k + 1], bounds)
        bounds = jnp.where(lane == 3 + k, high[k : k + 1], bounds)
    both = jnp.concatenate([lane_sums(total), bounds], axis=0)
    expansion_ref[...] = jnp.broadcast_to(both[None], expansion_ref.shape)


def pattern(index):
    steps = (index // (CHEB * CHEB) % CHEB, index // CHEB % CHEB, index % CHEB)
    points = [math.cos((2 * a + 1) * math.pi / (2 * CHEB)) for a in range(CHEB)]
    out = []
    for step in steps:
        value = jnp.full(index.shape, points[CHEB - 1], jnp.float32)
        for a in range(CHEB - 1):
            value = jnp.where(step == a, points[a], value)
        out.append(value)
    return out


def nodes(bounds, unit):
    out = []
    for k in range(3):
        low, high = bounds[:, k : k + 1], bounds[:, 3 + k : 4 + k]
        out.append(0.5 * (low + high) + 0.5 * (high - low) * unit[k])
    return out


def node_coupling(target, source):
    square = soft_square
    for t, s in zip(target, source, strict=True):
        apart = t - s
        square = square + apart * apart
    return lax.rsqrt(square)


def places(halo, rows):
    parts = [spread_rows(halo[rows + k : rows + k + 1], 8) for k in range(3)]
    return SIDE * jnp.concatenate(parts, axis=0)


def pair_kernel(shift, y, square_x, square_z):
    lane = iota((8, LANES), 1)
    apart = shift[1] + (y - lane // SIDE % SIDE).astype(jnp.float32)
    square = apart * apart + square_z
    even = [lax.rsqrt(x + square) for x in square_x]
    low = lane < LANES // 2
    return even, [jnp.where(low, a, b) for a, b in zip(even[:-1], even[1:], strict=True)]


def pair_squares(shift):
    lane, row = iota((8, LANES), 1), iota((8, LANES), 0)
    half = jnp.where(lane < LANES // 2, 0.0, 1.0)
    along = shift[2] + (row - lane % SIDE).astype(jnp.float32)
    square_x = []
    for m in range(-6, SIDE + 2, 2):
        apart = shift[0] + (m - half)
        square_x.append(apart * apart)
    return square_x, along * along + soft_square


def leaf_density(density_ref, leaf):
    rows = [density_ref[pl.ds(leaf * LEAF_ROWS + j, 1), :] for j in range(LEAF_ROWS)]
    rows = [jnp.broadcast_to(row, (8, LANES)) for row in rows]
    return rows, [pltpu.roll(row, LANES // 2, 1) for row in rows]


def pair_sums(kernel, density, y):
    for x in range(SIDE):
        first = x // 2 + 3
        k, rho = kernel[x % 2], density[x % 2]
        value = k[first] * rho[0]
        for j in range(1, LEAF_ROWS):
            value = value + k[first - j] * rho[j]
        yield slice((x * SIDE + y) * SIDE, (x * SIDE + y + 1) * SIDE), value


def leaf_place(place_ref, leaf):
    return [place_ref[pl.ds(leaf + 8 * k, 1), :] for k in range(3)]


def self_kernel(
    far_hbm, group_far_hbm, halo_ref, sum_ref, place_ref, mask_ref, far_ref, group_far_ref, sems
):
    moves = ((far_hbm, far_ref), (group_far_hbm, group_far_ref))
    copies = [pltpu.make_async_copy(a, b, sems.at[i]) for i, (a, b) in enumerate(moves)]
    for copy in copies:
        copy.start()
    leaves = sum_ref.shape[0]
    place_ref[...] = places(halo_ref[...], leaves * LEAF_ROWS)
    shift = [jnp.zeros((8, LANES), jnp.float32)] * 3
    square_x, square_z = pair_squares(shift)
    for y in range(SIDE):
        kernel = pair_kernel(shift, y, square_x, square_z)
        for leaf in range(leaves):
            for at, value in pair_sums(kernel, leaf_density(halo_ref, leaf), y):
                sum_ref[leaf, at, :] = value
    for copy in copies:
        copy.wait()
    dom_count, group_count = far_ref.shape[1], group_far_ref.shape[1]
    mask_ref[:dom_count, :] = spread_rows(far_ref[...].astype(jnp.float32), dom_count)
    mask_ref[dom_count:, :] = spread_rows(group_far_ref[...].astype(jnp.float32), group_count)


def near_kernel(
    leaves_ref, halo_ref, even_ref, odd_ref, own_ref, part_ref, out_ref, density_ref, place_ref, sum_ref
):
    leaves = leaves_ref.shape[0]
    rows = leaves * LEAF_ROWS
    is_odd = jnp.bitwise_and(lax.axis_index("dom"), 1) == 1
    even, odd = even_ref[...], odd_ref[...]
    window = (jnp.where(is_odd, even, odd), halo_ref[...], jnp.where(is_odd, odd, even))
    for side, held in enumerate(window):
        density_ref[side * rows : (side + 1) * rows, :] = held[:rows]
        place_ref[24 * side : 24 * (side + 1), :] = own_ref[...] if side == 1 else places(held, rows)
    for leaf in range(leaves):
        own_place = leaf_place(own_ref, leaf)
        named = [leaves_ref[leaf, slot] for slot in range(NEARL)]
        own = leaves + leaf
        others = (
            jnp.where(named[0] == own, named[1], named[0]),
            jnp.where(named[2] == own, named[1], named[2]),
        )
        for slot, position in enumerate(others):
            side = (position >= leaves).astype(jnp.int32)
            side = side + (position >= 2 * leaves).astype(jnp.int32)
            place = leaf_place(place_ref, 24 * side + position - leaves * side)
            shift = [jnp.broadcast_to(p - q, (8, LANES)) for p, q in zip(own_place, place, strict=True)]
            square_x, square_z = pair_squares(shift)
            density = leaf_density(density_ref, position)
            for y in range(SIDE):
                kernel = pair_kernel(shift, y, square_x, square_z)
                for at, value in pair_sums(kernel, density, y):
                    before = part_ref[leaf, at, :] if slot == 0 else sum_ref[leaf, at, :]
                    sum_ref[leaf, at, :] = before + value
        for j in range(LEAF_ROWS):
            part = lane_sums(sum_ref[leaf, j * LANES : (j + 1) * LANES, :])
            row = leaf * LEAF_ROWS + j
            out_ref[row : row + 1, :] = vol_weight * part


def far_field(expansion_ref, mask_ref, dev_ref):
    dom_count = lax.axis_size("dom")
    group_count = mask_ref.shape[0] - dom_count
    group, me = lax.axis_index("group"), lax.axis_index("dom")
    moments, bounds = expansion_ref[:, 0, :], expansion_ref[:, 1, :]
    lane = iota((1, LANES), 1)
    unit_row = pattern(lane % RANK)
    unit_column = pattern(iota((RANK, LANES), 0))
    group_bounds = []
    for h in range(group_count):
        part = bounds[h * dom_count : (h + 1) * dom_count]
        low = jnp.min(part, axis=0, keepdims=True)
        high = jnp.max(part, axis=0, keepdims=True)
        group_bounds.append(jnp.where(lane < 3, low, high))
    own_group_bounds = group_bounds[0]
    for h in range(1, group_count):
        own_group_bounds = jnp.where(group == h, group_bounds[h], own_group_bounds)
    target = nodes(own_group_bounds, unit_column)
    total = jnp.zeros((RANK, LANES), jnp.float32)
    for h in range(group_count):
        raised = jnp.sum(moments[h * dom_count : (h + 1) * dom_count], axis=0, keepdims=True)
        raised = jnp.where(lane >= RANK, raised, 0.0) * mask_ref[dom_count + h : dom_count + h + 1, :]
        total = total + node_coupling(target, nodes(group_bounds[h], unit_row)) * raised
    group_local = vol_weight * lane_sums(total)
    local = jnp.sum(dev_ref[0] * group_local, axis=1, keepdims=True)
    base = group * dom_count
    at = pl.ds(base, dom_count)
    own_bounds = expansion_ref[pl.ds(base + me, 1), 1, :]
    target = nodes(own_bounds, unit_column)
    low, half = lane < RANK, dom_count // 2
    source = [jnp.where(low, x[:half], x[half:]) for x in nodes(expansion_ref[at, 1, :], unit_row)]
    own_moments = expansion_ref[at, 0, :] * mask_ref[:dom_count, :]
    own_moments = jnp.where(low, own_moments[:half], pltpu.roll(own_moments[half:], RANK, 1))
    total = jnp.zeros((RANK, LANES), jnp.float32)
    for s in range(half):
        coupling = node_coupling(target, [x[s : s + 1] for x in source])
        total = total + coupling * own_moments[s : s + 1]
    local = local + vol_weight * jnp.sum(total, axis=1, keepdims=True)
    return jnp.broadcast_to(local, (RANK, LANES))


def potential_kernel(
    expansion_ref, mask_ref, weights_ref, dev_ref, near_ref, halo_ref, out_ref, density_ref
):
    density_ref[...] = halo_ref[: density_ref.shape[0], :]
    local = far_field(expansion_ref, mask_ref, dev_ref)
    for row in range(out_ref.shape[0]):
        at = slice(row * LANES, (row + 1) * LANES)
        far = jnp.sum(weights_ref[:RANK, at] * local, axis=0, keepdims=True)
        out_ref[row : row + 1, :] = near_ref[row : row + 1, :] + far


def in_hbm(x):
    return pltpu.with_memory_space_constraint(x, pltpu.HBM)


VMEM = pl.BlockSpec(memory_space=pltpu.VMEM)
SMEM = pl.BlockSpec(memory_space=pltpu.SMEM)
HBM = pl.BlockSpec(memory_space=pltpu.HBM)
ANY = pl.BlockSpec(memory_space=pl.ANY)


def local(
    orbitals,
    density_rows,
    near_blocks,
    leaf_coords,
    near_leaves,
    leaf_basis,
    leaf_transfer,
    dev_transfer,
    dev_far,
    group_far,
):
    points, width = orbitals.shape
    leaves = leaf_coords.shape[1]
    rows = leaves * LEAF_ROWS
    natural = density_rows.shape[1]
    devices = lax.axis_size("group") * lax.axis_size("dom")
    dom_count = lax.axis_size("dom")
    f32 = jnp.float32
    reorder = natural == width
    params = pltpu.CompilerParams(vmem_limit_bytes=(24 << 20) + 4 * natural * natural)

    def cost(flops, transcendentals=0):
        return pl.CostEstimate(
            flops=flops, bytes_accessed=4 << 20, transcendentals=transcendentals
        )

    def load():
        operands = (near_blocks, leaf_transfer, dev_transfer, leaf_basis)
        return pl.pallas_call(
            functools.partial(load_kernel, reorder),
            out_shape=(
                jax.ShapeDtypeStruct(density_rows.shape, jnp.bfloat16),
                jax.ShapeDtypeStruct((points, width), jnp.bfloat16),
                jax.ShapeDtypeStruct((natural, width), jnp.bfloat16),
                jax.ShapeDtypeStruct((2 * RANK, points), f32),
            ),
            in_specs=[HBM] * 6,
            out_specs=(VMEM,) * 4,
            scratch_shapes=[pltpu.VMEM(x.shape, x.dtype) for x in operands]
            + [pltpu.SemaphoreType.DMA((6,))],
            compiler_params=params,
            cost_estimate=cost(1 << 20),
            name="load",
        )(*[in_hbm(x) for x in operands], in_hbm(orbitals), in_hbm(density_rows))

    def prepare(loaded):
        orbit, pick, _ = loaded
        if not reorder:
            return [orbit, pick]
        return pl.pallas_call(
            prepare_kernel,
            out_shape=(
                jax.ShapeDtypeStruct((points, natural), jnp.bfloat16),
                jax.ShapeDtypeStruct((natural, natural), jnp.bfloat16),
            ),
            in_specs=[VMEM] * 2,
            out_specs=(VMEM, VMEM),
            compiler_params=params,
            cost_estimate=cost(2 * points * width * natural),
            name="prepare",
        )(orbit, pick)

    held, other, (_, _, weights), (orbit, pick) = gather_rows(density_rows, load, prepare)

    if reorder:
        rest = [
            pl.pallas_call(
                first_kernel,
                out_shape=jax.ShapeDtypeStruct((points, LANES), f32),
                in_specs=[VMEM] * 3,
                out_specs=VMEM,
                scratch_shapes=[pltpu.VMEM((natural // 2, natural), jnp.bfloat16)],
                compiler_params=params,
                cost_estimate=cost(points * width * width),
                name="first",
            )(orbit, held, pick)
        ]
        rows_shape = (natural // 2, natural)
    else:
        rest, rows_shape = [held, near_blocks], (width, natural)
    halo, expansion = pl.pallas_call(
        functools.partial(density_kernel, reorder),
        out_shape=(
            jax.ShapeDtypeStruct((rows + 8, LANES), f32),
            jax.ShapeDtypeStruct((devices, 2, LANES), f32),
        ),
        in_specs=[VMEM] * 6 + ([] if reorder else [SMEM]),
        out_specs=(VMEM, VMEM),
        scratch_shapes=[pltpu.VMEM(rows_shape, jnp.bfloat16)],
        compiler_params=params,
        cost_estimate=cost(points * width * width),
        name="density",
    )(leaf_coords, orbit, other, weights, pick, *rest)

    even = swap(halo, "dom", 1)
    pairs = [(i, i + 1 if i % 2 else i - 1) for i in range(1, dom_count - 1)]
    odd = lax.ppermute(halo, "dom", pairs)
    everyone = lax.all_to_all(expansion, ("group", "dom"), 0, 0)

    table = jax.ShapeDtypeStruct((rows, LANES), f32)
    sums = jax.ShapeDtypeStruct((leaves, LEAF, LANES), f32)
    places_shape = jax.ShapeDtypeStruct((24, LANES), f32)
    masks = jax.ShapeDtypeStruct((dev_far.shape[1] + group_far.shape[1], LANES), f32)
    near_sums, own_places, mask = pl.pallas_call(
        self_kernel,
        out_shape=(sums, places_shape, masks),
        in_specs=[HBM, HBM, VMEM],
        out_specs=(VMEM, VMEM, VMEM),
        scratch_shapes=[
            pltpu.VMEM(dev_far.shape, jnp.int32),
            pltpu.VMEM(group_far.shape, jnp.int32),
            pltpu.SemaphoreType.DMA((2,)),
        ],
        compiler_params=params,
        cost_estimate=cost(20 << 20, 4 << 20),
        name="self",
    )(in_hbm(dev_far), in_hbm(group_far), halo)
    near = pl.pallas_call(
        near_kernel,
        out_shape=table,
        in_specs=[VMEM] * 6,
        out_specs=VMEM,
        scratch_shapes=[
            pltpu.VMEM((3 * rows, LANES), f32),
            pltpu.VMEM((72, LANES), f32),
            pltpu.VMEM((leaves, LEAF, LANES), f32),
        ],
        compiler_params=params,
        cost_estimate=cost(20 << 20, 4 << 20),
        name="near",
    )(near_leaves, halo, even, odd, own_places, near_sums)
    hartree, density = pl.pallas_call(
        potential_kernel,
        out_shape=(table, table),
        in_specs=[VMEM] * 6,
        out_specs=(VMEM, VMEM),
        compiler_params=params,
        cost_estimate=cost(4 << 20, 1 << 20),
        name="potential",
    )(everyone, mask, weights, dev_transfer, near, halo)
    return (density.reshape(-1), hartree.reshape(-1))


def solution(mesh):
    in_specs = (
        P(("group", "dom"), None),
        P(("group", "dom"), None),
        P(("group", "dom"), None),
        P(None, ("group", "dom")),
        P(("group", "dom"), None),
        P(None, ("group", "dom")),
        P(("group", "dom"), None, None),
        P(("group", "dom"), None, None),
        P(("group", "dom"), None),
        P("group", None),
    )
    out_specs = (P(("group", "dom")), P(("group", "dom")))
    return jax.shard_map(local, mesh=mesh, in_specs=in_specs, out_specs=out_specs, check_vma=False)
```

```python
import functools
import math

import jax
import jax.numpy as jnp
from jax import lax
from jax.experimental import pallas as pl
from jax.experimental.pallas import tpu as pltpu
from jax.sharding import PartitionSpec as P

SIDE = 8
LEAF = 512
CHEB = 4
RANK = CHEB * CHEB * CHEB
BW = 16
BLOCK_ROWS = 2 * BW
NEARL = 3
LANES = 128
LEAF_ROWS = LEAF // LANES
TILE = 512

vol_weight = 0.1
soft_square = 1.0


def swap(value, axis, mask):
    return lax.ppermute(value, axis, [(i, i ^ mask) for i in range(lax.axis_size(axis))])


def piece_of(apart):
    pair = jnp.bitwise_and(lax.shift_right_logical(apart, 1), 3)
    place = jnp.where(pair == 0, 0, jnp.where(pair == 1, 3, pair - 1))
    return apart + 2 * (place - pair)


def gather_rows(rows, load, prepare):
    count = lax.axis_size("dom")
    beside, middle = swap(rows, "dom", 2), swap(rows, "dom", 8)
    own, *loaded = load()
    beside, loaded = lax.optimization_barrier((beside, loaded))
    pair = jnp.concatenate([own, beside], axis=0)
    far, close = swap(pair, "dom", 12), swap(pair, "dom", 4)
    middle, loaded = lax.optimization_barrier((middle, loaded))
    other_middle = swap(middle, "dom", 2)
    result = prepare(loaded)
    held = jnp.concatenate([pair, middle, other_middle, far, close], axis=0)
    bit = 16
    while bit < count:
        held = jnp.concatenate([held, swap(held, "dom", bit)], axis=0)
        bit *= 2
    held, result = lax.optimization_barrier((held, result))
    return held, swap(held, "dom", 1), loaded, result


def iota(shape, dim):
    return lax.broadcasted_iota(jnp.int32, shape, dim)


def lane_sums(x):
    return jnp.sum(x.T, axis=0, keepdims=True)


def spread_rows(row, count):
    size = row.shape[1]
    diagonal = iota((count, size), 0) == iota((count, size), 1)
    diagonal = jnp.where(diagonal, row, 0.0).astype(jnp.bfloat16)
    return jnp.dot(
        diagonal, jnp.ones((size, LANES), jnp.bfloat16), preferred_element_type=jnp.float32
    )


def split(x):
    high = x.astype(jnp.bfloat16)
    return high, (x - high.astype(jnp.float32)).astype(jnp.bfloat16)


def by_core(device, devices):
    chip = lax.shift_right_logical(device, 1)
    return jnp.bitwise_and(device, 1) * (devices // 2) + chip


def load_kernel(
    reorder,
    near_hbm,
    transfer_hbm,
    dev_hbm,
    basis_hbm,
    orbitals_hbm,
    rows_hbm,
    own_ref,
    orbit_ref,
    pick_ref,
    weights_ref,
    near_ref,
    transfer_ref,
    dev_ref,
    basis_ref,
    sems,
):
    moves = ((near_hbm, near_ref), (transfer_hbm, transfer_ref), (dev_hbm, dev_ref))
    moves += ((basis_hbm, basis_ref), (orbitals_hbm, orbit_ref), (rows_hbm, own_ref))
    copies = [pltpu.make_async_copy(a, b, sems.at[i]) for i, (a, b) in enumerate(moves)]
    for copy in copies:
        copy.start()
    copies[0].wait()
    blocks = near_ref.shape[1]
    width = blocks * BW
    expand = (iota((blocks, width), 1) // BW == iota((blocks, width), 0)).astype(jnp.float32)
    near = near_ref[...]
    if reorder:
        device = by_core(lax.shift_right_logical(near, 1), blocks // 2)
        near = 2 * device + jnp.bitwise_and(near, 1)
    near = jnp.broadcast_to(near.astype(jnp.float32), (8, blocks))
    column = jnp.dot(near, expand, preferred_element_type=jnp.float32)[:1].astype(jnp.int32) * BW
    column = column + iota((1, width), 1) % BW
    for start in range(0, pick_ref.shape[0], LEAF):
        size = min(LEAF, pick_ref.shape[0] - start)
        hit = iota((size, width), 0) + start == column
        pick_ref[start : start + size, :] = jnp.where(hit, 1.0, 0.0).astype(jnp.bfloat16)
    for copy in copies[1:4]:
        copy.wait()
    leaves = transfer_ref.shape[0]
    transfer = transfer_ref[...].reshape(leaves * RANK, RANK)
    high, low = split(transfer)
    dev_high, dev_low = split(dev_ref[0])
    raised = jnp.dot(
        jnp.concatenate([high, high, low], axis=1),
        jnp.concatenate([dev_high, dev_low, dev_high], axis=0),
        preferred_element_type=jnp.float32,
    )
    high, low = split(jnp.concatenate([transfer, raised], axis=1))
    for leaf in range(leaves):
        at, points = slice(leaf * RANK, (leaf + 1) * RANK), slice(leaf * LEAF, (leaf + 1) * LEAF)
        basis_high, basis_low = split(basis_ref[:, points])
        weights_ref[:, points] = lax.dot_general(
            jnp.concatenate([high[at], high[at], low[at]], axis=0),
            jnp.concatenate([basis_high, basis_low, basis_high], axis=0),
            (((0,), (0,)), ((), ())),
            preferred_element_type=jnp.float32,
        )
    for copy in copies[4:]:
        copy.wait()


def prepare_kernel(orbit_ref, pick_ref, sorted_ref, order_ref):
    for start in range(0, orbit_ref.shape[0], LEAF):
        part = lax.dot_general(
            orbit_ref[start : start + LEAF, :],
            pick_ref[...],
            (((1,), (1,)), ((), ())),
            preferred_element_type=jnp.float32,
        )
        sorted_ref[start : start + LEAF, :] = part.astype(jnp.bfloat16)
    size = order_ref.shape[0]
    column = iota((size, 1), 0)
    place = by_core(column // BLOCK_ROWS, size // BLOCK_ROWS) * BLOCK_ROWS + column % BLOCK_ROWS
    hit = iota((size, size), 1) == place
    order_ref[...] = jnp.where(hit, 1.0, 0.0).astype(jnp.bfloat16)


def half_matrix(pieces_ref, order_ref, rows_ref):
    chip = lax.shift_right_logical(lax.axis_index("dom"), 1)
    for c in range(pieces_ref.shape[0] // BLOCK_ROWS):
        first = piece_of(jnp.bitwise_xor(chip, c)) * BLOCK_ROWS
        at = pl.ds(pl.multiple_of(first, BLOCK_ROWS), BLOCK_ROWS)
        rows_ref[c * BLOCK_ROWS : (c + 1) * BLOCK_ROWS, :] = pieces_ref[at, :]
    matrix = jnp.dot(rows_ref[...], order_ref[...], preferred_element_type=jnp.float32)
    return matrix.astype(jnp.bfloat16)


def quadratic(orbit_ref, start, columns, matrix):
    points = slice(start, start + TILE)
    product = jnp.dot(orbit_ref[points, columns], matrix, preferred_element_type=jnp.float32)
    product = product * orbit_ref[points, :].astype(jnp.float32)
    folded = product[:, :LANES]
    for at in range(LANES, product.shape[1], LANES):
        folded = folded + product[:, at : at + LANES]
    return folded


def core_columns(core, width):
    return pl.ds(pl.multiple_of(core * (width // 2), LANES), width // 2)


def first_kernel(orbit_ref, held_ref, order_ref, out_ref, rows_ref):
    matrix = half_matrix(held_ref, order_ref, rows_ref)
    columns = core_columns(jnp.bitwise_and(lax.axis_index("dom"), 1), orbit_ref.shape[1])
    for start in range(0, orbit_ref.shape[0], TILE):
        out_ref[start : start + TILE, :] = quadratic(orbit_ref, start, columns, matrix)


def density_kernel(reorder, coords_ref, orbit_ref, other_ref, weights_ref, pick_ref, *refs):
    *inputs, halo_ref, expansion_ref, rows_ref = refs
    leaves = coords_ref.shape[1]
    me = lax.axis_index("dom")
    if reorder:
        matrix = half_matrix(other_ref, pick_ref, rows_ref)
        columns = core_columns(1 - jnp.bitwise_and(me, 1), orbit_ref.shape[1])
    else:
        held_ref, near_ref = inputs
        for k in range(near_ref.shape[1]):
            block = near_ref[0, k]
            apart = jnp.bitwise_xor(lax.shift_right_logical(block, 1), me)
            piece = piece_of(lax.shift_right_logical(apart, 1))
            first = piece * BLOCK_ROWS + jnp.bitwise_and(block, 1) * BW
            at = pl.ds(pl.multiple_of(first, BW), BW)
            mine = jnp.bitwise_and(apart, 1) == 0
            rows_ref[k * BW : (k + 1) * BW, :] = jnp.where(mine, held_ref[at, :], other_ref[at, :])
        matrix = jnp.dot(rows_ref[...], pick_ref[...], preferred_element_type=jnp.float32)
        matrix = matrix.astype(jnp.bfloat16)
        columns = slice(None)
    total = jnp.zeros((2 * RANK, LANES), jnp.float32)
    for start in range(0, leaves * LEAF, TILE):
        folded = quadratic(orbit_ref, start, columns, matrix)
        if reorder:
            folded = folded + inputs[0][start : start + TILE, :]
        for j in range(TILE // LANES):
            row = start // LANES + j
            part = lane_sums(folded[j * LANES : (j + 1) * LANES])
            halo_ref[row : row + 1, :] = part
            total = total + weights_ref[:, row * LANES : (row + 1) * LANES] * part
    coords = coords_ref[...].astype(jnp.float32)
    rows = leaves * LEAF_ROWS
    halo_ref[rows:, :] = jnp.zeros((halo_ref.shape[0] - rows, LANES), jnp.float32)
    halo_ref[rows : rows + 3, :leaves] = coords
    low = SIDE * jnp.min(coords, axis=1, keepdims=True)
    high = SIDE * jnp.max(coords, axis=1, keepdims=True) + (SIDE - 1)
    lane = iota((1, LANES), 1)
    bounds = jnp.zeros((1, LANES), jnp.float32)
    for k in range(3):
        bounds = jnp.where(lane == k, low[k : k + 1], bounds)
        bounds = jnp.where(lane == 3 + k, high[k : k + 1], bounds)
    both = jnp.concatenate([lane_sums(total), bounds], axis=0)
    expansion_ref[...] = jnp.broadcast_to(both[None], expansion_ref.shape)


def pattern(index):
    steps = (index // (CHEB * CHEB) % CHEB, index // CHEB % CHEB, index % CHEB)
    points = [math.cos((2 * a + 1) * math.pi / (2 * CHEB)) for a in range(CHEB)]
    out = []
    for step in steps:
        value = jnp.full(index.shape, points[CHEB - 1], jnp.float32)
        for a in range(CHEB - 1):
            value = jnp.where(step == a, points[a], value)
        out.append(value)
    return out


def nodes(bounds, unit):
    out = []
    for k in range(3):
        low, high = bounds[:, k : k + 1], bounds[:, 3 + k : 4 + k]
        out.append(0.5 * (low + high) + 0.5 * (high - low) * unit[k])
    return out


def node_coupling(target, source):
    square = soft_square
    for t, s in zip(target, source, strict=True):
        apart = t - s
        square = square + apart * apart
    return lax.rsqrt(square)


def places(halo, rows):
    parts = [spread_rows(halo[rows + k : rows + k + 1], 8) for k in range(3)]
    return SIDE * jnp.concatenate(parts, axis=0)


def pair_kernel(shift, y, square_x, square_z):
    lane = iota((8, LANES), 1)
    apart = shift[1] + (y - lane // SIDE % SIDE).astype(jnp.float32)
    square = apart * apart + square_z
    even = [lax.rsqrt(x + square) for x in square_x]
    low = lane < LANES // 2
    return even, [jnp.where(low, a, b) for a, b in zip(even[:-1], even[1:], strict=True)]


def pair_squares(shift):
    lane, row = iota((8, LANES), 1), iota((8, LANES), 0)
    half = jnp.where(lane < LANES // 2, 0.0, 1.0)
    along = shift[2] + (row - lane % SIDE).astype(jnp.float32)
    square_x = []
    for m in range(-6, SIDE + 2, 2):
        apart = shift[0] + (m - half)
        square_x.append(apart * apart)
    return square_x, along * along + soft_square


def leaf_density(density_ref, leaf):
    rows = [density_ref[pl.ds(leaf * LEAF_ROWS + j, 1), :] for j in range(LEAF_ROWS)]
    rows = [jnp.broadcast_to(row, (8, LANES)) for row in rows]
    return rows, [pltpu.roll(row, LANES // 2, 1) for row in rows]


def pair_sums(kernel, density, y):
    for x in range(SIDE):
        first = x // 2 + 3
        k, rho = kernel[x % 2], density[x % 2]
        value = k[first] * rho[0]
        for j in range(1, LEAF_ROWS):
            value = value + k[first - j] * rho[j]
        yield slice((x * SIDE + y) * SIDE, (x * SIDE + y + 1) * SIDE), value


def leaf_place(place_ref, leaf):
    return [place_ref[pl.ds(leaf + 8 * k, 1), :] for k in range(3)]


def self_kernel(
    far_hbm, group_far_hbm, halo_ref, sum_ref, place_ref, mask_ref, far_ref, group_far_ref, sems
):
    moves = ((far_hbm, far_ref), (group_far_hbm, group_far_ref))
    copies = [pltpu.make_async_copy(a, b, sems.at[i]) for i, (a, b) in enumerate(moves)]
    for copy in copies:
        copy.start()
    leaves = sum_ref.shape[0]
    place_ref[...] = places(halo_ref[...], leaves * LEAF_ROWS)
    shift = [jnp.zeros((8, LANES), jnp.float32)] * 3
    square_x, square_z = pair_squares(shift)
    for y in range(SIDE):
        kernel = pair_kernel(shift, y, square_x, square_z)
        for leaf in range(leaves):
            for at, value in pair_sums(kernel, leaf_density(halo_ref, leaf), y):
                sum_ref[leaf, at, :] = value
    for copy in copies:
        copy.wait()
    dom_count, group_count = far_ref.shape[1], group_far_ref.shape[1]
    mask_ref[:dom_count, :] = spread_rows(far_ref[...].astype(jnp.float32), dom_count)
    mask_ref[dom_count:, :] = spread_rows(group_far_ref[...].astype(jnp.float32), group_count)


def near_kernel(
    leaves_ref, halo_ref, even_ref, odd_ref, own_ref, part_ref, out_ref, density_ref, place_ref, sum_ref
):
    leaves = leaves_ref.shape[0]
    rows = leaves * LEAF_ROWS
    is_odd = jnp.bitwise_and(lax.axis_index("dom"), 1) == 1
    even, odd = even_ref[...], odd_ref[...]
    window = (jnp.where(is_odd, even, odd), halo_ref[...], jnp.where(is_odd, odd, even))
    for side, held in enumerate(window):
        density_ref[side * rows : (side + 1) * rows, :] = held[:rows]
        place_ref[24 * side : 24 * (side + 1), :] = own_ref[...] if side == 1 else places(held, rows)
    for leaf in range(leaves):
        own_place = leaf_place(own_ref, leaf)
        named = [leaves_ref[leaf, slot] for slot in range(NEARL)]
        own = leaves + leaf
        others = (
            jnp.where(named[0] == own, named[1], named[0]),
            jnp.where(named[2] == own, named[1], named[2]),
        )
        for slot, position in enumerate(others):
            side = (position >= leaves).astype(jnp.int32)
            side = side + (position >= 2 * leaves).astype(jnp.int32)
            place = leaf_place(place_ref, 24 * side + position - leaves * side)
            shift = [jnp.broadcast_to(p - q, (8, LANES)) for p, q in zip(own_place, place, strict=True)]
            square_x, square_z = pair_squares(shift)
            density = leaf_density(density_ref, position)
            for y in range(SIDE):
                kernel = pair_kernel(shift, y, square_x, square_z)
                for at, value in pair_sums(kernel, density, y):
                    before = part_ref[leaf, at, :] if slot == 0 else sum_ref[leaf, at, :]
                    sum_ref[leaf, at, :] = before + value
        for j in range(LEAF_ROWS):
            part = lane_sums(sum_ref[leaf, j * LANES : (j + 1) * LANES, :])
            row = leaf * LEAF_ROWS + j
            out_ref[row : row + 1, :] = vol_weight * part


def far_field(expansion_ref, mask_ref, dev_ref):
    dom_count = lax.axis_size("dom")
    group_count = mask_ref.shape[0] - dom_count
    group, me = lax.axis_index("group"), lax.axis_index("dom")
    moments, bounds = expansion_ref[:, 0, :], expansion_ref[:, 1, :]
    lane = iota((1, LANES), 1)
    unit_row = pattern(lane % RANK)
    unit_column = pattern(iota((RANK, LANES), 0))
    group_bounds = []
    for h in range(group_count):
        part = bounds[h * dom_count : (h + 1) * dom_count]
        low = jnp.min(part, axis=0, keepdims=True)
        high = jnp.max(part, axis=0, keepdims=True)
        group_bounds.append(jnp.where(lane < 3, low, high))
    own_group_bounds = group_bounds[0]
    for h in range(1, group_count):
        own_group_bounds = jnp.where(group == h, group_bounds[h], own_group_bounds)
    target = nodes(own_group_bounds, unit_column)
    total = jnp.zeros((RANK, LANES), jnp.float32)
    for h in range(group_count):
        raised = jnp.sum(moments[h * dom_count : (h + 1) * dom_count], axis=0, keepdims=True)
        raised = jnp.where(lane >= RANK, raised, 0.0) * mask_ref[dom_count + h : dom_count + h + 1, :]
        total = total + node_coupling(target, nodes(group_bounds[h], unit_row)) * raised
    group_local = vol_weight * lane_sums(total)
    local = jnp.sum(dev_ref[0] * group_local, axis=1, keepdims=True)
    base = group * dom_count
    at = pl.ds(base, dom_count)
    own_bounds = expansion_ref[pl.ds(base + me, 1), 1, :]
    target = nodes(own_bounds, unit_column)
    low, half = lane < RANK, dom_count // 2
    source = [jnp.where(low, x[:half], x[half:]) for x in nodes(expansion_ref[at, 1, :], unit_row)]
    own_moments = expansion_ref[at, 0, :] * mask_ref[:dom_count, :]
    own_moments = jnp.where(low, own_moments[:half], pltpu.roll(own_moments[half:], RANK, 1))
    total = jnp.zeros((RANK, LANES), jnp.float32)
    for s in range(half):
        coupling = node_coupling(target, [x[s : s + 1] for x in source])
        total = total + coupling * own_moments[s : s + 1]
    local = local + vol_weight * jnp.sum(total, axis=1, keepdims=True)
    return jnp.broadcast_to(local, (RANK, LANES))


def potential_kernel(
    expansion_ref, mask_ref, weights_ref, dev_ref, near_ref, halo_ref, out_ref, density_ref
):
    density_ref[...] = halo_ref[: density_ref.shape[0], :]
    local = far_field(expansion_ref, mask_ref, dev_ref)
    for row in range(out_ref.shape[0]):
        at = slice(row * LANES, (row + 1) * LANES)
        far = jnp.sum(weights_ref[:RANK, at] * local, axis=0, keepdims=True)
        out_ref[row : row + 1, :] = near_ref[row : row + 1, :] + far


def in_hbm(x):
    return pltpu.with_memory_space_constraint(x, pltpu.HBM)


VMEM = pl.BlockSpec(memory_space=pltpu.VMEM)
SMEM = pl.BlockSpec(memory_space=pltpu.SMEM)
HBM = pl.BlockSpec(memory_space=pltpu.HBM)
ANY = pl.BlockSpec(memory_space=pl.ANY)


def local(
    orbitals,
    density_rows,
    near_blocks,
    leaf_coords,
    near_leaves,
    leaf_basis,
    leaf_transfer,
    dev_transfer,
    dev_far,
    group_far,
):
    points, width = orbitals.shape
    leaves = leaf_coords.shape[1]
    rows = leaves * LEAF_ROWS
    natural = density_rows.shape[1]
    devices = lax.axis_size("group") * lax.axis_size("dom")
    dom_count = lax.axis_size("dom")
    f32 = jnp.float32
    reorder = natural == width
    params = pltpu.CompilerParams(vmem_limit_bytes=(24 << 20) + 4 * natural * natural)

    def cost(flops, transcendentals=0):
        return pl.CostEstimate(
            flops=flops, bytes_accessed=4 << 20, transcendentals=transcendentals
        )

    def load():
        operands = (near_blocks, leaf_transfer, dev_transfer, leaf_basis)
        return pl.pallas_call(
            functools.partial(load_kernel, reorder),
            out_shape=(
                jax.ShapeDtypeStruct(density_rows.shape, jnp.bfloat16),
                jax.ShapeDtypeStruct((points, width), jnp.bfloat16),
                jax.ShapeDtypeStruct((natural, width), jnp.bfloat16),
                jax.ShapeDtypeStruct((2 * RANK, points), f32),
            ),
            in_specs=[HBM] * 6,
            out_specs=(VMEM,) * 4,
            scratch_shapes=[pltpu.VMEM(x.shape, x.dtype) for x in operands]
            + [pltpu.SemaphoreType.DMA((6,))],
            compiler_params=params,
            cost_estimate=cost(1 << 20),
            name="load",
        )(*[in_hbm(x) for x in operands], in_hbm(orbitals), in_hbm(density_rows))

    def prepare(loaded):
        orbit, pick, _ = loaded
        if not reorder:
            return [orbit, pick]
        return pl.pallas_call(
            prepare_kernel,
            out_shape=(
                jax.ShapeDtypeStruct((points, natural), jnp.bfloat16),
                jax.ShapeDtypeStruct((natural, natural), jnp.bfloat16),
            ),
            in_specs=[VMEM] * 2,
            out_specs=(VMEM, VMEM),
            compiler_params=params,
            cost_estimate=cost(2 * points * width * natural),
            name="prepare",
        )(orbit, pick)

    held, other, (_, _, weights), (orbit, pick) = gather_rows(density_rows, load, prepare)

    if reorder:
        rest = [
            pl.pallas_call(
                first_kernel,
                out_shape=jax.ShapeDtypeStruct((points, LANES), f32),
                in_specs=[VMEM] * 3,
                out_specs=VMEM,
                scratch_shapes=[pltpu.VMEM((natural // 2, natural), jnp.bfloat16)],
                compiler_params=params,
                cost_estimate=cost(points * width * width),
                name="first",
            )(orbit, held, pick)
        ]
        rows_shape = (natural // 2, natural)
    else:
        rest, rows_shape = [held, near_blocks], (width, natural)
    halo, expansion = pl.pallas_call(
        functools.partial(density_kernel, reorder),
        out_shape=(
            jax.ShapeDtypeStruct((rows + 8, LANES), f32),
            jax.ShapeDtypeStruct((devices, 2, LANES), f32),
        ),
        in_specs=[VMEM] * 6 + ([] if reorder else [SMEM]),
        out_specs=(VMEM, VMEM),
        scratch_shapes=[pltpu.VMEM(rows_shape, jnp.bfloat16)],
        compiler_params=params,
        cost_estimate=cost(points * width * width),
        name="density",
    )(leaf_coords, orbit, other, weights, pick, *rest)

    even = swap(halo, "dom", 1)
    pairs = [(i, i + 1 if i % 2 else i - 1) for i in range(1, dom_count - 1)]
    odd = lax.ppermute(halo, "dom", pairs)
    everyone = lax.all_to_all(expansion, ("group", "dom"), 0, 0)

    table = jax.ShapeDtypeStruct((rows, LANES), f32)
    sums = jax.ShapeDtypeStruct((leaves, LEAF, LANES), f32)
    places_shape = jax.ShapeDtypeStruct((24, LANES), f32)
    masks = jax.ShapeDtypeStruct((dev_far.shape[1] + group_far.shape[1], LANES), f32)
    near_sums, own_places, mask = pl.pallas_call(
        self_kernel,
        out_shape=(sums, places_shape, masks),
        in_specs=[HBM, HBM, VMEM],
        out_specs=(VMEM, VMEM, VMEM),
        scratch_shapes=[
            pltpu.VMEM(dev_far.shape, jnp.int32),
            pltpu.VMEM(group_far.shape, jnp.int32),
            pltpu.SemaphoreType.DMA((2,)),
        ],
        compiler_params=params,
        cost_estimate=cost(20 << 20, 4 << 20),
        name="self",
    )(in_hbm(dev_far), in_hbm(group_far), halo)
    near = pl.pallas_call(
        near_kernel,
        out_shape=table,
        in_specs=[VMEM] * 6,
        out_specs=VMEM,
        scratch_shapes=[
            pltpu.VMEM((3 * rows, LANES), f32),
            pltpu.VMEM((72, LANES), f32),
            pltpu.VMEM((leaves, LEAF, LANES), f32),
        ],
        compiler_params=params,
        cost_estimate=cost(20 << 20, 4 << 20),
        name="near",
    )(near_leaves, halo, even, odd, own_places, near_sums)
    hartree, density = pl.pallas_call(
        potential_kernel,
        out_shape=(table, table),
        in_specs=[VMEM] * 6,
        out_specs=(VMEM, VMEM),
        compiler_params=params,
        cost_estimate=cost(4 << 20, 1 << 20),
        name="potential",
    )(everyone, mask, weights, dev_transfer, near, halo)
    return (density.reshape(-1), hartree.reshape(-1))


def solution(mesh):
    in_specs = (
        P(("group", "dom"), None),
        P(("group", "dom"), None),
        P(("group", "dom"), None),
        P(None, ("group", "dom")),
        P(("group", "dom"), None),
        P(None, ("group", "dom")),
        P(("group", "dom"), None, None),
        P(("group", "dom"), None, None),
        P(("group", "dom"), None),
        P("group", None),
    )
    out_specs = (P(("group", "dom")), P(("group", "dom")))
    return jax.shard_map(local, mesh=mesh, in_specs=in_specs, out_specs=out_specs, check_vma=False)
```
